512 devices in a mesh: dp: 32 (over y, x, core), feat: 16 (over z).
Axes of the slice: x: 4, y: 4, z: 16, core: 2. Of those that a mesh axis runs over, the one named last changes fastest.
Arguments:
- edge_feats: bfloat16 [65536, 768], P('dp', 'feat'), may hold values from -6 to 6
- edge_dst: int32 [65536], P('dp'), may hold values from 0 to 16383, as said below
- self_feats: bfloat16 [16384, 768], P('dp', 'feat'), may hold values from -6 to 6
- neigh_one: bfloat16 [768, 1024], P('feat'), may hold values from -0.21875 to 0.21875
- self_one: bfloat16 [768, 1024], P('feat'), may hold values from -0.21875 to 0.21875
- bias_one: float32 [1024], P('feat'), may hold values from -3 to 3
- tile_index: int32 [128, 2], P('dp'), may hold values from 0 to 3
- tile_values: bfloat16 [128, 128, 128], P('dp'), may hold values from -0.5 to 0.5
- seed_live: int32 [16384], P('dp'), may hold values 0 or 1
- neigh_two: bfloat16 [1024, 1024], P('feat'), may hold values from -0.1875 to 0.1875
- self_two: bfloat16 [1024, 1024], P('feat'), may hold values from -0.1875 to 0.1875
- bias_two: float32 [1024], P('feat'), may hold values from -3 to 3
- cotangent: bfloat16 [16384, 1024], P('dp', 'feat'), may hold values from -0.046875 to 0.046875
Outputs:
- second_out: bfloat16 [16384, 1024], P('dp', 'feat')
- grad_neigh: float32 [1024, 1024], P('feat')
- grad_self: float32 [1024, 1024], P('feat')
The draws below stay inside these ranges and needn't reach their ends.
Inputs may be any that keep to these rules, and one draw needn't show every extreme that they name: `edge_dst`: the owner of target vertex v is v // 512. Among the 2048 edges of one index of dp at most 128 have targets of one owner; in every draw each index of dp has some owner with exactly 128, and some owner receives exactly 128 from every index of dp.
All inputs are finite; a program needn't handle non-finite values. No bound on the sum of `seed_live` on one device may be relied on, other than what follows from the above.
Results may differ from the reference program's by a relative error of at most 0.0053.
Values may be sent and summed in bfloat16 or wider, within the bound.
No kernel may reach another device: no remote copies, remote signals or barrier semaphores. Data moves between devices by JAX's collectives and lax.ppermute only.
A program may use at most 128 MiB of HBM per device.

```python
import jax
import jax.numpy as jnp
from jax import lax

F = 768
H = 1024
EDGE_DEV = 2048
TGT_DEV = 512
TILES_DEV = 4
EDGES = 65536
TARGETS = 16384
TILES = 128
N_DP = 32


def draw_edge_dst(key, part):
    key = jax.random.fold_in(key, 7)
    bucket_cap = 2 * EDGE_DEV // N_DP
    slot_count = 2 * EDGE_DEV
    weight_key, force_key, device_key = jax.random.split(key, 3)
    owner_weight = jax.random.randint(weight_key, (N_DP,), 0, 4)
    common_owner = jax.random.randint(force_key, (), 0, N_DP)
    owner_weight = jnp.where(jnp.arange(N_DP) == common_owner, 4, owner_weight)
    slot_owner = jnp.arange(slot_count) // bucket_cap

    def one_device(per_device):
        pick_key, jitter_key, local_key, order_key = jax.random.split(per_device, 4)
        favored = jax.random.randint(pick_key, (), 0, N_DP)
        jitter_vals = jax.random.randint(jitter_key, (slot_count,), 0, 1024)
        ranking = jnp.where(slot_owner == favored, 8, owner_weight[slot_owner]) * 1024 + jitter_vals
        ranking = ranking * slot_count + jnp.arange(slot_count)
        top_scores, chosen = lax.top_k(ranking, EDGE_DEV)
        owner_ids = chosen // bucket_cap
        local_ids = jax.random.randint(local_key, (EDGE_DEV,), 0, TGT_DEV)
        vertex_ids = owner_ids * TGT_DEV + local_ids
        return jax.random.permutation(order_key, vertex_ids)
    result = jax.vmap(one_device)(jax.random.split(device_key, N_DP))
    return result.reshape(-1).astype(jnp.int32)


def with_ends(values, key, low, top_value):
    extent = values.shape
    spot = [jax.random.randint(jax.random.fold_in(key, axis), (), 0, extent[axis]) for axis in range(len(extent))]
    values = values.at[tuple(spot)].set(low)
    longest = extent.index(max(extent))
    spot[longest] = (spot[longest] + 1) % extent[longest]
    return values.at[tuple(spot)].set(top_value)


def levels(rng, extent, cuts, smallest, largest):
    loudness, own = 1.0, jax.random.fold_in(rng, 6)
    for axis_at, shards_of in cuts:
        draws = jnp.exp(jax.random.uniform(jax.random.fold_in(own, axis_at), (shards_of,), jnp.float32, smallest / len(cuts), largest / len(cuts)))
        loudness = loudness * jnp.repeat(draws, extent[axis_at] // shards_of).reshape([-1 if axis == axis_at else 1 for axis in range(len(extent))])
    return loudness


def normal_values(key, extent, spread, reach, pieces=(), held_as=jnp.bfloat16):
    entries = spread * jax.random.normal(key, extent, jnp.float32)
    if pieces:
        entries = entries * levels(key, extent, pieces, -0.22, 0.18)
    return jnp.clip(entries, -reach, reach).astype(held_as)


def setup_inputs(seed: int = 0) -> dict:
    splits = jax.random.split(jax.random.key(seed), 14)
    edge_feats = normal_values(splits[0], (EDGES, F), 1.0, 6.0, ((0, 32), (1, 16)))
    edge_dst = draw_edge_dst(jax.random.fold_in(splits[13], 71), 0)
    self_feats = normal_values(splits[2], (TARGETS, F), 1.0, 6.0, ((0, 32), (1, 16)))
    neigh_one = normal_values(splits[3], (F, H), F ** -0.5, 0.21875, ((0, 16),))
    self_one = normal_values(splits[4], (F, H), F ** -0.5, 0.21875, ((0, 16),))
    bias_one = normal_values(splits[5], (H,), 0.5, 3.0, ((0, 16),), jnp.float32)
    tile_index = with_ends(jax.random.randint(splits[6], (TILES, 2), 0, TGT_DEV // 128), jax.random.fold_in(splits[6], 1), 0, (TGT_DEV // 128) - 1).astype(jnp.int32)
    tile_values = normal_values(splits[7], (TILES, 128, 128), 128 ** -0.5, 0.5, ((0, 32),))
    seed_live = with_ends((jax.random.randint(splits[8], (TARGETS,), 0, 4) < 3).astype(jnp.int32), jax.random.fold_in(splits[8], 1), 0, 1)
    neigh_two = normal_values(splits[9], (H, H), H ** -0.5, 0.1875, ((0, 16),))
    self_two = normal_values(splits[10], (H, H), H ** -0.5, 0.1875, ((0, 16),))
    bias_two = normal_values(splits[11], (H,), 0.5, 3.0, ((0, 16),), jnp.float32)
    cotangent = normal_values(splits[12], (TARGETS, H), TARGETS ** -0.5, 0.046875, ((0, 32), (1, 16)))
    return dict(edge_feats=edge_feats, edge_dst=edge_dst, self_feats=self_feats, neigh_one=neigh_one, self_one=self_one, bias_one=bias_one, tile_index=tile_index, tile_values=tile_values, seed_live=seed_live, neigh_two=neigh_two, self_two=self_two, bias_two=bias_two, cotangent=cotangent)


def reference(edge_feats, edge_dst, self_feats, neigh_one, self_one, bias_one, tile_index, tile_values, seed_live, neigh_two, self_two, bias_two, cotangent):
    summed = jax.ops.segment_sum(edge_feats.astype(jnp.float32), edge_dst, num_segments=TARGETS)
    degree = jax.ops.segment_sum(jnp.ones(edge_dst.shape, jnp.float32), edge_dst, num_segments=TARGETS)
    neigh_mean = (summed / jnp.maximum(degree, 1.0)[:, None]).astype(jnp.bfloat16)
    first = jnp.dot(neigh_mean, neigh_one, preferred_element_type=jnp.float32)
    first = first + jnp.dot(self_feats, self_one, preferred_element_type=jnp.float32)
    hidden = jax.nn.relu(first + bias_one).astype(jnp.bfloat16)
    tile_count = TGT_DEV // 128
    owner_base = (jnp.arange(TILES, dtype=jnp.int32) // TILES_DEV) * tile_count
    hidden_tiles = hidden.reshape(TARGETS // 128, 128, H)
    sources = hidden_tiles[(owner_base + tile_index[:, 1]).astype(jnp.int32)]
    tile_terms = jnp.einsum("kij,kjc->kic", tile_values.astype(jnp.float32), sources.astype(jnp.float32))
    aggregated = jax.ops.segment_sum(tile_terms, (owner_base + tile_index[:, 0]).astype(jnp.int32), num_segments=TARGETS // 128)
    aggregated = aggregated.reshape(TARGETS, H).astype(jnp.bfloat16)
    live_mask = seed_live.astype(jnp.float32)[:, None]
    second = jnp.dot(aggregated, neigh_two, preferred_element_type=jnp.float32)
    second = second + jnp.dot(hidden, self_two, preferred_element_type=jnp.float32) + bias_two
    second_out = (second * live_mask).astype(jnp.bfloat16)
    masked_grad = (cotangent.astype(jnp.float32) * live_mask).astype(jnp.bfloat16)
    grad_neigh = jnp.dot(aggregated.T, masked_grad, preferred_element_type=jnp.float32)
    grad_self = jnp.dot(hidden.T, masked_grad, preferred_element_type=jnp.float32)
    return second_out, grad_neigh, grad_self
```

```python
import functools

import jax
import jax.numpy as jnp
from jax import lax
from jax.experimental import pallas as pl
from jax.experimental.pallas import tpu as pltpu
from jax.sharding import PartitionSpec as P

BF = jnp.bfloat16
F32 = jnp.float32
NT = (((1,), (1,)), ((), ()))
TN = (((0,), (0,)), ((), ()))
ROWS = 64
GROUP = 4
VMEM_LIMIT = 48 * 1024 * 1024


def call(kernel, out_shape, n_in, scratch=(), smem=(), flops=0, nbytes=0):
    in_specs = [
        pl.BlockSpec(memory_space=pltpu.SMEM if i in smem else pltpu.VMEM) for i in range(n_in)
    ]
    out_specs = jax.tree.map(lambda _: pl.BlockSpec(memory_space=pltpu.VMEM), out_shape)
    return pl.pallas_call(
        kernel,
        out_shape=out_shape,
        in_specs=in_specs,
        out_specs=out_specs,
        scratch_shapes=list(scratch),
        compiler_params=pltpu.CompilerParams(vmem_limit_bytes=VMEM_LIMIT),
        cost_estimate=pl.CostEstimate(flops=flops, bytes_accessed=nbytes, transcendentals=0),
    )


def pack_kernel(groups, tgt_rows, feats_ref, dst_ref, send_ref, masked):
    cols, edges = feats_ref.shape
    cap = send_ref.shape[2]
    dst = jnp.concatenate([dst_ref[i : i + 1, :] for i in range(dst_ref.shape[0])], axis=1)
    owner = dst // tgt_rows
    local = dst - owner * tgt_rows
    half = tgt_rows // 2
    code = jnp.where(local < half, local - half, local - (half - 1)).astype(F32)
    owner_hot = lax.broadcasted_iota(jnp.int32, (groups, edges), 0) == owner
    owner_hot = owner_hot.astype(F32)
    step = 256
    before = (
        lax.broadcasted_iota(jnp.int32, (step, step), 0)
        < lax.broadcasted_iota(jnp.int32, (step, step), 1)
    ).astype(BF)
    seen = jnp.zeros((groups, 1), F32)
    ranks = []
    for i in range(edges // step):
        part = owner_hot[:, i * step : (i + 1) * step]
        prior = jnp.dot(part.astype(BF), before, preferred_element_type=F32) + seen
        ranks.append(jnp.sum(prior * part, axis=0, keepdims=True))
        seen = seen + jnp.sum(part, axis=1, keepdims=True)
    rank = jnp.concatenate(ranks, axis=1).astype(jnp.int32)
    rank_hot = (lax.broadcasted_iota(jnp.int32, (cap, edges), 0) == rank).astype(F32).astype(BF)
    extra_row = lax.broadcasted_iota(jnp.int32, (ROWS - cols, edges), 0)
    extra = jnp.where(extra_row == 0, code, jnp.where(extra_row == 1, 1.0, 0.0)).astype(BF)
    hot = owner_hot.astype(BF)
    some = masked.shape[0] // ROWS
    for g in range(groups // some):
        for j in range(some):
            o = g * some + j
            live = hot[o : o + 1, :]
            masked[j * ROWS : j * ROWS + cols, :] = feats_ref[...] * live
            masked[j * ROWS + cols : (j + 1) * ROWS, :] = extra * live
        out = lax.dot_general(masked[...], rank_hot, NT, preferred_element_type=F32).astype(BF)
        for j in range(some):
            send_ref[g * some + j] = out[j * ROWS : (j + 1) * ROWS, :]


def mean_kernel(recv_ref, self_ref, out_ref):
    groups, rows, cap = recv_ref.shape
    cols, targets = self_ref.shape
    tiles = out_ref.shape[0]
    half = targets // 2
    vertex = lax.broadcasted_iota(jnp.int32, (targets, 1), 0)
    vertex = jnp.where(vertex < half, vertex - half, vertex - (half - 1)).astype(F32)
    acc = jnp.zeros((rows, targets), F32)
    some = 8
    for g in range(groups // some):
        part = jnp.concatenate([recv_ref[g * some + j] for j in range(some)], axis=1)
        code = part[cols : cols + 1, :].astype(F32)
        hot = (vertex == code).astype(F32).astype(BF)
        acc = acc + lax.dot_general(part, hot, NT, preferred_element_type=F32)
    degree = jnp.maximum(acc[cols + 1 : cols + 2, :], 1.0)
    mean = (acc[:cols, :] / degree).astype(BF)
    width = targets // tiles
    for t in range(tiles):
        out_ref[t, :cols, :] = mean[:, t * width : (t + 1) * width]
        out_ref[t, cols:, :] = self_ref[:, t * width : (t + 1) * width]


def hidden_kernel(parts_ref, bias_ref, index_ref, values_ref, live_ref, out_ref, left_ref, acc):
    n, cols, width = parts_ref.shape
    tiles = out_ref.shape[0]
    bias = bias_ref[...]
    for t in range(tiles):
        total = parts_ref[t].astype(F32)
        for k in range(1, n // tiles):
            total = total + parts_ref[k * tiles + t].astype(F32)
        out_ref[t, cols:, :] = jnp.maximum(total + bias, 0.0).astype(BF)
    acc[...] = jnp.zeros_like(acc)
    for k in range(values_ref.shape[0]):
        source = out_ref[index_ref[k, 1], cols:, :]
        target = index_ref[k, 0]
        acc[target] += lax.dot_general(source, values_ref[k], NT, preferred_element_type=F32)
    for t in range(tiles):
        out_ref[t, :cols, :] = acc[t].astype(BF)
        live = live_ref[t : t + 1, :].astype(BF)
        left_ref[:, t * width : (t + 1) * width] = out_ref[t] * live


def grad_kernel(left_ref, cot_ref, out_ref):
    pieces, piece_rows, piece_cols = out_ref.shape
    quarters = left_ref.shape[0] // piece_rows
    for c in range(pieces // quarters):
        cot = cot_ref[c * piece_cols : (c + 1) * piece_cols, :]
        block = lax.dot_general(left_ref[...], cot, NT, preferred_element_type=F32).astype(BF)
        for q in range(quarters):
            out_ref[c * quarters + q] = block[q * piece_rows : (q + 1) * piece_rows, :]


def body(
    edge_feats,
    edge_dst,
    self_feats,
    neigh_one,
    self_one,
    bias_one,
    tile_index,
    tile_values,
    seed_live,
    neigh_two,
    self_two,
    bias_two,
    cotangent,
):
    groups = lax.axis_size("dp")
    n_feat = lax.axis_size("feat")
    edges, cols = edge_feats.shape
    targets = self_feats.shape[0]
    hid = bias_one.shape[0]
    full = neigh_one.shape[1]
    cap = 2 * edges // groups
    tiles = targets // 128
    near = [[GROUP * i + j for j in range(GROUP)] for i in range(n_feat // GROUP)]

    with jax.named_scope("weights"):
        first_w = lax.all_gather(
            jnp.concatenate([neigh_one, self_one], axis=0),
            "feat", axis=0, tiled=True, axis_index_groups=near,
        )
        second_w = lax.all_gather(
            jnp.concatenate([neigh_two, self_two], axis=0),
            "feat", axis=0, tiled=True, axis_index_groups=near,
        )
    with jax.named_scope("cotangent"):
        full_cot = lax.all_gather(cotangent.T, "feat", axis=0, tiled=True)

    with jax.named_scope("edges"):
        send = call(
            functools.partial(pack_kernel, groups, targets),
            jax.ShapeDtypeStruct((groups, ROWS, cap), BF),
            2,
            scratch=[pltpu.VMEM((8 * ROWS, edges), BF)],
            flops=2 * groups * ROWS * edges * cap,
            nbytes=8 << 20,
        )(edge_feats.T, edge_dst.reshape(-1, 128))
        recv = lax.all_to_all(send, "dp", split_axis=0, concat_axis=0, tiled=True)
        acts = call(
            mean_kernel,
            jax.ShapeDtypeStruct((tiles, 2 * cols, 128), BF),
            2,
            flops=2 * groups * ROWS * cap * targets,
            nbytes=8 << 20,
        )(recv, self_feats.T)

    with jax.named_scope("first"):
        acts = lax.all_to_all(
            acts, "feat", split_axis=0, concat_axis=0, tiled=True, axis_index_groups=near
        )
        first = lax.dot_general(
            first_w, acts.reshape(-1, 128), TN, preferred_element_type=F32
        ).astype(BF)
        first = lax.all_to_all(
            first.reshape(n_feat, hid, 128), "feat", split_axis=0, concat_axis=0, tiled=True
        )
        pair, left = call(
            hidden_kernel,
            (
                jax.ShapeDtypeStruct((tiles, 2 * hid, 128), BF),
                jax.ShapeDtypeStruct((2 * hid, targets), BF),
            ),
            5,
            scratch=[pltpu.VMEM((tiles, hid, 128), F32)],
            smem=(2,),
            flops=2 * 4 * hid * 128 * 128,
            nbytes=4 << 20,
        )(
            first,
            bias_one.reshape(hid, 1),
            tile_index,
            tile_values,
            seed_live.reshape(tiles, 128).astype(F32),
        )

    with jax.named_scope("grads"):
        piece_rows = 2 * hid * full // 128 // groups
        terms = call(
            grad_kernel,
            jax.ShapeDtypeStruct((groups, piece_rows, 128), BF),
            2,
            flops=2 * 2 * hid * targets * full,
            nbytes=2 << 20,
        )(left, full_cot)
        terms = lax.all_to_all(terms, "dp", split_axis=0, concat_axis=0, tiled=True)
        mine = jnp.sum(terms.astype(F32), axis=0, keepdims=True)
        grads = lax.all_gather(mine, "dp", axis=0, tiled=True)
        grads = grads.reshape(full // 128, 2 * hid // piece_rows, piece_rows, 128)
        grads = grads.transpose(1, 2, 0, 3).reshape(2, hid, full)

    with jax.named_scope("second"):
        pair = lax.all_to_all(
            pair, "feat", split_axis=0, concat_axis=0, tiled=True, axis_index_groups=near
        )
        second = lax.dot_general(
            second_w, pair.reshape(-1, 128), TN, preferred_element_type=F32
        ).astype(BF)
        second = lax.all_to_all(
            second.reshape(n_feat, hid, 128), "feat", split_axis=0, concat_axis=0, tiled=True
        )
        second = jnp.sum(second.reshape(n_feat // tiles, tiles, hid, 128).astype(F32), axis=0)
        second = second + bias_two[None, :, None]
        second = second * seed_live.reshape(tiles, 1, 128).astype(F32)
        second_out = second.astype(BF).transpose(0, 2, 1).reshape(targets, hid)
    return (second_out, grads[0], grads[1])


def solution(mesh):
    in_specs = (
        P("dp", "feat"),
        P("dp"),
        P("dp", "feat"),
        P("feat", None),
        P("feat", None),
        P("feat"),
        P("dp", None),
        P("dp", None, None),
        P("dp"),
        P("feat", None),
        P("feat", None),
        P("feat"),
        P("dp", "feat"),
    )
    out_specs = (P("dp", "feat"), P("feat", None), P("feat", None))
    return jax.shard_map(body, mesh=mesh, in_specs=in_specs, out_specs=out_specs, check_vma=False)
```

```python
import functools

import jax
import jax.numpy as jnp
from jax import lax
from jax.experimental import pallas as pl
from jax.experimental.pallas import tpu as pltpu
from jax.sharding import PartitionSpec as P

BF = jnp.bfloat16
F32 = jnp.float32
NT = (((1,), (1,)), ((), ()))
TN = (((0,), (0,)), ((), ()))
ROWS = 64
GROUP = 4
VMEM_LIMIT = 48 * 1024 * 1024


def call(kernel, out_shape, n_in, scratch=(), smem=(), flops=0, nbytes=0):
    in_specs = [
        pl.BlockSpec(memory_space=pltpu.SMEM if i in smem else pltpu.VMEM) for i in range(n_in)
    ]
    out_specs = jax.tree.map(lambda _: pl.BlockSpec(memory_space=pltpu.VMEM), out_shape)
    return pl.pallas_call(
        kernel,
        out_shape=out_shape,
        in_specs=in_specs,
        out_specs=out_specs,
        scratch_shapes=list(scratch),
        compiler_params=pltpu.CompilerParams(vmem_limit_bytes=VMEM_LIMIT),
        cost_estimate=pl.CostEstimate(flops=flops, bytes_accessed=nbytes, transcendentals=0),
    )


def pack_kernel(groups, tgt_rows, feats_ref, dst_ref, send_ref, masked):
    cols, edges = feats_ref.shape
    cap = send_ref.shape[2]
    dst = jnp.concatenate([dst_ref[i : i + 1, :] for i in range(dst_ref.shape[0])], axis=1)
    owner = dst // tgt_rows
    local = dst - owner * tgt_rows
    half = tgt_rows // 2
    code = jnp.where(local < half, local - half, local - (half - 1)).astype(F32)
    owner_hot = lax.broadcasted_iota(jnp.int32, (groups, edges), 0) == owner
    owner_hot = owner_hot.astype(F32)
    step = 256
    before = (
        lax.broadcasted_iota(jnp.int32, (step, step), 0)
        < lax.broadcasted_iota(jnp.int32, (step, step), 1)
    ).astype(BF)
    seen = jnp.zeros((groups, 1), F32)
    ranks = []
    for i in range(edges // step):
        part = owner_hot[:, i * step : (i + 1) * step]
        prior = jnp.dot(part.astype(BF), before, preferred_element_type=F32) + seen
        ranks.append(jnp.sum(prior * part, axis=0, keepdims=True))
        seen = seen + jnp.sum(part, axis=1, keepdims=True)
    rank = jnp.concatenate(ranks, axis=1).astype(jnp.int32)
    rank_hot = (lax.broadcasted_iota(jnp.int32, (cap, edges), 0) == rank).astype(F32).astype(BF)
    extra_row = lax.broadcasted_iota(jnp.int32, (ROWS - cols, edges), 0)
    extra = jnp.where(extra_row == 0, code, jnp.where(extra_row == 1, 1.0, 0.0)).astype(BF)
    hot = owner_hot.astype(BF)
    some = masked.shape[0] // ROWS
    for g in range(groups // some):
        for j in range(some):
            o = g * some + j
            live = hot[o : o + 1, :]
            masked[j * ROWS : j * ROWS + cols, :] = feats_ref[...] * live
            masked[j * ROWS + cols : (j + 1) * ROWS, :] = extra * live
        out = lax.dot_general(masked[...], rank_hot, NT, preferred_element_type=F32).astype(BF)
        for j in range(some):
            send_ref[g * some + j] = out[j * ROWS : (j + 1) * ROWS, :]


def mean_kernel(recv_ref, self_ref, out_ref):
    groups, rows, cap = recv_ref.shape
    cols, targets = self_ref.shape
    tiles = out_ref.shape[0]
    half = targets // 2
    vertex = lax.broadcasted_iota(jnp.int32, (targets, 1), 0)
    vertex = jnp.where(vertex < half, vertex - half, vertex - (half - 1)).astype(F32)
    acc = jnp.zeros((rows, targets), F32)
    some = 8
    for g in range(groups // some):
        part = jnp.concatenate([recv_ref[g * some + j] for j in range(some)], axis=1)
        code = part[cols : cols + 1, :].astype(F32)
        hot = (vertex == code).astype(F32).astype(BF)
        acc = acc + lax.dot_general(part, hot, NT, preferred_element_type=F32)
    degree = jnp.maximum(acc[cols + 1 : cols + 2, :], 1.0)
    mean = (acc[:cols, :] / degree).astype(BF)
    width = targets // tiles
    for t in range(tiles):
        out_ref[t, :cols, :] = mean[:, t * width : (t + 1) * width]
        out_ref[t, cols:, :] = self_ref[:, t * width : (t + 1) * width]


def hidden_kernel(parts_ref, bias_ref, out_ref):
    n, cols, width = parts_ref.shape
    copies, tiles = out_ref.shape[:2]
    bias = bias_ref[...]
    for t in range(tiles):
        total = parts_ref[t].astype(F32)
        for k in range(1, n // tiles):
            total = total + parts_ref[k * tiles + t].astype(F32)
        hidden = jnp.maximum(total + bias, 0.0).astype(BF)
        for c in range(copies):
            out_ref[c, t] = hidden


def aggregate_kernel(mine_ref, hid_ref, index_ref, values_ref, live_ref, own_ref, left_ref, hidden, acc):
    group, tiles, cols, width = hid_ref.shape
    wide = group * cols
    for t in range(tiles):
        for j in range(group):
            hidden[t, j * cols : (j + 1) * cols, :] = hid_ref[j, t]
    acc[...] = jnp.zeros_like(acc)
    for k in range(values_ref.shape[0]):
        source = hidden[index_ref[k, 1]]
        target = index_ref[k, 0]
        acc[target] += lax.dot_general(source, values_ref[k], NT, preferred_element_type=F32)
    for t in range(tiles):
        live = live_ref[t : t + 1, :].astype(BF)
        at = slice(t * width, (t + 1) * width)
        left_ref[:wide, at] = acc[t].astype(BF) * live
        left_ref[wide:, at] = hidden[t] * live
    mine = mine_ref[0]
    agg = acc[mine].astype(BF)
    hid = hidden[mine]
    for j in range(group):
        own_ref[j, :cols, :] = agg[j * cols : (j + 1) * cols, :]
        own_ref[j, cols:, :] = hid[j * cols : (j + 1) * cols, :]


def grad_kernel(left_ref, cot_ref, out_ref):
    group = 4
    rows, width = left_ref.shape[0], 128
    block = lax.dot_general(left_ref[...], cot_ref[...], NT, preferred_element_type=F32)
    wide = rows // 2
    cols = wide // group
    at = 0
    for w in range(2):
        for r in range(0, cols, 8):
            for c in range(0, cot_ref.shape[0], width):
                rows_of = [
                    block[w * wide + j * cols + r : w * wide + j * cols + r + 8, c : c + width]
                    for j in range(group)
                ]
                out_ref[at] = jnp.concatenate(rows_of, axis=0).astype(BF)
                at += 1


def place_kernel(pieces_ref, neigh_ref, self_ref):
    half = 64
    at = 0
    for out_ref in (neigh_ref, self_ref):
        for r in range(0, out_ref.shape[0], 8):
            for c in range(2):
                parts = [pieces_ref[at, h] for h in range(4)]
                for e in range(2):
                    for p in range(2):
                        pair = [parts[2 * p + i][:, e * half : (e + 1) * half] for i in range(2)]
                        to = (8 * c + 4 * e + 2 * p) * half
                        out_ref[r : r + 8, to : to + 2 * half] = jnp.concatenate(pair, axis=1)
                at += 1


def body(
    edge_feats,
    edge_dst,
    self_feats,
    neigh_one,
    self_one,
    bias_one,
    tile_index,
    tile_values,
    seed_live,
    neigh_two,
    self_two,
    bias_two,
    cotangent,
):
    groups = lax.axis_size("dp")
    n_feat = lax.axis_size("feat")
    edges, cols = edge_feats.shape
    targets = self_feats.shape[0]
    hid = bias_one.shape[0]
    full = neigh_one.shape[1]
    cap = 2 * edges // groups
    tiles = targets // 128
    blocks = n_feat // GROUP
    near = [[GROUP * i + j for j in range(GROUP)] for i in range(blocks)]
    far = [[i + GROUP * j for j in range(blocks)] for i in range(GROUP)]

    def swap(x, axis, among=None):
        return lax.all_to_all(
            x, axis, split_axis=0, concat_axis=0, tiled=True, axis_index_groups=among
        )

    def spread(x, n, axis, among=None):
        return swap(jnp.broadcast_to(x[None], (n,) + x.shape), axis, among)

    with jax.named_scope("weights"):
        first_w = spread(jnp.concatenate([neigh_one, self_one], axis=0), GROUP, "feat", near)
        second_w = spread(jnp.concatenate([neigh_two, self_two], axis=0), GROUP, "feat", near)
    with jax.named_scope("cotangent"):
        cot = spread(cotangent.T, blocks, "feat", far).reshape(blocks * hid, targets)

    with jax.named_scope("edges"):
        send = call(
            functools.partial(pack_kernel, groups, targets),
            jax.ShapeDtypeStruct((groups, ROWS, cap), BF),
            2,
            scratch=[pltpu.VMEM((8 * ROWS, edges), BF)],
            flops=2 * groups * ROWS * edges * cap,
            nbytes=8 << 20,
        )(edge_feats.T, edge_dst.reshape(-1, 128))
        recv = swap(send, "dp")
        acts = call(
            mean_kernel,
            jax.ShapeDtypeStruct((tiles, 2 * cols, 128), BF),
            2,
            flops=2 * groups * ROWS * cap * targets,
            nbytes=8 << 20,
        )(recv, self_feats.T)

    with jax.named_scope("first"):
        acts = swap(acts, "feat", near)
        first = lax.dot_general(
            first_w.reshape(-1, full), acts.reshape(-1, 128), TN, preferred_element_type=F32
        ).astype(BF)
        first = swap(first.reshape(n_feat, hid, 128), "feat")
        hidden = call(
            hidden_kernel,
            jax.ShapeDtypeStruct((GROUP, tiles, hid, 128), BF),
            2,
            nbytes=1 << 20,
        )(first, bias_one.reshape(hid, 1))
        hidden = swap(hidden, "feat", near)
        live = seed_live.reshape(tiles, 128).astype(F32)
        own, left = call(
            aggregate_kernel,
            (
                jax.ShapeDtypeStruct((GROUP, 2 * hid, 128), BF),
                jax.ShapeDtypeStruct((2 * GROUP * hid, targets), BF),
            ),
            5,
            scratch=[
                pltpu.VMEM((tiles, GROUP * hid, 128), BF),
                pltpu.VMEM((tiles, GROUP * hid, 128), F32),
            ],
            smem=(0, 2),
            flops=2 * 4 * GROUP * hid * 128 * 128,
            nbytes=4 << 20,
        )((lax.axis_index("feat") % GROUP).reshape(1), hidden, tile_index, tile_values, live)

    with jax.named_scope("grads"):
        terms = call(
            grad_kernel,
            jax.ShapeDtypeStruct((groups, GROUP * 8, 128), BF),
            2,
            flops=2 * 2 * hid * targets * full,
            nbytes=2 << 20,
        )(left, cot)
        terms = swap(terms, "dp")
        mine = jnp.sum(terms.astype(F32), axis=0).reshape(GROUP, 8, 128)
        mine = swap(mine, "feat", near)
        pieces = spread(mine, groups, "dp")
        grad_neigh, grad_self = call(
            place_kernel,
            (jax.ShapeDtypeStruct((hid, full), F32), jax.ShapeDtypeStruct((hid, full), F32)),
            1,
            nbytes=1 << 20,
        )(pieces)

    with jax.named_scope("second"):
        second = lax.dot_general(
            second_w.reshape(-1, full), own.reshape(-1, 128), TN, preferred_element_type=F32
        ).astype(BF)
        second = swap(second.reshape(n_feat, hid, 128), "feat")
        second = jnp.sum(second.reshape(blocks, tiles, hid, 128).astype(F32), axis=0)
        second = second + bias_two[None, :, None]
        second = second * live[:, None, :]
        second_out = second.astype(BF).transpose(0, 2, 1).reshape(targets, hid)
    return (second_out, grad_neigh, grad_self)


def solution(mesh):
    in_specs = (
        P("dp", "feat"),
        P("dp"),
        P("dp", "feat"),
        P("feat", None),
        P("feat", None),
        P("feat"),
        P("dp", None),
        P("dp", None, None),
        P("dp"),
        P("feat", None),
        P("feat", None),
        P("feat"),
        P("dp", "feat"),
    )
    out_specs = (P("dp", "feat"), P("feat", None), P("feat", None))
    return jax.shard_map(body, mesh=mesh, in_specs=in_specs, out_specs=out_specs, check_vma=False)
```

```python
import functools

import jax
import jax.numpy as jnp
from jax import lax
from jax.experimental import pallas as pl
from jax.experimental.pallas import tpu as pltpu
from jax.sharding import PartitionSpec as P

BF = jnp.bfloat16
F32 = jnp.float32
NT = (((1,), (1,)), ((), ()))
TN = (((0,), (0,)), ((), ()))
ROWS = 64
GROUP = 4
VMEM_LIMIT = 48 * 1024 * 1024


def call(kernel, out_shape, n_in, scratch=(), smem=(), late=(), flops=0, nbytes=0):
    spaces = {i: pltpu.SMEM for i in smem} | {i: pl.ANY for i in late}
    in_specs = [pl.BlockSpec(memory_space=spaces.get(i, pltpu.VMEM)) for i in range(n_in)]
    out_specs = jax.tree.map(lambda _: pl.BlockSpec(memory_space=pltpu.VMEM), out_shape)
    return pl.pallas_call(
        kernel,
        out_shape=out_shape,
        in_specs=in_specs,
        out_specs=out_specs,
        scratch_shapes=list(scratch),
        compiler_params=pltpu.CompilerParams(vmem_limit_bytes=VMEM_LIMIT),
        cost_estimate=pl.CostEstimate(flops=flops, bytes_accessed=nbytes, transcendentals=0),
    )


def pack_kernel(groups, tgt_rows, feats_ref, dst_ref, send_ref, masked):
    cols, edges = feats_ref.shape
    cap = send_ref.shape[2]
    dst = jnp.concatenate([dst_ref[i : i + 1, :] for i in range(dst_ref.shape[0])], axis=1)
    owner = dst // tgt_rows
    local = dst - owner * tgt_rows
    half = tgt_rows // 2
    code = jnp.where(local < half, local - half, local - (half - 1)).astype(F32)
    owner_hot = lax.broadcasted_iota(jnp.int32, (groups, edges), 0) == owner
    owner_hot = owner_hot.astype(F32)
    step = 256
    before = (
        lax.broadcasted_iota(jnp.int32, (step, step), 0)
        < lax.broadcasted_iota(jnp.int32, (step, step), 1)
    ).astype(BF)
    seen = jnp.zeros((groups, 1), F32)
    ranks = []
    for i in range(edges // step):
        part = owner_hot[:, i * step : (i + 1) * step]
        prior = jnp.dot(part.astype(BF), before, preferred_element_type=F32) + seen
        ranks.append(jnp.sum(prior * part, axis=0, keepdims=True))
        seen = seen + jnp.sum(part, axis=1, keepdims=True)
    rank = jnp.concatenate(ranks, axis=1).astype(jnp.int32)
    rank_hot = (lax.broadcasted_iota(jnp.int32, (cap, edges), 0) == rank).astype(F32).astype(BF)
    extra_row = lax.broadcasted_iota(jnp.int32, (ROWS - cols, edges), 0)
    extra = jnp.where(extra_row == 0, code, jnp.where(extra_row == 1, 1.0, 0.0)).astype(BF)
    hot = owner_hot.astype(BF)
    some = masked.shape[0] // ROWS
    for g in range(groups // some):
        for j in range(some):
            o = g * some + j
            live = hot[o : o + 1, :]
            masked[j * ROWS : j * ROWS + cols, :] = feats_ref[...] * live
            masked[j * ROWS + cols : (j + 1) * ROWS, :] = extra * live
        out = lax.dot_general(masked[...], rank_hot, NT, preferred_element_type=F32).astype(BF)
        for j in range(some):
            send_ref[g * some + j] = out[j * ROWS : (j + 1) * ROWS, :]


def column_sets(weight, group):
    half = 64
    n = weight.shape[1] // half
    sets = []
    for j in range(group):
        blocks = [weight[:, b * half : (b + 1) * half] for b in range(j, n, group)]
        sets.append(jnp.concatenate(blocks, axis=1))
    return sets


def first_pieces_kernel(mine_ref, neigh_ref, own_ref, self_ref, cot_ref, late_ref, out_ref, cot_out_ref):
    del late_ref
    mine = mine_ref[0]
    rows = neigh_ref.shape[0]
    group, _, width = out_ref.shape
    both = zip(column_sets(neigh_ref[...], group), column_sets(own_ref[...], group))
    for j, (neigh, own) in enumerate(both):
        to = jnp.bitwise_xor(mine, j)
        out_ref[to, :rows, :] = neigh
        out_ref[to, rows : 2 * rows, :] = own
        out_ref[to, 2 * rows : 3 * rows, :] = self_ref[:, :width]
        out_ref[to, 3 * rows :, :] = self_ref[:, width:]
    cot_out_ref[...] = cot_ref[...]


def second_pieces_kernel(mine_ref, neigh_ref, own_ref, late_ref, out_ref):
    del late_ref
    mine = mine_ref[0]
    rows = neigh_ref.shape[0]
    both = zip(column_sets(neigh_ref[...], out_ref.shape[0]), column_sets(own_ref[...], out_ref.shape[0]))
    for j, (neigh, own) in enumerate(both):
        to = jnp.bitwise_xor(mine, j)
        out_ref[to, :rows, :] = neigh
        out_ref[to, rows:, :] = own


def mean_kernel(cols, recv_ref, cot_ref, far_ref, late1_ref, late2_ref, late3_ref, out_ref, cots_ref):
    del late1_ref, late2_ref, late3_ref
    groups, rows, cap = recv_ref.shape
    targets = out_ref.shape[2]
    half = targets // 2
    vertex = lax.broadcasted_iota(jnp.int32, (targets, 1), 0)
    vertex = jnp.where(vertex < half, vertex - half, vertex - (half - 1)).astype(F32)
    acc = jnp.zeros((rows, targets), F32)
    some = 8
    for g in range(groups // some):
        part = jnp.concatenate([recv_ref[g * some + j] for j in range(some)], axis=1)
        code = part[cols : cols + 1, :].astype(F32)
        hot = (vertex == code).astype(F32).astype(BF)
        acc = acc + lax.dot_general(part, hot, NT, preferred_element_type=F32)
    degree = jnp.maximum(acc[cols + 1 : cols + 2, :], 1.0)
    mean = (acc[:cols, :] / degree).astype(BF)
    for j in range(out_ref.shape[0]):
        out_ref[j] = mean
    cots_ref[0] = cot_ref[...]
    cots_ref[1] = far_ref[...]


def first_kernel(mine_ref, mean_ref, p0_ref, p1_ref, p2_ref, p3_ref, out_ref, weight, acts):
    mine = mine_ref[0]
    group, rows, targets = mean_ref.shape
    width = targets // 2
    for k, piece in enumerate((p0_ref, p1_ref, p2_ref, p3_ref)):
        at = slice(2 * rows * k, 2 * rows * (k + 1))
        mid = 2 * rows * k + rows
        weight[at, :] = piece[: 2 * rows, :]
        acts[2 * rows * k : mid, :] = mean_ref[jnp.bitwise_xor(mine, k)]
        acts[mid : mid + rows, :width] = piece[2 * rows : 3 * rows, :]
        acts[mid : mid + rows, width:] = piece[3 * rows :, :]
    total = lax.dot_general(weight[...], acts[...], TN, preferred_element_type=F32)
    n, cols, _ = out_ref.shape
    for z in range(n):
        out_ref[z] = total[z * cols : (z + 1) * cols, :].astype(BF)


def hidden_kernel(parts_ref, bias_ref, late_ref, out_ref):
    del late_ref
    total = parts_ref[0].astype(F32)
    for k in range(1, parts_ref.shape[0]):
        total = total + parts_ref[k].astype(F32)
    hidden = jnp.maximum(total + bias_ref[...], 0.0).astype(BF)
    for c in range(out_ref.shape[0]):
        out_ref[c] = hidden


def grad_kernel(
    place_ref, index_ref, hid_ref, values_ref, live_ref, near_ref, far_ref, agg_ref, out_ref, left, cot, acc
):
    group, cols, targets = hid_ref.shape
    width = values_ref.shape[1]
    wide = group * cols
    across = place_ref[0]
    for k, ref in enumerate((near_ref, near_ref, far_ref, far_ref)):
        cot[jnp.bitwise_xor(across, k)] = ref[k % 2]
    acc[...] = jnp.zeros_like(acc)
    for k in range(values_ref.shape[0]):
        source = index_ref[k, 1]
        at = pl.ds(pl.multiple_of(source * width, width), width)
        rows = jnp.concatenate([hid_ref[j, :, at] for j in range(group)], axis=0)
        target = index_ref[k, 0]
        acc[target] += lax.dot_general(rows, values_ref[k], NT, preferred_element_type=F32)
    live = live_ref[...].astype(BF)
    for t in range(targets // width):
        at = slice(t * width, (t + 1) * width)
        tile = acc[t].astype(BF)
        agg_ref[:, at] = tile
        left[:wide, at] = tile * live[:, at]
    for j in range(group):
        left[wide + j * cols : wide + (j + 1) * cols, :] = hid_ref[j] * live
    right = jnp.concatenate([cot[j] for j in range(group)], axis=0)
    block = lax.dot_general(left[...], right, NT, preferred_element_type=F32)
    at = 0
    for w in range(2):
        for r in range(0, cols, 8):
            for c in range(0, right.shape[0], 128):
                rows_of = [
                    block[w * wide + j * cols + r : w * wide + j * cols + r + 8, c : c + 128]
                    for j in range(group)
                ]
                out_ref[at] = jnp.concatenate(rows_of, axis=0).astype(BF)
                at += 1


def second_kernel(mine_ref, agg_ref, hid_ref, p0_ref, p1_ref, p2_ref, p3_ref, out_ref, weight, acts):
    mine = mine_ref[0]
    group, rows, targets = hid_ref.shape
    for k, piece in enumerate((p0_ref, p1_ref, p2_ref, p3_ref)):
        weight[jnp.bitwise_xor(mine, k)] = piece[...]
    for j in range(group):
        acts[2 * rows * j : 2 * rows * j + rows, :] = agg_ref[j * rows : (j + 1) * rows, :]
        acts[2 * rows * j + rows : 2 * rows * (j + 1), :] = hid_ref[j]
    both = jnp.concatenate([weight[j] for j in range(group)], axis=0)
    total = lax.dot_general(both, acts[...], TN, preferred_element_type=F32)
    n, cols, _ = out_ref.shape
    for z in range(n):
        out_ref[z] = total[z * cols : (z + 1) * cols, :].astype(BF)


def sum_kernel(mine_ref, terms_ref, out_ref):
    mine = mine_ref[0]
    total = terms_ref[0].astype(F32)
    for d in range(1, terms_ref.shape[0]):
        total = total + terms_ref[d].astype(F32)
    rows = out_ref.shape[1]
    for j in range(out_ref.shape[0]):
        out_ref[jnp.bitwise_xor(mine, j)] = total[j * rows : (j + 1) * rows, :]


def copies_kernel(p0_ref, p1_ref, p2_ref, p3_ref, late_ref, out_ref):
    del late_ref
    whole = jnp.concatenate([p0_ref[...], p1_ref[...], p2_ref[...], p3_ref[...]], axis=0)
    for d in range(out_ref.shape[0]):
        out_ref[d] = whole


def place_kernel(mine_ref, pieces_ref, neigh_ref, self_ref):
    mine = mine_ref[0]
    half = 64
    at = 0
    for out_ref in (neigh_ref, self_ref):
        for r in range(0, out_ref.shape[0], 8):
            for c in range(2):
                parts = [
                    pieces_ref[at, pl.ds(pl.multiple_of(jnp.bitwise_xor(mine, h) * 8, 8), 8), :]
                    for h in range(4)
                ]
                for e in range(2):
                    for p in range(2):
                        pair = [parts[2 * p + i][:, e * half : (e + 1) * half] for i in range(2)]
                        to = (8 * c + 4 * e + 2 * p) * half
                        out_ref[r : r + 8, to : to + 2 * half] = jnp.concatenate(pair, axis=1)
                at += 1


def out_kernel(parts_ref, bias_ref, live_ref, out_ref):
    total = parts_ref[0].astype(F32)
    for k in range(1, parts_ref.shape[0]):
        total = total + parts_ref[k].astype(F32)
    out_ref[...] = ((total + bias_ref[...]) * live_ref[...]).astype(BF)


def body(
    edge_feats,
    edge_dst,
    self_feats,
    neigh_one,
    self_one,
    bias_one,
    tile_index,
    tile_values,
    seed_live,
    neigh_two,
    self_two,
    bias_two,
    cotangent,
):
    groups = lax.axis_size("dp")
    n_feat = lax.axis_size("feat")
    edges, cols = edge_feats.shape
    targets = self_feats.shape[0]
    hid = bias_one.shape[0]
    full = neigh_one.shape[1]
    cap = 2 * edges // groups
    blocks = n_feat // GROUP
    wide = full // GROUP
    near = [[GROUP * i + j for j in range(GROUP)] for i in range(blocks)]
    far = [[i + GROUP * j for j in range(blocks)] for i in range(GROUP)]
    z = lax.axis_index("feat")
    mine = (z % GROUP).reshape(1)
    across = (z // GROUP).reshape(1)
    live = seed_live.reshape(1, targets).astype(F32)

    def swap(x, axis, among=None):
        return lax.all_to_all(
            x, axis, split_axis=0, concat_axis=0, tiled=True, axis_index_groups=among
        )

    def trade(x, k):
        return lax.ppermute(x, "feat", [(i, i ^ k) for i in range(n_feat)])

    def shape(*dims, dtype=BF):
        return jax.ShapeDtypeStruct(dims, dtype)

    with jax.named_scope("edges"):
        send = call(
            functools.partial(pack_kernel, groups, targets),
            shape(groups, ROWS, cap),
            2,
            scratch=[pltpu.VMEM((8 * ROWS, edges), BF)],
            flops=2 * groups * ROWS * edges * cap,
            nbytes=8 << 20,
        )(edge_feats.T, edge_dst.reshape(-1, 128))
        recv = swap(send, "dp")
    with jax.named_scope("pieces"):
        pieces, cot = call(
            first_pieces_kernel,
            (shape(GROUP, 4 * cols, wide), shape(hid, targets)),
            6,
            smem=(0,),
            late=(5,),
            nbytes=2 << 20,
        )(mine, neigh_one, self_one, self_feats.T, cotangent.T, send)
        got = [trade(pieces[k], k) for k in range(1, GROUP)]
        cot_far = trade(cot, GROUP)
    with jax.named_scope("mean"):
        mean, cots = call(
            functools.partial(mean_kernel, cols),
            (shape(GROUP, cols, targets), shape(2, hid, targets)),
            6,
            late=(3, 4, 5),
            flops=2 * groups * ROWS * cap * targets,
            nbytes=8 << 20,
        )(recv, cot, cot_far, *got)
        cots_far = trade(cots, 2 * GROUP)
        mean = swap(mean, "feat", near)
    with jax.named_scope("first"):
        first = call(
            first_kernel,
            shape(blocks, hid, targets),
            6,
            scratch=[pltpu.VMEM((8 * cols, wide), BF), pltpu.VMEM((8 * cols, targets), BF)],
            smem=(0,),
            flops=2 * 8 * cols * wide * targets,
            nbytes=2 << 20,
        )(mine, mean, pieces[0], *got)
        first = swap(first, "feat", far)
        hidden = call(
            hidden_kernel, shape(GROUP, hid, targets), 3, late=(2,), nbytes=1 << 20
        )(first, bias_one.reshape(hid, 1), cots_far)
        hidden = swap(hidden, "feat", near)
    with jax.named_scope("grads"):
        agg, terms = call(
            grad_kernel,
            (shape(wide, targets), shape(groups, GROUP * 8, 128)),
            7,
            scratch=[
                pltpu.VMEM((2 * wide, targets), BF),
                pltpu.VMEM((blocks, hid, targets), BF),
                pltpu.VMEM((targets // 128, wide, 128), F32),
            ],
            smem=(0, 1),
            flops=2 * 2 * wide * targets * wide,
            nbytes=4 << 20,
        )(across, tile_index, hidden, tile_values, live, cots, cots_far)
        terms = swap(terms, "dp")
        mine_sum = call(
            sum_kernel, shape(GROUP, 8, 128, dtype=F32), 2, smem=(0,), nbytes=1 << 20
        )(mine, terms)
        sums = [mine_sum[0]] + [trade(mine_sum[k], k) for k in range(1, GROUP)]
    with jax.named_scope("second"):
        pieces = call(
            second_pieces_kernel,
            shape(GROUP, 2 * hid, wide),
            4,
            smem=(0,),
            late=(3,),
            nbytes=1 << 20,
        )(mine, neigh_two, self_two, agg)
        got = [trade(pieces[k], k) for k in range(1, GROUP)]
        second = call(
            second_kernel,
            shape(blocks, hid, targets),
            7,
            scratch=[pltpu.VMEM((GROUP, 2 * hid, wide), BF), pltpu.VMEM((2 * wide, targets), BF)],
            smem=(0,),
            flops=2 * 2 * wide * wide * targets,
            nbytes=2 << 20,
        )(mine, agg, hidden, pieces[0], *got)
        second = swap(second, "feat", far)
        second_out = call(out_kernel, shape(hid, targets), 3, nbytes=1 << 20)(
            second, bias_two.reshape(hid, 1), live
        ).T
    with jax.named_scope("place"):
        spread = call(
            copies_kernel, shape(groups, GROUP * 8, 128, dtype=F32), 5, late=(4,), nbytes=1 << 20
        )(*sums, second)
        spread = swap(spread, "dp")
        grad_neigh, grad_self = call(
            place_kernel,
            (shape(hid, full, dtype=F32), shape(hid, full, dtype=F32)),
            2,
            smem=(0,),
            nbytes=1 << 20,
        )(mine, spread)
    return (second_out, grad_neigh, grad_self)


def solution(mesh):
    in_specs = (
        P("dp", "feat"),
        P("dp"),
        P("dp", "feat"),
        P("feat", None),
        P("feat", None),
        P("feat"),
        P("dp", None),
        P("dp", None, None),
        P("dp"),
        P("feat", None),
        P("feat", None),
        P("feat"),
        P("dp", "feat"),
    )
    out_specs = (P("dp", "feat"), P("feat", None), P("feat", None))
    return jax.shard_map(body, mesh=mesh, in_specs=in_specs, out_specs=out_specs, check_vma=False)
```

```python
import functools

import jax
import jax.numpy as jnp
from jax import lax
from jax.experimental import pallas as pl
from jax.experimental.pallas import tpu as pltpu
from jax.sharding import PartitionSpec as P

BF = jnp.bfloat16
F32 = jnp.float32
NT = (((1,), (1,)), ((), ()))
TN = (((0,), (0,)), ((), ()))
ROWS = 64
GROUP = 4
VMEM_LIMIT = 48 * 1024 * 1024


def call(kernel, out_shape, n_in, scratch=(), smem=(), late=(), flops=0, nbytes=0):
    spaces = {i: pltpu.SMEM for i in smem} | {i: pl.ANY for i in late}
    in_specs = [pl.BlockSpec(memory_space=spaces.get(i, pltpu.VMEM)) for i in range(n_in)]
    out_specs = jax.tree.map(lambda _: pl.BlockSpec(memory_space=pltpu.VMEM), out_shape)
    return pl.pallas_call(
        kernel,
        out_shape=out_shape,
        in_specs=in_specs,
        out_specs=out_specs,
        scratch_shapes=list(scratch),
        compiler_params=pltpu.CompilerParams(vmem_limit_bytes=VMEM_LIMIT),
        cost_estimate=pl.CostEstimate(flops=flops, bytes_accessed=nbytes, transcendentals=0),
    )


def pack_kernel(groups, tgt_rows, feats_ref, dst_ref, send_ref, masked):
    cols, edges = feats_ref.shape
    cap = send_ref.shape[2]
    dst = jnp.concatenate([dst_ref[i : i + 1, :] for i in range(dst_ref.shape[0])], axis=1)
    owner = dst // tgt_rows
    local = dst - owner * tgt_rows
    half = tgt_rows // 2
    code = jnp.where(local < half, local - half, local - (half - 1)).astype(F32)
    owner_hot = lax.broadcasted_iota(jnp.int32, (groups, edges), 0) == owner
    owner_hot = owner_hot.astype(F32)
    step = 256
    before = (
        lax.broadcasted_iota(jnp.int32, (step, step), 0)
        < lax.broadcasted_iota(jnp.int32, (step, step), 1)
    ).astype(BF)
    seen = jnp.zeros((groups, 1), F32)
    ranks = []
    for i in range(edges // step):
        part = owner_hot[:, i * step : (i + 1) * step]
        prior = jnp.dot(part.astype(BF), before, preferred_element_type=F32) + seen
        ranks.append(jnp.sum(prior * part, axis=0, keepdims=True))
        seen = seen + jnp.sum(part, axis=1, keepdims=True)
    rank = jnp.concatenate(ranks, axis=1).astype(jnp.int32)
    rank_hot = (lax.broadcasted_iota(jnp.int32, (cap, edges), 0) == rank).astype(F32).astype(BF)
    extra_row = lax.broadcasted_iota(jnp.int32, (ROWS - cols, edges), 0)
    extra = jnp.where(extra_row == 0, code, jnp.where(extra_row == 1, 1.0, 0.0)).astype(BF)
    hot = owner_hot.astype(BF)
    some = masked.shape[0] // ROWS
    for g in range(groups // some):
        for j in range(some):
            o = g * some + j
            live = hot[o : o + 1, :]
            masked[j * ROWS : j * ROWS + cols, :] = feats_ref[...] * live
            masked[j * ROWS + cols : (j + 1) * ROWS, :] = extra * live
        out = lax.dot_general(masked[...], rank_hot, NT, preferred_element_type=F32).astype(BF)
        for j in range(some):
            send_ref[g * some + j] = out[j * ROWS : (j + 1) * ROWS, :]


def column_sets(weight, group):
    half = 64
    n = weight.shape[1] // half
    sets = []
    for j in range(group):
        blocks = [weight[:, b * half : (b + 1) * half] for b in range(j, n, group)]
        sets.append(jnp.concatenate(blocks, axis=1))
    return sets


def first_pieces_kernel(mine_ref, neigh_ref, own_ref, self_ref, late_ref, out_ref):
    del late_ref
    mine = mine_ref[0]
    rows = neigh_ref.shape[0]
    group, _, width = out_ref.shape
    both = zip(column_sets(neigh_ref[...], group), column_sets(own_ref[...], group))
    for j, (neigh, own) in enumerate(both):
        to = jnp.bitwise_xor(mine, j)
        out_ref[to, :rows, :] = neigh
        out_ref[to, rows : 2 * rows, :] = own
        out_ref[to, 2 * rows : 3 * rows, :] = self_ref[:, :width]
        out_ref[to, 3 * rows :, :] = self_ref[:, width:]


def second_pieces_kernel(mine_ref, neigh_ref, own_ref, late_ref, out_ref):
    del late_ref
    mine = mine_ref[0]
    rows = neigh_ref.shape[0]
    both = zip(column_sets(neigh_ref[...], out_ref.shape[0]), column_sets(own_ref[...], out_ref.shape[0]))
    for j, (neigh, own) in enumerate(both):
        to = jnp.bitwise_xor(mine, j)
        out_ref[to, :rows, :] = neigh
        out_ref[to, rows:, :] = own


def mean_kernel(cols, recv_ref, late1_ref, late2_ref, late3_ref, out_ref):
    del late1_ref, late2_ref, late3_ref
    groups, rows, cap = recv_ref.shape
    targets = out_ref.shape[2]
    half = targets // 2
    vertex = lax.broadcasted_iota(jnp.int32, (targets, 1), 0)
    vertex = jnp.where(vertex < half, vertex - half, vertex - (half - 1)).astype(F32)
    acc = jnp.zeros((rows, targets), F32)
    some = 8
    for g in range(groups // some):
        part = jnp.concatenate([recv_ref[g * some + j] for j in range(some)], axis=1)
        code = part[cols : cols + 1, :].astype(F32)
        hot = (vertex == code).astype(F32).astype(BF)
        acc = acc + lax.dot_general(part, hot, NT, preferred_element_type=F32)
    degree = jnp.maximum(acc[cols + 1 : cols + 2, :], 1.0)
    mean = (acc[:cols, :] / degree).astype(BF)
    for j in range(out_ref.shape[0]):
        out_ref[j] = mean


def first_kernel(
    mine_ref, mean_ref, p0_ref, p1_ref, p2_ref, p3_ref, cot_ref, out_ref, weight, acts
):
    mine = mine_ref[0]
    group, rows, targets = mean_ref.shape
    width = targets // 2
    for k, piece in enumerate((p0_ref, p1_ref, p2_ref, p3_ref)):
        at = slice(2 * rows * k, 2 * rows * (k + 1))
        mid = 2 * rows * k + rows
        weight[at, :] = piece[: 2 * rows, :]
        acts[2 * rows * k : mid, :] = mean_ref[jnp.bitwise_xor(mine, k)]
        acts[mid : mid + rows, :width] = piece[2 * rows : 3 * rows, :]
        acts[mid : mid + rows, width:] = piece[3 * rows :, :]
    total = lax.dot_general(weight[...], acts[...], TN, preferred_element_type=F32)
    cols = cot_ref.shape[0]
    for z in range(out_ref.shape[0]):
        out_ref[z, :cols, :] = total[z * cols : (z + 1) * cols, :].astype(BF)
        out_ref[z, cols:, :] = cot_ref[...]


def hidden_kernel(parts_ref, bias_ref, late1_ref, late2_ref, late3_ref, out_ref):
    del late1_ref, late2_ref, late3_ref
    cols = bias_ref.shape[0]
    total = parts_ref[0, :cols, :].astype(F32)
    for k in range(1, parts_ref.shape[0]):
        total = total + parts_ref[k, :cols, :].astype(F32)
    hidden = jnp.maximum(total + bias_ref[...], 0.0).astype(BF)
    for c in range(out_ref.shape[0]):
        out_ref[c] = hidden


def grad_kernel(index_ref, hid_ref, values_ref, live_ref, parts_ref, agg_ref, out_ref, left, acc):
    group, cols, targets = hid_ref.shape
    width = values_ref.shape[1]
    wide = group * cols
    acc[...] = jnp.zeros_like(acc)
    for k in range(values_ref.shape[0]):
        source = index_ref[k, 1]
        at = pl.ds(pl.multiple_of(source * width, width), width)
        rows = jnp.concatenate([hid_ref[j, :, at] for j in range(group)], axis=0)
        target = index_ref[k, 0]
        acc[target] += lax.dot_general(rows, values_ref[k], NT, preferred_element_type=F32)
    live = live_ref[...].astype(BF)
    for t in range(targets // width):
        at = slice(t * width, (t + 1) * width)
        tile = acc[t].astype(BF)
        agg_ref[:, at] = tile
        left[:wide, at] = tile * live[:, at]
    for j in range(group):
        left[wide + j * cols : wide + (j + 1) * cols, :] = hid_ref[j] * live
    right = jnp.concatenate([parts_ref[j, cols:, :] for j in range(parts_ref.shape[0])], axis=0)
    block = lax.dot_general(left[...], right, NT, preferred_element_type=F32)
    at = 0
    for w in range(2):
        for r in range(0, cols, 8):
            for c in range(0, right.shape[0], 128):
                rows_of = [
                    block[w * wide + j * cols + r : w * wide + j * cols + r + 8, c : c + 128]
                    for j in range(group)
                ]
                out_ref[at] = jnp.concatenate(rows_of, axis=0).astype(BF)
                at += 1


def second_kernel(mine_ref, agg_ref, hid_ref, p0_ref, p1_ref, p2_ref, p3_ref, out_ref, weight, acts):
    mine = mine_ref[0]
    group, rows, targets = hid_ref.shape
    for k, piece in enumerate((p0_ref, p1_ref, p2_ref, p3_ref)):
        weight[jnp.bitwise_xor(mine, k)] = piece[...]
    for j in range(group):
        acts[2 * rows * j : 2 * rows * j + rows, :] = agg_ref[j * rows : (j + 1) * rows, :]
        acts[2 * rows * j + rows : 2 * rows * (j + 1), :] = hid_ref[j]
    both = jnp.concatenate([weight[j] for j in range(group)], axis=0)
    total = lax.dot_general(both, acts[...], TN, preferred_element_type=F32)
    n, cols, _ = out_ref.shape
    for z in range(n):
        out_ref[z] = total[z * cols : (z + 1) * cols, :].astype(BF)


def sum_kernel(mine_ref, terms_ref, out_ref):
    mine = mine_ref[0]
    total = terms_ref[0].astype(F32)
    for d in range(1, terms_ref.shape[0]):
        total = total + terms_ref[d].astype(F32)
    rows = out_ref.shape[1]
    for j in range(out_ref.shape[0]):
        out_ref[jnp.bitwise_xor(mine, j)] = total[j * rows : (j + 1) * rows, :]


def copies_kernel(p0_ref, p1_ref, p2_ref, p3_ref, late_ref, out_ref):
    del late_ref
    whole = jnp.concatenate([p0_ref[...], p1_ref[...], p2_ref[...], p3_ref[...]], axis=0)
    for d in range(out_ref.shape[0]):
        out_ref[d] = whole


def place_kernel(mine_ref, pieces_ref, neigh_ref, self_ref):
    mine = mine_ref[0]
    half = 64
    at = 0
    for out_ref in (neigh_ref, self_ref):
        for r in range(0, out_ref.shape[0], 8):
            for c in range(2):
                parts = [
                    pieces_ref[at, pl.ds(pl.multiple_of(jnp.bitwise_xor(mine, h) * 8, 8), 8), :]
                    for h in range(4)
                ]
                for e in range(2):
                    for p in range(2):
                        pair = [parts[2 * p + i][:, e * half : (e + 1) * half] for i in range(2)]
                        to = (8 * c + 4 * e + 2 * p) * half
                        out_ref[r : r + 8, to : to + 2 * half] = jnp.concatenate(pair, axis=1)
                at += 1


def out_kernel(parts_ref, bias_ref, live_ref, out_ref):
    total = parts_ref[0].astype(F32)
    for k in range(1, parts_ref.shape[0]):
        total = total + parts_ref[k].astype(F32)
    out_ref[...] = ((total + bias_ref[...]) * live_ref[...]).astype(BF)


def body(
    edge_feats,
    edge_dst,
    self_feats,
    neigh_one,
    self_one,
    bias_one,
    tile_index,
    tile_values,
    seed_live,
    neigh_two,
    self_two,
    bias_two,
    cotangent,
):
    groups = lax.axis_size("dp")
    n_feat = lax.axis_size("feat")
    edges, cols = edge_feats.shape
    targets = self_feats.shape[0]
    hid = bias_one.shape[0]
    full = neigh_one.shape[1]
    cap = 2 * edges // groups
    blocks = n_feat // GROUP
    wide = full // GROUP
    near = [[GROUP * i + j for j in range(GROUP)] for i in range(blocks)]
    far = [[i + GROUP * j for j in range(blocks)] for i in range(GROUP)]
    z = lax.axis_index("feat")
    mine = (z % GROUP).reshape(1)
    live = seed_live.reshape(1, targets).astype(F32)

    def swap(x, axis, among=None):
        return lax.all_to_all(
            x, axis, split_axis=0, concat_axis=0, tiled=True, axis_index_groups=among
        )

    def trade(x, k):
        return lax.ppermute(x, "feat", [(i, i ^ k) for i in range(n_feat)])

    def shape(*dims, dtype=BF):
        return jax.ShapeDtypeStruct(dims, dtype)

    with jax.named_scope("edges"):
        send = call(
            functools.partial(pack_kernel, groups, targets),
            shape(groups, ROWS, cap),
            2,
            scratch=[pltpu.VMEM((8 * ROWS, edges), BF)],
            flops=2 * groups * ROWS * edges * cap,
            nbytes=8 << 20,
        )(edge_feats.T, edge_dst.reshape(-1, 128))
        recv = swap(send, "dp")
    with jax.named_scope("pieces"):
        pieces = call(
            first_pieces_kernel,
            shape(GROUP, 4 * cols, wide),
            5,
            smem=(0,),
            late=(4,),
            nbytes=2 << 20,
        )(mine, neigh_one, self_one, self_feats.T, send)
        got = [trade(pieces[k], k) for k in range(1, GROUP)]
    with jax.named_scope("mean"):
        mean = call(
            functools.partial(mean_kernel, cols),
            shape(GROUP, cols, targets),
            4,
            late=(1, 2, 3),
            flops=2 * groups * ROWS * cap * targets,
            nbytes=8 << 20,
        )(recv, *got)
        mean = swap(mean, "feat", near)
    with jax.named_scope("first"):
        first = call(
            first_kernel,
            shape(blocks, 2 * hid, targets),
            7,
            scratch=[pltpu.VMEM((8 * cols, wide), BF), pltpu.VMEM((8 * cols, targets), BF)],
            smem=(0,),
            flops=2 * 8 * cols * wide * targets,
            nbytes=2 << 20,
        )(mine, mean, pieces[0], *got, cotangent.T)
        parts = swap(first, "feat", far)
    with jax.named_scope("pieces"):
        pieces = call(
            second_pieces_kernel,
            shape(GROUP, 2 * hid, wide),
            4,
            smem=(0,),
            late=(3,),
            nbytes=1 << 20,
        )(mine, neigh_two, self_two, first)
        got = [trade(pieces[k], k) for k in range(1, GROUP)]
    with jax.named_scope("hidden"):
        hidden = call(
            hidden_kernel, shape(GROUP, hid, targets), 5, late=(2, 3, 4), nbytes=1 << 20
        )(parts, bias_one.reshape(hid, 1), *got)
        hidden = swap(hidden, "feat", near)
    with jax.named_scope("grads"):
        agg, terms = call(
            grad_kernel,
            (shape(wide, targets), shape(groups, GROUP * 8, 128)),
            5,
            scratch=[
                pltpu.VMEM((2 * wide, targets), BF),
                pltpu.VMEM((targets // 128, wide, 128), F32),
            ],
            smem=(0,),
            flops=2 * 2 * wide * targets * wide,
            nbytes=4 << 20,
        )(tile_index, hidden, tile_values, live, parts)
        terms = swap(terms, "dp")
        mine_sum = call(
            sum_kernel, shape(GROUP, 8, 128, dtype=F32), 2, smem=(0,), nbytes=1 << 20
        )(mine, terms)
        sums = [mine_sum[0]] + [trade(mine_sum[k], k) for k in range(1, GROUP)]
    with jax.named_scope("second"):
        second = call(
            second_kernel,
            shape(blocks, hid, targets),
            7,
            scratch=[pltpu.VMEM((GROUP, 2 * hid, wide), BF), pltpu.VMEM((2 * wide, targets), BF)],
            smem=(0,),
            flops=2 * 2 * wide * wide * targets,
            nbytes=2 << 20,
        )(mine, agg, hidden, pieces[0], *got)
        second = swap(second, "feat", far)
        second_out = call(out_kernel, shape(hid, targets), 3, nbytes=1 << 20)(
            second, bias_two.reshape(hid, 1), live
        ).T
    with jax.named_scope("place"):
        spread = call(
            copies_kernel, shape(groups, GROUP * 8, 128, dtype=F32), 5, late=(4,), nbytes=1 << 20
        )(*sums, second)
        spread = swap(spread, "dp")
        grad_neigh, grad_self = call(
            place_kernel,
            (shape(hid, full, dtype=F32), shape(hid, full, dtype=F32)),
            2,
            smem=(0,),
            nbytes=1 << 20,
        )(mine, spread)
    return (second_out, grad_neigh, grad_self)


def solution(mesh):
    in_specs = (
        P("dp", "feat"),
        P("dp"),
        P("dp", "feat"),
        P("feat", None),
        P("feat", None),
        P("feat"),
        P("dp", None),
        P("dp", None, None),
        P("dp"),
        P("feat", None),
        P("feat", None),
        P("feat"),
        P("dp", "feat"),
    )
    out_specs = (P("dp", "feat"), P("feat", None), P("feat", None))
    return jax.shard_map(body, mesh=mesh, in_specs=in_specs, out_specs=out_specs, check_vma=False)
```

```python
import functools

import jax
import jax.numpy as jnp
from jax import lax
from jax.experimental import pallas as pl
from jax.experimental.pallas import tpu as pltpu
from jax.sharding import PartitionSpec as P

BF = jnp.bfloat16
F32 = jnp.float32
NT = (((1,), (1,)), ((), ()))
TN = (((0,), (0,)), ((), ()))
ROWS = 64
GROUP = 4
VMEM_LIMIT = 48 * 1024 * 1024


def call(kernel, out_shape, n_in, scratch=(), smem=(), late=(), flops=0, nbytes=0):
    spaces = {i: pltpu.SMEM for i in smem} | {i: pl.ANY for i in late}
    in_specs = [pl.BlockSpec(memory_space=spaces.get(i, pltpu.VMEM)) for i in range(n_in)]
    out_specs = jax.tree.map(lambda _: pl.BlockSpec(memory_space=pltpu.VMEM), out_shape)
    return pl.pallas_call(
        kernel,
        out_shape=out_shape,
        in_specs=in_specs,
        out_specs=out_specs,
        scratch_shapes=list(scratch),
        compiler_params=pltpu.CompilerParams(vmem_limit_bytes=VMEM_LIMIT),
        cost_estimate=pl.CostEstimate(flops=flops, bytes_accessed=nbytes, transcendentals=0),
    )


def pack_kernel(groups, tgt_rows, feats_ref, dst_ref, send_ref, masked):
    cols, edges = feats_ref.shape
    cap = send_ref.shape[2]
    dst = jnp.concatenate([dst_ref[i : i + 1, :] for i in range(dst_ref.shape[0])], axis=1)
    owner = dst // tgt_rows
    local = dst - owner * tgt_rows
    half = tgt_rows // 2
    code = jnp.where(local < half, local - half, local - (half - 1)).astype(F32)
    owner_hot = lax.broadcasted_iota(jnp.int32, (groups, edges), 0) == owner
    owner_hot = owner_hot.astype(F32)
    step = 256
    before = (
        lax.broadcasted_iota(jnp.int32, (step, step), 0)
        < lax.broadcasted_iota(jnp.int32, (step, step), 1)
    ).astype(BF)
    seen = jnp.zeros((groups, 1), F32)
    ranks = []
    for i in range(edges // step):
        part = owner_hot[:, i * step : (i + 1) * step]
        prior = jnp.dot(part.astype(BF), before, preferred_element_type=F32) + seen
        ranks.append(jnp.sum(prior * part, axis=0, keepdims=True))
        seen = seen + jnp.sum(part, axis=1, keepdims=True)
    rank = jnp.concatenate(ranks, axis=1).astype(jnp.int32)
    rank_hot = (lax.broadcasted_iota(jnp.int32, (cap, edges), 0) == rank).astype(F32).astype(BF)
    extra_row = lax.broadcasted_iota(jnp.int32, (ROWS - cols, edges), 0)
    extra = jnp.where(extra_row == 0, code, jnp.where(extra_row == 1, 1.0, 0.0)).astype(BF)
    hot = owner_hot.astype(BF)
    some = masked.shape[0] // ROWS
    for g in range(groups // some):
        for j in range(some):
            o = g * some + j
            live = hot[o : o + 1, :]
            masked[j * ROWS : j * ROWS + cols, :] = feats_ref[...] * live
            masked[j * ROWS + cols : (j + 1) * ROWS, :] = extra * live
        out = lax.dot_general(masked[...], rank_hot, NT, preferred_element_type=F32).astype(BF)
        for j in range(some):
            send_ref[g * some + j] = out[j * ROWS : (j + 1) * ROWS, :]


def column_sets(weight, group):
    half = 64
    n = weight.shape[1] // half
    sets = []
    for j in range(group):
        blocks = [weight[:, b * half : (b + 1) * half] for b in range(j, n, group)]
        sets.append(jnp.concatenate(blocks, axis=1))
    return sets


def first_pieces_kernel(mine_ref, neigh_ref, own_ref, self_ref, late_ref, out_ref):
    del late_ref
    mine = mine_ref[0]
    rows = neigh_ref.shape[0]
    group, _, width = out_ref.shape
    both = zip(column_sets(neigh_ref[...], group), column_sets(own_ref[...], group))
    for j, (neigh, own) in enumerate(both):
        to = jnp.bitwise_xor(mine, j)
        out_ref[to, :rows, :] = neigh
        out_ref[to, rows : 2 * rows, :] = own
        out_ref[to, 2 * rows : 3 * rows, :] = self_ref[:, :width]
        out_ref[to, 3 * rows :, :] = self_ref[:, width:]


def second_pieces_kernel(mine_ref, neigh_ref, own_ref, late_ref, out_ref):
    del late_ref
    mine = mine_ref[0]
    rows = neigh_ref.shape[0]
    both = zip(column_sets(neigh_ref[...], out_ref.shape[0]), column_sets(own_ref[...], out_ref.shape[0]))
    for j, (neigh, own) in enumerate(both):
        to = jnp.bitwise_xor(mine, j)
        out_ref[to, :rows, :] = neigh
        out_ref[to, rows:, :] = own


def mean_kernel(cols, recv_ref, late1_ref, late2_ref, late3_ref, out_ref):
    del late1_ref, late2_ref, late3_ref
    groups, rows, cap = recv_ref.shape
    targets = out_ref.shape[2]
    half = targets // 2
    vertex = lax.broadcasted_iota(jnp.int32, (targets, 1), 0)
    vertex = jnp.where(vertex < half, vertex - half, vertex - (half - 1)).astype(F32)
    acc = jnp.zeros((rows, targets), F32)
    some = 8
    for g in range(groups // some):
        part = jnp.concatenate([recv_ref[g * some + j] for j in range(some)], axis=1)
        code = part[cols : cols + 1, :].astype(F32)
        hot = (vertex == code).astype(F32).astype(BF)
        acc = acc + lax.dot_general(part, hot, NT, preferred_element_type=F32)
    degree = jnp.maximum(acc[cols + 1 : cols + 2, :], 1.0)
    mean = (acc[:cols, :] / degree).astype(BF)
    for j in range(out_ref.shape[0]):
        out_ref[j] = mean


def first_kernel(
    mine_ref, mean_ref, p0_ref, p1_ref, p2_ref, p3_ref, out_ref, weight, acts
):
    mine = mine_ref[0]
    group, rows, targets = mean_ref.shape
    width = targets // 2
    for k, piece in enumerate((p0_ref, p1_ref, p2_ref, p3_ref)):
        at = slice(2 * rows * k, 2 * rows * (k + 1))
        mid = 2 * rows * k + rows
        weight[at, :] = piece[: 2 * rows, :]
        acts[2 * rows * k : mid, :] = mean_ref[jnp.bitwise_xor(mine, k)]
        acts[mid : mid + rows, :width] = piece[2 * rows : 3 * rows, :]
        acts[mid : mid + rows, width:] = piece[3 * rows :, :]
    total = lax.dot_general(weight[...], acts[...], TN, preferred_element_type=F32)
    cols = out_ref.shape[1]
    for z in range(out_ref.shape[0]):
        out_ref[z] = total[z * cols : (z + 1) * cols, :].astype(BF)


def hidden_kernel(parts_ref, bias_ref, late1_ref, late2_ref, late3_ref, out_ref):
    del late1_ref, late2_ref, late3_ref
    total = parts_ref[0].astype(F32)
    for k in range(1, parts_ref.shape[0]):
        total = total + parts_ref[k].astype(F32)
    hidden = jnp.maximum(total + bias_ref[...], 0.0).astype(BF)
    for c in range(out_ref.shape[0]):
        out_ref[c] = hidden


def grad_kernel(index_ref, hid_ref, values_ref, live_ref, cot_ref, agg_ref, out_ref, left, acc):
    group, cols, targets = hid_ref.shape
    width = values_ref.shape[1]
    wide = group * cols
    acc[...] = jnp.zeros_like(acc)
    for k in range(values_ref.shape[0]):
        source = index_ref[k, 1]
        at = pl.ds(pl.multiple_of(source * width, width), width)
        rows = jnp.concatenate([hid_ref[j, :, at] for j in range(group)], axis=0)
        target = index_ref[k, 0]
        acc[target] += lax.dot_general(rows, values_ref[k], NT, preferred_element_type=F32)
    live = live_ref[...].astype(BF)
    for t in range(targets // width):
        at = slice(t * width, (t + 1) * width)
        tile = acc[t].astype(BF)
        agg_ref[:, at] = tile
        left[:wide, at] = tile * live[:, at]
    for j in range(group):
        left[wide + j * cols : wide + (j + 1) * cols, :] = hid_ref[j] * live
    block = lax.dot_general(left[...], cot_ref[...], NT, preferred_element_type=F32)
    at = 0
    for w in range(2):
        for r in range(0, cols, 8):
            for c in range(0, cot_ref.shape[0], 128):
                rows_of = [
                    block[w * wide + j * cols + r : w * wide + j * cols + r + 8, c : c + 128]
                    for j in range(group)
                ]
                out_ref[at] = jnp.concatenate(rows_of, axis=0).astype(BF)
                at += 1


def second_kernel(mine_ref, agg_ref, hid_ref, p0_ref, p1_ref, p2_ref, p3_ref, out_ref, weight, acts):
    mine = mine_ref[0]
    group, rows, targets = hid_ref.shape
    for k, piece in enumerate((p0_ref, p1_ref, p2_ref, p3_ref)):
        weight[jnp.bitwise_xor(mine, k)] = piece[...]
    for j in range(group):
        acts[2 * rows * j : 2 * rows * j + rows, :] = agg_ref[j * rows : (j + 1) * rows, :]
        acts[2 * rows * j + rows : 2 * rows * (j + 1), :] = hid_ref[j]
    both = jnp.concatenate([weight[j] for j in range(group)], axis=0)
    total = lax.dot_general(both, acts[...], TN, preferred_element_type=F32)
    n, cols, _ = out_ref.shape
    for z in range(n):
        out_ref[z] = total[z * cols : (z + 1) * cols, :].astype(BF)


def sum_kernel(mine_ref, terms_ref, out_ref):
    mine = mine_ref[0]
    total = terms_ref[0].astype(F32)
    for d in range(1, terms_ref.shape[0]):
        total = total + terms_ref[d].astype(F32)
    rows = out_ref.shape[1]
    for j in range(out_ref.shape[0]):
        out_ref[jnp.bitwise_xor(mine, j)] = total[j * rows : (j + 1) * rows, :]


def copies_kernel(p0_ref, p1_ref, p2_ref, p3_ref, late_ref, out_ref):
    del late_ref
    whole = jnp.concatenate([p0_ref[...], p1_ref[...], p2_ref[...], p3_ref[...]], axis=0)
    for d in range(out_ref.shape[0]):
        out_ref[d] = whole


def place_kernel(mine_ref, pieces_ref, neigh_ref, self_ref):
    mine = mine_ref[0]
    half = 64
    at = 0
    for out_ref in (neigh_ref, self_ref):
        for r in range(0, out_ref.shape[0], 8):
            for c in range(2):
                parts = [
                    pieces_ref[at, pl.ds(pl.multiple_of(jnp.bitwise_xor(mine, h) * 8, 8), 8), :]
                    for h in range(4)
                ]
                for e in range(2):
                    for p in range(2):
                        pair = [parts[2 * p + i][:, e * half : (e + 1) * half] for i in range(2)]
                        to = (8 * c + 4 * e + 2 * p) * half
                        out_ref[r : r + 8, to : to + 2 * half] = jnp.concatenate(pair, axis=1)
                at += 1


def out_kernel(parts_ref, bias_ref, live_ref, out_ref):
    total = parts_ref[0].astype(F32)
    for k in range(1, parts_ref.shape[0]):
        total = total + parts_ref[k].astype(F32)
    out_ref[...] = ((total + bias_ref[...]) * live_ref[...]).astype(BF)


def body(
    edge_feats,
    edge_dst,
    self_feats,
    neigh_one,
    self_one,
    bias_one,
    tile_index,
    tile_values,
    seed_live,
    neigh_two,
    self_two,
    bias_two,
    cotangent,
):
    groups = lax.axis_size("dp")
    n_feat = lax.axis_size("feat")
    edges, cols = edge_feats.shape
    targets = self_feats.shape[0]
    hid = bias_one.shape[0]
    full = neigh_one.shape[1]
    cap = 2 * edges // groups
    blocks = n_feat // GROUP
    wide = full // GROUP
    near = [[GROUP * i + j for j in range(GROUP)] for i in range(blocks)]
    far = [[i + GROUP * j for j in range(blocks)] for i in range(GROUP)]
    z = lax.axis_index("feat")
    mine = (z % GROUP).reshape(1)
    live = seed_live.reshape(1, targets).astype(F32)

    def swap(x, axis, among=None):
        return lax.all_to_all(
            x, axis, split_axis=0, concat_axis=0, tiled=True, axis_index_groups=among
        )

    def trade(x, k):
        return lax.ppermute(x, "feat", [(i, i ^ k) for i in range(n_feat)])

    def shape(*dims, dtype=BF):
        return jax.ShapeDtypeStruct(dims, dtype)

    with jax.named_scope("cotangent"):
        cot = lax.all_gather(cotangent.T, "feat", axis=0, tiled=True, axis_index_groups=far)
    with jax.named_scope("edges"):
        send = call(
            functools.partial(pack_kernel, groups, targets),
            shape(groups, ROWS, cap),
            2,
            scratch=[pltpu.VMEM((8 * ROWS, edges), BF)],
            flops=2 * groups * ROWS * edges * cap,
            nbytes=8 << 20,
        )(edge_feats.T, edge_dst.reshape(-1, 128))
        recv = swap(send, "dp")
    with jax.named_scope("pieces"):
        pieces = call(
            first_pieces_kernel,
            shape(GROUP, 4 * cols, wide),
            5,
            smem=(0,),
            late=(4,),
            nbytes=2 << 20,
        )(mine, neigh_one, self_one, self_feats.T, send)
        got = [trade(pieces[k], k) for k in range(1, GROUP)]
    with jax.named_scope("mean"):
        mean = call(
            functools.partial(mean_kernel, cols),
            shape(GROUP, cols, targets),
            4,
            late=(1, 2, 3),
            flops=2 * groups * ROWS * cap * targets,
            nbytes=8 << 20,
        )(recv, *got)
        mean = swap(mean, "feat", near)
    with jax.named_scope("first"):
        first = call(
            first_kernel,
            shape(blocks, hid, targets),
            6,
            scratch=[pltpu.VMEM((8 * cols, wide), BF), pltpu.VMEM((8 * cols, targets), BF)],
            smem=(0,),
            flops=2 * 8 * cols * wide * targets,
            nbytes=2 << 20,
        )(mine, mean, pieces[0], *got)
        parts = swap(first, "feat", far)
    with jax.named_scope("pieces"):
        pieces = call(
            second_pieces_kernel,
            shape(GROUP, 2 * hid, wide),
            4,
            smem=(0,),
            late=(3,),
            nbytes=1 << 20,
        )(mine, neigh_two, self_two, first)
        got = [trade(pieces[k], k) for k in range(1, GROUP)]
    with jax.named_scope("hidden"):
        hidden = call(
            hidden_kernel, shape(GROUP, hid, targets), 5, late=(2, 3, 4), nbytes=1 << 20
        )(parts, bias_one.reshape(hid, 1), *got)
        hidden = swap(hidden, "feat", near)
    with jax.named_scope("grads"):
        agg, terms = call(
            grad_kernel,
            (shape(wide, targets), shape(groups, GROUP * 8, 128)),
            5,
            scratch=[
                pltpu.VMEM((2 * wide, targets), BF),
                pltpu.VMEM((targets // 128, wide, 128), F32),
            ],
            smem=(0,),
            flops=2 * 2 * wide * targets * wide,
            nbytes=4 << 20,
        )(tile_index, hidden, tile_values, live, cot)
        terms = swap(terms, "dp")
        mine_sum = call(
            sum_kernel, shape(GROUP, 8, 128, dtype=F32), 2, smem=(0,), nbytes=1 << 20
        )(mine, terms)
        sums = [mine_sum[0]] + [trade(mine_sum[k], k) for k in range(1, GROUP)]
    with jax.named_scope("second"):
        second = call(
            second_kernel,
            shape(blocks, hid, targets),
            7,
            scratch=[pltpu.VMEM((GROUP, 2 * hid, wide), BF), pltpu.VMEM((2 * wide, targets), BF)],
            smem=(0,),
            flops=2 * 2 * wide * wide * targets,
            nbytes=2 << 20,
        )(mine, agg, hidden, pieces[0], *got)
        second = swap(second, "feat", far)
        second_out = call(out_kernel, shape(hid, targets), 3, nbytes=1 << 20)(
            second, bias_two.reshape(hid, 1), live
        ).T
    with jax.named_scope("place"):
        spread = call(
            copies_kernel, shape(groups, GROUP * 8, 128, dtype=F32), 5, late=(4,), nbytes=1 << 20
        )(*sums, second)
        spread = swap(spread, "dp")
        grad_neigh, grad_self = call(
            place_kernel,
            (shape(hid, full, dtype=F32), shape(hid, full, dtype=F32)),
            2,
            smem=(0,),
            nbytes=1 << 20,
        )(mine, spread)
    return (second_out, grad_neigh, grad_self)


def solution(mesh):
    in_specs = (
        P("dp", "feat"),
        P("dp"),
        P("dp", "feat"),
        P("feat", None),
        P("feat", None),
        P("feat"),
        P("dp", None),
        P("dp", None, None),
        P("dp"),
        P("feat", None),
        P("feat", None),
        P("feat"),
        P("dp", "feat"),
    )
    out_specs = (P("dp", "feat"), P("feat", None), P("feat", None))
    return jax.shard_map(body, mesh=mesh, in_specs=in_specs, out_specs=out_specs, check_vma=False)
```

```python
import functools

import jax
import jax.numpy as jnp
from jax import lax
from jax.experimental import pallas as pl
from jax.experimental.pallas import tpu as pltpu
from jax.sharding import PartitionSpec as P

BF = jnp.bfloat16
F32 = jnp.float32
NT = (((1,), (1,)), ((), ()))
TN = (((0,), (0,)), ((), ()))
ROWS = 64
GROUP = 4
VMEM_LIMIT = 48 * 1024 * 1024


def call(kernel, out_shape, n_in, scratch=(), smem=(), late=(), flops=0, nbytes=0):
    spaces = {i: pltpu.SMEM for i in smem} | {i: pl.ANY for i in late}
    in_specs = [pl.BlockSpec(memory_space=spaces.get(i, pltpu.VMEM)) for i in range(n_in)]
    out_specs = jax.tree.map(lambda _: pl.BlockSpec(memory_space=pltpu.VMEM), out_shape)
    return pl.pallas_call(
        kernel,
        out_shape=out_shape,
        in_specs=in_specs,
        out_specs=out_specs,
        scratch_shapes=list(scratch),
        compiler_params=pltpu.CompilerParams(vmem_limit_bytes=VMEM_LIMIT),
        cost_estimate=pl.CostEstimate(flops=flops, bytes_accessed=nbytes, transcendentals=0),
    )


def pack_kernel(groups, tgt_rows, feats_ref, dst_ref, send_ref, masked):
    cols, edges = feats_ref.shape
    cap = send_ref.shape[2]
    dst = jnp.concatenate([dst_ref[i : i + 1, :] for i in range(dst_ref.shape[0])], axis=1)
    owner = dst // tgt_rows
    local = dst - owner * tgt_rows
    half = tgt_rows // 2
    code = jnp.where(local < half, local - half, local - (half - 1)).astype(F32)
    owner_hot = lax.broadcasted_iota(jnp.int32, (groups, edges), 0) == owner
    owner_hot = owner_hot.astype(F32)
    step = 256
    before = (
        lax.broadcasted_iota(jnp.int32, (step, step), 0)
        < lax.broadcasted_iota(jnp.int32, (step, step), 1)
    ).astype(BF)
    seen = jnp.zeros((groups, 1), F32)
    ranks = []
    for i in range(edges // step):
        part = owner_hot[:, i * step : (i + 1) * step]
        prior = jnp.dot(part.astype(BF), before, preferred_element_type=F32) + seen
        ranks.append(jnp.sum(prior * part, axis=0, keepdims=True))
        seen = seen + jnp.sum(part, axis=1, keepdims=True)
    rank = jnp.concatenate(ranks, axis=1).astype(jnp.int32)
    rank_hot = (lax.broadcasted_iota(jnp.int32, (cap, edges), 0) == rank).astype(F32).astype(BF)
    extra_row = lax.broadcasted_iota(jnp.int32, (ROWS - cols, edges), 0)
    extra = jnp.where(extra_row == 0, code, jnp.where(extra_row == 1, 1.0, 0.0)).astype(BF)
    hot = owner_hot.astype(BF)
    some = masked.shape[0] // ROWS
    for g in range(groups // some):
        for j in range(some):
            o = g * some + j
            live = hot[o : o + 1, :]
            masked[j * ROWS : j * ROWS + cols, :] = feats_ref[...] * live
            masked[j * ROWS + cols : (j + 1) * ROWS, :] = extra * live
        out = lax.dot_general(masked[...], rank_hot, NT, preferred_element_type=F32).astype(BF)
        for j in range(some):
            send_ref[g * some + j] = out[j * ROWS : (j + 1) * ROWS, :]


def column_sets(weight, group):
    half = 64
    n = weight.shape[1] // half
    sets = []
    for j in range(group):
        blocks = [weight[:, b * half : (b + 1) * half] for b in range(j, n, group)]
        sets.append(jnp.concatenate(blocks, axis=1))
    return sets


def first_pieces_kernel(mine_ref, neigh_ref, own_ref, self_ref, late_ref, out_ref):
    del late_ref
    mine = mine_ref[0]
    rows = neigh_ref.shape[0]
    group, _, width = out_ref.shape
    both = zip(column_sets(neigh_ref[...], group), column_sets(own_ref[...], group))
    for j, (neigh, own) in enumerate(both):
        to = jnp.bitwise_xor(mine, j)
        out_ref[to, :rows, :] = neigh
        out_ref[to, rows : 2 * rows, :] = own
        out_ref[to, 2 * rows : 3 * rows, :] = self_ref[:, :width]
        out_ref[to, 3 * rows :, :] = self_ref[:, width:]


def second_pieces_kernel(mine_ref, neigh_ref, own_ref, late_ref, out_ref):
    del late_ref
    mine = mine_ref[0]
    rows = neigh_ref.shape[0]
    both = zip(column_sets(neigh_ref[...], out_ref.shape[0]), column_sets(own_ref[...], out_ref.shape[0]))
    for j, (neigh, own) in enumerate(both):
        to = jnp.bitwise_xor(mine, j)
        out_ref[to, :rows, :] = neigh
        out_ref[to, rows:, :] = own


def mean_kernel(cols, recv_ref, late1_ref, late2_ref, late3_ref, out_ref):
    del late1_ref, late2_ref, late3_ref
    groups, rows, cap = recv_ref.shape
    targets = out_ref.shape[2]
    half = targets // 2
    vertex = lax.broadcasted_iota(jnp.int32, (targets, 1), 0)
    vertex = jnp.where(vertex < half, vertex - half, vertex - (half - 1)).astype(F32)
    acc = jnp.zeros((rows, targets), F32)
    some = 8
    for g in range(groups // some):
        part = jnp.concatenate([recv_ref[g * some + j] for j in range(some)], axis=1)
        code = part[cols : cols + 1, :].astype(F32)
        hot = (vertex == code).astype(F32).astype(BF)
        acc = acc + lax.dot_general(part, hot, NT, preferred_element_type=F32)
    degree = jnp.maximum(acc[cols + 1 : cols + 2, :], 1.0)
    mean = (acc[:cols, :] / degree).astype(BF)
    for j in range(out_ref.shape[0]):
        out_ref[j] = mean


def first_kernel(
    mine_ref, mean_ref, p0_ref, p1_ref, p2_ref, p3_ref, out_ref, weight, acts
):
    mine = mine_ref[0]
    group, rows, targets = mean_ref.shape
    width = targets // 2
    for k, piece in enumerate((p0_ref, p1_ref, p2_ref, p3_ref)):
        at = slice(2 * rows * k, 2 * rows * (k + 1))
        mid = 2 * rows * k + rows
        weight[at, :] = piece[: 2 * rows, :]
        acts[2 * rows * k : mid, :] = mean_ref[jnp.bitwise_xor(mine, k)]
        acts[mid : mid + rows, :width] = piece[2 * rows : 3 * rows, :]
        acts[mid : mid + rows, width:] = piece[3 * rows :, :]
    total = lax.dot_general(weight[...], acts[...], TN, preferred_element_type=F32)
    cols = out_ref.shape[1]
    for z in range(out_ref.shape[0]):
        out_ref[z] = total[z * cols : (z + 1) * cols, :].astype(BF)


def hidden_kernel(
    parts_ref, bias_ref, index_ref, values_ref, live_ref, pieces_ref, pay_ref, left_ref, source, acc
):
    cols, targets = bias_ref.shape[0], live_ref.shape[1]
    width = values_ref.shape[1]
    wide = pay_ref.shape[2]
    total = parts_ref[0].astype(F32)
    for k in range(1, parts_ref.shape[0]):
        total = total + parts_ref[k].astype(F32)
    hidden = jnp.maximum(total + bias_ref[...], 0.0).astype(BF)
    for k in range(pay_ref.shape[0]):
        pay_ref[k, :cols, :] = hidden[:, :wide]
        pay_ref[k, cols : 2 * cols, :] = hidden[:, wide:]
        pay_ref[k, 2 * cols :, :] = pieces_ref[k]
    live = live_ref[...].astype(BF)
    for t in range(targets // width):
        source[t] = hidden[:, t * width : (t + 1) * width]
    acc[...] = jnp.zeros_like(acc)
    for k in range(values_ref.shape[0]):
        target = index_ref[k, 0]
        acc[target] += lax.dot_general(
            source[index_ref[k, 1]], values_ref[k], NT, preferred_element_type=F32
        )
    for t in range(targets // width):
        at = slice(t * width, (t + 1) * width)
        left_ref[:cols, at] = acc[t].astype(BF) * live[:, at]
    left_ref[cols:, :] = hidden * live


def grad_kernel(left_ref, cot_ref, out_ref):
    pieces, piece_rows, piece_cols = out_ref.shape
    quarters = left_ref.shape[0] // piece_rows
    for c in range(pieces // quarters):
        cot = cot_ref[c * piece_cols : (c + 1) * piece_cols, :]
        block = lax.dot_general(left_ref[...], cot, NT, preferred_element_type=F32).astype(BF)
        for q in range(quarters):
            out_ref[c * quarters + q] = block[q * piece_rows : (q + 1) * piece_rows, :]


def second_kernel(
    across_ref, index_ref, values_ref, p0_ref, p1_ref, p2_ref, p3_ref, out_ref, weight, acts, source, acc
):
    across = across_ref[0]
    n, cols, targets = out_ref.shape
    wide = p0_ref.shape[1]
    width = values_ref.shape[1]
    group = 4
    for k, ref in enumerate((p0_ref, p1_ref, p2_ref, p3_ref)):
        mine = slice(k * cols, (k + 1) * cols)
        acts[mine, :wide] = ref[:cols, :]
        acts[mine, wide:] = ref[cols : 2 * cols, :]
        weight[mine, :] = ref[3 * cols :, :]
        weight[(group + k) * cols : (group + k + 1) * cols, :] = ref[2 * cols : 3 * cols, :]
        for t in range(targets // width):
            half, at = divmod(t * width, wide)
            source[t, mine, :] = ref[half * cols : (half + 1) * cols, at : at + width]
    acc[...] = jnp.zeros_like(acc)
    for k in range(values_ref.shape[0]):
        target = index_ref[k, 0]
        acc[target] += lax.dot_general(
            source[index_ref[k, 1]], values_ref[k], NT, preferred_element_type=F32
        )
    for t in range(targets // width):
        acts[group * cols :, t * width : (t + 1) * width] = acc[t].astype(BF)
    total = lax.dot_general(weight[...], acts[...], TN, preferred_element_type=F32)
    for z in range(n):
        out_ref[jnp.bitwise_xor(across, z)] = total[z * cols : (z + 1) * cols, :].astype(BF)


def copies_kernel(terms_ref, out_ref):
    total = terms_ref[0].astype(F32)
    for d in range(1, terms_ref.shape[0]):
        total = total + terms_ref[d].astype(F32)
    for d in range(out_ref.shape[0]):
        out_ref[d] = total


def place_kernel(pieces_ref, neigh_ref, self_ref):
    pieces, rows, cols = pieces_ref.shape
    halves = neigh_ref.shape[0] // rows
    quarters = 2 * halves
    for i, out_ref in enumerate((neigh_ref, self_ref)):
        for c in range(pieces // quarters):
            for h in range(halves):
                out_ref[h * rows : (h + 1) * rows, c * cols : (c + 1) * cols] = pieces_ref[
                    c * quarters + i * halves + h
                ]


def out_kernel(p0_ref, p1_ref, p2_ref, p3_ref, bias_ref, live_ref, out_ref):
    total = p0_ref[...].astype(F32) + p1_ref[...].astype(F32)
    total = total + (p2_ref[...].astype(F32) + p3_ref[...].astype(F32))
    out_ref[...] = ((total + bias_ref[...]) * live_ref[...]).astype(BF)


def body(
    edge_feats,
    edge_dst,
    self_feats,
    neigh_one,
    self_one,
    bias_one,
    tile_index,
    tile_values,
    seed_live,
    neigh_two,
    self_two,
    bias_two,
    cotangent,
):
    groups = lax.axis_size("dp")
    n_feat = lax.axis_size("feat")
    edges, cols = edge_feats.shape
    targets = self_feats.shape[0]
    hid = bias_one.shape[0]
    full = neigh_one.shape[1]
    cap = 2 * edges // groups
    blocks = n_feat // GROUP
    wide = full // GROUP
    near = [[GROUP * i + j for j in range(GROUP)] for i in range(blocks)]
    far = [[i + GROUP * j for j in range(blocks)] for i in range(GROUP)]
    z = lax.axis_index("feat")
    mine = (z % GROUP).reshape(1)
    across = (z // GROUP).reshape(1)
    live = seed_live.reshape(1, targets).astype(F32)

    def swap(x, axis, among=None):
        return lax.all_to_all(
            x, axis, split_axis=0, concat_axis=0, tiled=True, axis_index_groups=among
        )

    def trade(x, k):
        return lax.ppermute(x, "feat", [(i, i ^ k) for i in range(n_feat)])

    def shape(*dims, dtype=BF):
        return jax.ShapeDtypeStruct(dims, dtype)

    with jax.named_scope("cotangent"):
        cot = lax.all_gather(cotangent.T, "feat", axis=0, tiled=True)
    with jax.named_scope("edges"):
        send = call(
            functools.partial(pack_kernel, groups, targets),
            shape(groups, ROWS, cap),
            2,
            scratch=[pltpu.VMEM((8 * ROWS, edges), BF)],
            flops=2 * groups * ROWS * edges * cap,
            nbytes=8 << 20,
        )(edge_feats.T, edge_dst.reshape(-1, 128))
        recv = swap(send, "dp")
    with jax.named_scope("pieces"):
        pieces = call(
            first_pieces_kernel,
            shape(GROUP, 4 * cols, wide),
            5,
            smem=(0,),
            late=(4,),
            nbytes=2 << 20,
        )(mine, neigh_one, self_one, self_feats.T, send)
        got = [trade(pieces[k], k) for k in range(1, GROUP)]
    with jax.named_scope("mean"):
        mean = call(
            functools.partial(mean_kernel, cols),
            shape(GROUP, cols, targets),
            4,
            late=(1, 2, 3),
            flops=2 * groups * ROWS * cap * targets,
            nbytes=8 << 20,
        )(recv, *got)
        mean = swap(mean, "feat", near)
    with jax.named_scope("first"):
        first = call(
            first_kernel,
            shape(blocks, hid, targets),
            6,
            scratch=[pltpu.VMEM((8 * cols, wide), BF), pltpu.VMEM((8 * cols, targets), BF)],
            smem=(0,),
            flops=2 * 8 * cols * wide * targets,
            nbytes=2 << 20,
        )(mine, mean, pieces[0], *got)
        parts = swap(first, "feat", far)
    with jax.named_scope("pieces"):
        pieces = call(
            second_pieces_kernel,
            shape(GROUP, 2 * hid, wide),
            4,
            smem=(0,),
            late=(3,),
            nbytes=1 << 20,
        )(mine, neigh_two, self_two, first)
    with jax.named_scope("hidden"):
        pay, left = call(
            hidden_kernel,
            (shape(GROUP, 4 * hid, wide), shape(2 * hid, targets)),
            6,
            scratch=[
                pltpu.VMEM((targets // 128, hid, 128), BF),
                pltpu.VMEM((targets // 128, hid, 128), F32),
            ],
            smem=(2,),
            nbytes=1 << 20,
        )(parts, bias_one.reshape(hid, 1), tile_index, tile_values, live, pieces)
        got = [trade(pay[k], k) for k in range(1, GROUP)]
    with jax.named_scope("grads"):
        piece_rows = 2 * hid * full // 128 // groups
        terms = call(
            grad_kernel,
            shape(groups, piece_rows, 128),
            2,
            flops=2 * 2 * hid * targets * full,
            nbytes=2 << 20,
        )(left, cot)
        terms = swap(terms, "dp")
        spread = call(
            copies_kernel, shape(groups, piece_rows, 128, dtype=F32), 1, nbytes=1 << 20
        )(terms)
        spread = swap(spread, "dp")
        grad_neigh, grad_self = call(
            place_kernel,
            (shape(hid, full, dtype=F32), shape(hid, full, dtype=F32)),
            1,
            nbytes=1 << 20,
        )(spread)
    with jax.named_scope("second"):
        second = call(
            second_kernel,
            shape(blocks, hid, targets),
            7,
            scratch=[
                pltpu.VMEM((2 * wide, wide), BF),
                pltpu.VMEM((2 * wide, targets), BF),
                pltpu.VMEM((targets // 128, wide, 128), BF),
                pltpu.VMEM((targets // 128, wide, 128), F32),
            ],
            smem=(0, 1),
            flops=2 * 2 * wide * wide * targets,
            nbytes=2 << 20,
        )(across, tile_index, tile_values, pay[0], *got)
        sums = [second[0]] + [trade(second[k], GROUP * k) for k in range(1, blocks)]
        second_out = call(out_kernel, shape(hid, targets), 6, nbytes=1 << 20)(
            *sums, bias_two.reshape(hid, 1), live
        ).T
    return (second_out, grad_neigh, grad_self)


def solution(mesh):
    in_specs = (
        P("dp", "feat"),
        P("dp"),
        P("dp", "feat"),
        P("feat", None),
        P("feat", None),
        P("feat"),
        P("dp", None),
        P("dp", None, None),
        P("dp"),
        P("feat", None),
        P("feat", None),
        P("feat"),
        P("dp", "feat"),
    )
    out_specs = (P("dp", "feat"), P("feat", None), P("feat", None))
    return jax.shard_map(body, mesh=mesh, in_specs=in_specs, out_specs=out_specs, check_vma=False)
```

```python
import functools

import jax
import jax.numpy as jnp
from jax import lax
from jax.experimental import pallas as pl
from jax.experimental.pallas import tpu as pltpu
from jax.sharding import PartitionSpec as P

BF = jnp.bfloat16
F32 = jnp.float32
NT = (((1,), (1,)), ((), ()))
TN = (((0,), (0,)), ((), ()))
ROWS = 64
GROUP = 4
VMEM_LIMIT = 48 * 1024 * 1024


def call(kernel, out_shape, n_in, scratch=(), smem=(), late=(), flops=0, nbytes=0):
    spaces = {i: pltpu.SMEM for i in smem} | {i: pl.ANY for i in late}
    in_specs = [pl.BlockSpec(memory_space=spaces.get(i, pltpu.VMEM)) for i in range(n_in)]
    out_specs = jax.tree.map(lambda _: pl.BlockSpec(memory_space=pltpu.VMEM), out_shape)
    return pl.pallas_call(
        kernel,
        out_shape=out_shape,
        in_specs=in_specs,
        out_specs=out_specs,
        scratch_shapes=list(scratch),
        compiler_params=pltpu.CompilerParams(vmem_limit_bytes=VMEM_LIMIT),
        cost_estimate=pl.CostEstimate(flops=flops, bytes_accessed=nbytes, transcendentals=0),
    )


def pack_kernel(groups, tgt_rows, feats_ref, dst_ref, send_ref, masked):
    cols, edges = feats_ref.shape
    cap = send_ref.shape[2]
    dst = jnp.concatenate([dst_ref[i : i + 1, :] for i in range(dst_ref.shape[0])], axis=1)
    owner = dst // tgt_rows
    local = dst - owner * tgt_rows
    half = tgt_rows // 2
    code = jnp.where(local < half, local - half, local - (half - 1)).astype(F32)
    owner_hot = lax.broadcasted_iota(jnp.int32, (groups, edges), 0) == owner
    owner_hot = owner_hot.astype(F32)
    step = 256
    before = (
        lax.broadcasted_iota(jnp.int32, (step, step), 0)
        < lax.broadcasted_iota(jnp.int32, (step, step), 1)
    ).astype(BF)
    seen = jnp.zeros((groups, 1), F32)
    ranks = []
    for i in range(edges // step):
        part = owner_hot[:, i * step : (i + 1) * step]
        prior = jnp.dot(part.astype(BF), before, preferred_element_type=F32) + seen
        ranks.append(jnp.sum(prior * part, axis=0, keepdims=True))
        seen = seen + jnp.sum(part, axis=1, keepdims=True)
    rank = jnp.concatenate(ranks, axis=1).astype(jnp.int32)
    rank_hot = (lax.broadcasted_iota(jnp.int32, (cap, edges), 0) == rank).astype(F32).astype(BF)
    extra_row = lax.broadcasted_iota(jnp.int32, (ROWS - cols, edges), 0)
    extra = jnp.where(extra_row == 0, code, jnp.where(extra_row == 1, 1.0, 0.0)).astype(BF)
    hot = owner_hot.astype(BF)
    some = masked.shape[0] // ROWS
    for g in range(groups // some):
        for j in range(some):
            o = g * some + j
            live = hot[o : o + 1, :]
            masked[j * ROWS : j * ROWS + cols, :] = feats_ref[...] * live
            masked[j * ROWS + cols : (j + 1) * ROWS, :] = extra * live
        out = lax.dot_general(masked[...], rank_hot, NT, preferred_element_type=F32).astype(BF)
        for j in range(some):
            send_ref[g * some + j] = out[j * ROWS : (j + 1) * ROWS, :]


def column_sets(weight, group):
    half = 64
    n = weight.shape[1] // half
    sets = []
    for j in range(group):
        blocks = [weight[:, b * half : (b + 1) * half] for b in range(j, n, group)]
        sets.append(jnp.concatenate(blocks, axis=1))
    return sets


def first_pieces_kernel(mine_ref, neigh_ref, own_ref, self_ref, late_ref, out_ref):
    del late_ref
    mine = mine_ref[0]
    rows = neigh_ref.shape[0]
    group, _, width = out_ref.shape
    both = zip(column_sets(neigh_ref[...], group), column_sets(own_ref[...], group))
    for j, (neigh, own) in enumerate(both):
        to = jnp.bitwise_xor(mine, j)
        out_ref[to, :rows, :] = neigh
        out_ref[to, rows : 2 * rows, :] = own
        out_ref[to, 2 * rows : 3 * rows, :] = self_ref[:, :width]
        out_ref[to, 3 * rows :, :] = self_ref[:, width:]


def second_pieces_kernel(mine_ref, neigh_ref, own_ref, late_ref, out_ref):
    del late_ref
    mine = mine_ref[0]
    rows = neigh_ref.shape[0]
    both = zip(column_sets(neigh_ref[...], out_ref.shape[0]), column_sets(own_ref[...], out_ref.shape[0]))
    for j, (neigh, own) in enumerate(both):
        to = jnp.bitwise_xor(mine, j)
        out_ref[to, :rows, :] = neigh
        out_ref[to, rows:, :] = own


def mean_kernel(cols, recv_ref, late1_ref, late2_ref, late3_ref, out_ref):
    del late1_ref, late2_ref, late3_ref
    groups, rows, cap = recv_ref.shape
    targets = out_ref.shape[2]
    half = targets // 2
    vertex = lax.broadcasted_iota(jnp.int32, (targets, 1), 0)
    vertex = jnp.where(vertex < half, vertex - half, vertex - (half - 1)).astype(F32)
    acc = jnp.zeros((rows, targets), F32)
    some = 8
    for g in range(groups // some):
        part = jnp.concatenate([recv_ref[g * some + j] for j in range(some)], axis=1)
        code = part[cols : cols + 1, :].astype(F32)
        hot = (vertex == code).astype(F32).astype(BF)
        acc = acc + lax.dot_general(part, hot, NT, preferred_element_type=F32)
    degree = jnp.maximum(acc[cols + 1 : cols + 2, :], 1.0)
    mean = (acc[:cols, :] / degree).astype(BF)
    for j in range(out_ref.shape[0]):
        out_ref[j] = mean


def first_kernel(
    mine_ref, mean_ref, p0_ref, p1_ref, p2_ref, p3_ref, out_ref, weight, acts
):
    mine = mine_ref[0]
    group, rows, targets = mean_ref.shape
    width = targets // 2
    for k, piece in enumerate((p0_ref, p1_ref, p2_ref, p3_ref)):
        at = slice(2 * rows * k, 2 * rows * (k + 1))
        mid = 2 * rows * k + rows
        weight[at, :] = piece[: 2 * rows, :]
        acts[2 * rows * k : mid, :] = mean_ref[jnp.bitwise_xor(mine, k)]
        acts[mid : mid + rows, :width] = piece[2 * rows : 3 * rows, :]
        acts[mid : mid + rows, width:] = piece[3 * rows :, :]
    total = lax.dot_general(weight[...], acts[...], TN, preferred_element_type=F32)
    cols = out_ref.shape[1]
    for z in range(out_ref.shape[0]):
        out_ref[z] = total[z * cols : (z + 1) * cols, :].astype(BF)


def hidden_kernel(
    parts_ref, bias_ref, index_ref, values_ref, live_ref, pieces_ref, pay_ref, left_ref, source, acc
):
    cols, targets = bias_ref.shape[0], live_ref.shape[1]
    width = values_ref.shape[1]
    wide = pay_ref.shape[2]
    total = parts_ref[0].astype(F32)
    for k in range(1, parts_ref.shape[0]):
        total = total + parts_ref[k].astype(F32)
    hidden = jnp.maximum(total + bias_ref[...], 0.0).astype(BF)
    for k in range(pay_ref.shape[0]):
        pay_ref[k, :cols, :] = hidden[:, :wide]
        pay_ref[k, cols : 2 * cols, :] = hidden[:, wide:]
        pay_ref[k, 2 * cols :, :] = pieces_ref[k]
    live = live_ref[...].astype(BF)
    for t in range(targets // width):
        source[t] = hidden[:, t * width : (t + 1) * width]
    acc[...] = jnp.zeros_like(acc)
    for k in range(values_ref.shape[0]):
        target = index_ref[k, 0]
        acc[target] += lax.dot_general(
            source[index_ref[k, 1]], values_ref[k], NT, preferred_element_type=F32
        )
    for t in range(targets // width):
        at = slice(t * width, (t + 1) * width)
        left_ref[:cols, at] = acc[t].astype(BF) * live[:, at]
    left_ref[cols:, :] = hidden * live


def grad_kernel(left_ref, cot_ref, out_ref):
    pieces, piece_rows, piece_cols = out_ref.shape
    quarters = left_ref.shape[0] // piece_rows
    for c in range(pieces // quarters):
        cot = cot_ref[c * piece_cols : (c + 1) * piece_cols, :]
        block = lax.dot_general(left_ref[...], cot, NT, preferred_element_type=F32).astype(BF)
        for q in range(quarters):
            out_ref[c * quarters + q] = block[q * piece_rows : (q + 1) * piece_rows, :]


def second_kernel(
    across_ref, index_ref, values_ref, p0_ref, p1_ref, p2_ref, p3_ref, out_ref, weight, acts, source, acc
):
    across = across_ref[0]
    n, cols, targets = out_ref.shape
    wide = p0_ref.shape[1]
    width = values_ref.shape[1]
    group = 4
    for k, ref in enumerate((p0_ref, p1_ref, p2_ref, p3_ref)):
        mine = slice(k * cols, (k + 1) * cols)
        acts[mine, :wide] = ref[:cols, :]
        acts[mine, wide:] = ref[cols : 2 * cols, :]
        weight[mine, :] = ref[3 * cols :, :]
        weight[(group + k) * cols : (group + k + 1) * cols, :] = ref[2 * cols : 3 * cols, :]
        for t in range(targets // width):
            half, at = divmod(t * width, wide)
            source[t, mine, :] = ref[half * cols : (half + 1) * cols, at : at + width]
    acc[...] = jnp.zeros_like(acc)
    for k in range(values_ref.shape[0]):
        target = index_ref[k, 0]
        acc[target] += lax.dot_general(
            source[index_ref[k, 1]], values_ref[k], NT, preferred_element_type=F32
        )
    for t in range(targets // width):
        acts[group * cols :, t * width : (t + 1) * width] = acc[t].astype(BF)
    total = lax.dot_general(weight[...], acts[...], TN, preferred_element_type=F32)
    for z in range(n):
        out_ref[jnp.bitwise_xor(across, z)] = total[z * cols : (z + 1) * cols, :].astype(BF)


def copies_kernel(terms_ref, late1_ref, late2_ref, late3_ref, out_ref):
    del late1_ref, late2_ref, late3_ref
    total = terms_ref[0].astype(F32)
    for d in range(1, terms_ref.shape[0]):
        total = total + terms_ref[d].astype(F32)
    for d in range(out_ref.shape[0]):
        out_ref[d] = total


def place_kernel(pieces_ref, neigh_ref, self_ref):
    pieces, rows, cols = pieces_ref.shape
    halves = neigh_ref.shape[0] // rows
    quarters = 2 * halves
    for i, out_ref in enumerate((neigh_ref, self_ref)):
        for c in range(pieces // quarters):
            for h in range(halves):
                out_ref[h * rows : (h + 1) * rows, c * cols : (c + 1) * cols] = pieces_ref[
                    c * quarters + i * halves + h
                ]


def out_kernel(p0_ref, p1_ref, p2_ref, p3_ref, bias_ref, live_ref, out_ref):
    total = p0_ref[...].astype(F32) + p1_ref[...].astype(F32)
    total = total + (p2_ref[...].astype(F32) + p3_ref[...].astype(F32))
    out_ref[...] = ((total + bias_ref[...]) * live_ref[...]).astype(BF)


def body(
    edge_feats,
    edge_dst,
    self_feats,
    neigh_one,
    self_one,
    bias_one,
    tile_index,
    tile_values,
    seed_live,
    neigh_two,
    self_two,
    bias_two,
    cotangent,
):
    groups = lax.axis_size("dp")
    n_feat = lax.axis_size("feat")
    edges, cols = edge_feats.shape
    targets = self_feats.shape[0]
    hid = bias_one.shape[0]
    full = neigh_one.shape[1]
    cap = 2 * edges // groups
    blocks = n_feat // GROUP
    wide = full // GROUP
    near = [[GROUP * i + j for j in range(GROUP)] for i in range(blocks)]
    far = [[i + GROUP * j for j in range(blocks)] for i in range(GROUP)]
    z = lax.axis_index("feat")
    mine = (z % GROUP).reshape(1)
    across = (z // GROUP).reshape(1)
    live = seed_live.reshape(1, targets).astype(F32)

    def swap(x, axis, among=None):
        return lax.all_to_all(
            x, axis, split_axis=0, concat_axis=0, tiled=True, axis_index_groups=among
        )

    def trade(x, k):
        return lax.ppermute(x, "feat", [(i, i ^ k) for i in range(n_feat)])

    def shape(*dims, dtype=BF):
        return jax.ShapeDtypeStruct(dims, dtype)

    with jax.named_scope("cotangent"):
        cot = lax.all_gather(cotangent.T, "feat", axis=0, tiled=True)
    with jax.named_scope("edges"):
        send = call(
            functools.partial(pack_kernel, groups, targets),
            shape(groups, ROWS, cap),
            2,
            scratch=[pltpu.VMEM((8 * ROWS, edges), BF)],
            flops=2 * groups * ROWS * edges * cap,
            nbytes=8 << 20,
        )(edge_feats.T, edge_dst.reshape(-1, 128))
        recv = swap(send, "dp")
    with jax.named_scope("pieces"):
        pieces = call(
            first_pieces_kernel,
            shape(GROUP, 4 * cols, wide),
            5,
            smem=(0,),
            late=(4,),
            nbytes=2 << 20,
        )(mine, neigh_one, self_one, self_feats.T, send)
        got = [trade(pieces[k], k) for k in range(1, GROUP)]
    with jax.named_scope("mean"):
        mean = call(
            functools.partial(mean_kernel, cols),
            shape(GROUP, cols, targets),
            4,
            late=(1, 2, 3),
            flops=2 * groups * ROWS * cap * targets,
            nbytes=8 << 20,
        )(recv, *got)
        mean = swap(mean, "feat", near)
    with jax.named_scope("first"):
        first = call(
            first_kernel,
            shape(blocks, hid, targets),
            6,
            scratch=[pltpu.VMEM((8 * cols, wide), BF), pltpu.VMEM((8 * cols, targets), BF)],
            smem=(0,),
            flops=2 * 8 * cols * wide * targets,
            nbytes=2 << 20,
        )(mine, mean, pieces[0], *got)
        parts = swap(first, "feat", far)
    with jax.named_scope("pieces"):
        pieces = call(
            second_pieces_kernel,
            shape(GROUP, 2 * hid, wide),
            4,
            smem=(0,),
            late=(3,),
            nbytes=1 << 20,
        )(mine, neigh_two, self_two, first)
    with jax.named_scope("hidden"):
        pay, left = call(
            hidden_kernel,
            (shape(GROUP, 4 * hid, wide), shape(2 * hid, targets)),
            6,
            scratch=[
                pltpu.VMEM((targets // 128, hid, 128), BF),
                pltpu.VMEM((targets // 128, hid, 128), F32),
            ],
            smem=(2,),
            nbytes=1 << 20,
        )(parts, bias_one.reshape(hid, 1), tile_index, tile_values, live, pieces)
        got = [trade(pay[k], k) for k in range(1, GROUP)]
    with jax.named_scope("grads"):
        piece_rows = 2 * hid * full // 128 // groups
        terms = call(
            grad_kernel,
            shape(groups, piece_rows, 128),
            2,
            flops=2 * 2 * hid * targets * full,
            nbytes=2 << 20,
        )(left, cot)
        terms = swap(terms, "dp")
        spread = call(
            copies_kernel,
            shape(groups, piece_rows, 128, dtype=F32),
            4,
            late=(1, 2, 3),
            nbytes=1 << 20,
        )(terms, *got)
        spread = swap(spread, "dp")
        grad_neigh, grad_self = call(
            place_kernel,
            (shape(hid, full, dtype=F32), shape(hid, full, dtype=F32)),
            1,
            nbytes=1 << 20,
        )(spread)
    with jax.named_scope("second"):
        second = call(
            second_kernel,
            shape(blocks, hid, targets),
            7,
            scratch=[
                pltpu.VMEM((2 * wide, wide), BF),
                pltpu.VMEM((2 * wide, targets), BF),
                pltpu.VMEM((targets // 128, wide, 128), BF),
                pltpu.VMEM((targets // 128, wide, 128), F32),
            ],
            smem=(0, 1),
            flops=2 * 2 * wide * wide * targets,
            nbytes=2 << 20,
        )(across, tile_index, tile_values, pay[0], *got)
        sums = [second[0]] + [trade(second[k], GROUP * k) for k in range(1, blocks)]
        second_out = call(out_kernel, shape(hid, targets), 6, nbytes=1 << 20)(
            *sums, bias_two.reshape(hid, 1), live
        ).T
    return (second_out, grad_neigh, grad_self)


def solution(mesh):
    in_specs = (
        P("dp", "feat"),
        P("dp"),
        P("dp", "feat"),
        P("feat", None),
        P("feat", None),
        P("feat"),
        P("dp", None),
        P("dp", None, None),
        P("dp"),
        P("feat", None),
        P("feat", None),
        P("feat"),
        P("dp", "feat"),
    )
    out_specs = (P("dp", "feat"), P("feat", None), P("feat", None))
    return jax.shard_map(body, mesh=mesh, in_specs=in_specs, out_specs=out_specs, check_vma=False)
```

```python
import functools

import jax
import jax.numpy as jnp
from jax import lax
from jax.experimental import pallas as pl
from jax.experimental.pallas import tpu as pltpu
from jax.sharding import PartitionSpec as P

BF = jnp.bfloat16
F32 = jnp.float32
NT = (((1,), (1,)), ((), ()))
TN = (((0,), (0,)), ((), ()))
ROWS = 64
GROUP = 4
VMEM_LIMIT = 48 * 1024 * 1024


def call(kernel, out_shape, n_in, scratch=(), smem=(), late=(), flops=0, nbytes=0):
    spaces = {i: pltpu.SMEM for i in smem} | {i: pl.ANY for i in late}
    in_specs = [pl.BlockSpec(memory_space=spaces.get(i, pltpu.VMEM)) for i in range(n_in)]
    out_specs = jax.tree.map(lambda _: pl.BlockSpec(memory_space=pltpu.VMEM), out_shape)
    return pl.pallas_call(
        kernel,
        out_shape=out_shape,
        in_specs=in_specs,
        out_specs=out_specs,
        scratch_shapes=list(scratch),
        compiler_params=pltpu.CompilerParams(vmem_limit_bytes=VMEM_LIMIT),
        cost_estimate=pl.CostEstimate(flops=flops, bytes_accessed=nbytes, transcendentals=0),
    )


def pack_kernel(groups, tgt_rows, feats_ref, dst_ref, send_ref, masked):
    cols, edges = feats_ref.shape
    cap = send_ref.shape[2]
    dst = jnp.concatenate([dst_ref[i : i + 1, :] for i in range(dst_ref.shape[0])], axis=1)
    owner = dst // tgt_rows
    local = dst - owner * tgt_rows
    half = tgt_rows // 2
    code = jnp.where(local < half, local - half, local - (half - 1)).astype(F32)
    owner_hot = lax.broadcasted_iota(jnp.int32, (groups, edges), 0) == owner
    owner_hot = owner_hot.astype(F32)
    step = 256
    before = (
        lax.broadcasted_iota(jnp.int32, (step, step), 0)
        < lax.broadcasted_iota(jnp.int32, (step, step), 1)
    ).astype(BF)
    seen = jnp.zeros((groups, 1), F32)
    ranks = []
    for i in range(edges // step):
        part = owner_hot[:, i * step : (i + 1) * step]
        prior = jnp.dot(part.astype(BF), before, preferred_element_type=F32) + seen
        ranks.append(jnp.sum(prior * part, axis=0, keepdims=True))
        seen = seen + jnp.sum(part, axis=1, keepdims=True)
    rank = jnp.concatenate(ranks, axis=1).astype(jnp.int32)
    rank_hot = (lax.broadcasted_iota(jnp.int32, (cap, edges), 0) == rank).astype(F32).astype(BF)
    extra_row = lax.broadcasted_iota(jnp.int32, (ROWS - cols, edges), 0)
    extra = jnp.where(extra_row == 0, code, jnp.where(extra_row == 1, 1.0, 0.0)).astype(BF)
    hot = owner_hot.astype(BF)
    some = masked.shape[0] // ROWS
    for g in range(groups // some):
        for j in range(some):
            o = g * some + j
            live = hot[o : o + 1, :]
            masked[j * ROWS : j * ROWS + cols, :] = feats_ref[...] * live
            masked[j * ROWS + cols : (j + 1) * ROWS, :] = extra * live
        out = lax.dot_general(masked[...], rank_hot, NT, preferred_element_type=F32).astype(BF)
        for j in range(some):
            send_ref[g * some + j] = out[j * ROWS : (j + 1) * ROWS, :]


def column_sets(weight, group):
    half = 64
    n = weight.shape[1] // half
    sets = []
    for j in range(group):
        blocks = [weight[:, b * half : (b + 1) * half] for b in range(j, n, group)]
        sets.append(jnp.concatenate(blocks, axis=1))
    return sets


def first_pieces_kernel(neigh_ref, own_ref, self_ref, cot_ref, late_ref, out_ref, cot_out_ref):
    del late_ref
    rows = neigh_ref.shape[0]
    group, _, width = out_ref.shape
    both = zip(column_sets(neigh_ref[...], group), column_sets(own_ref[...], group))
    for j, (neigh, own) in enumerate(both):
        out_ref[j, :rows, : width // 2] = neigh
        out_ref[j, :rows, width // 2 :] = own
        out_ref[j, rows:, :] = self_ref[...]
    cot_out_ref[...] = cot_ref[...]


def second_pieces_kernel(neigh_ref, own_ref, late_ref, out_ref):
    del late_ref
    group, _, width = out_ref.shape
    both = zip(column_sets(neigh_ref[...], group), column_sets(own_ref[...], group))
    for j, (neigh, own) in enumerate(both):
        out_ref[j, :, : width // 2] = neigh
        out_ref[j, :, width // 2 :] = own


def mean_kernel(cols, recv_ref, pieces_ref, late_ref, out_ref):
    del late_ref
    groups, rows, cap = recv_ref.shape
    targets = out_ref.shape[2]
    half = targets // 2
    vertex = lax.broadcasted_iota(jnp.int32, (targets, 1), 0)
    vertex = jnp.where(vertex < half, vertex - half, vertex - (half - 1)).astype(F32)
    acc = jnp.zeros((rows, targets), F32)
    some = 8
    for g in range(groups // some):
        part = jnp.concatenate([recv_ref[g * some + j] for j in range(some)], axis=1)
        code = part[cols : cols + 1, :].astype(F32)
        hot = (vertex == code).astype(F32).astype(BF)
        acc = acc + lax.dot_general(part, hot, NT, preferred_element_type=F32)
    degree = jnp.maximum(acc[cols + 1 : cols + 2, :], 1.0)
    mean = (acc[:cols, :] / degree).astype(BF)
    for j in range(out_ref.shape[0]):
        out_ref[j, :cols, :] = mean
        out_ref[j, cols:, :] = pieces_ref[j]


def first_kernel(got_ref, out_ref, weight, acts):
    group, rows, targets = got_ref.shape
    rows = rows // 3
    width = targets // 2
    for j in range(group):
        low, mid, high = 2 * rows * j, 2 * rows * j + rows, 2 * rows * (j + 1)
        acts[low:mid, :] = got_ref[j, :rows, :]
        weight[low:mid, :] = got_ref[j, rows : 2 * rows, :width]
        weight[mid:high, :] = got_ref[j, rows : 2 * rows, width:]
        acts[mid:high, :] = got_ref[j, 2 * rows :, :]
    total = lax.dot_general(weight[...], acts[...], TN, preferred_element_type=F32)
    cols = out_ref.shape[1]
    for z in range(out_ref.shape[0]):
        out_ref[z] = total[z * cols : (z + 1) * cols, :].astype(BF)


def hidden_kernel(parts_ref, bias_ref, pieces_ref, out_ref):
    cols = bias_ref.shape[0]
    total = parts_ref[0].astype(F32)
    for k in range(1, parts_ref.shape[0]):
        total = total + parts_ref[k].astype(F32)
    hidden = jnp.maximum(total + bias_ref[...], 0.0).astype(BF)
    for c in range(out_ref.shape[0]):
        out_ref[c, :cols, :] = hidden
        out_ref[c, cols:, :] = pieces_ref[c]


def grad_kernel(
    index_ref, got_ref, values_ref, live_ref, cot_ref, agg_ref, out_ref, left, source, acc
):
    group, cols, targets = got_ref.shape
    cols = cols // 2
    width = values_ref.shape[1]
    wide = group * cols
    for t in range(targets // width):
        for j in range(group):
            at = slice(j * cols, (j + 1) * cols)
            source[t, at, :] = got_ref[j, :cols, t * width : (t + 1) * width]
    acc[...] = jnp.zeros_like(acc)
    for k in range(values_ref.shape[0]):
        target = index_ref[k, 0]
        acc[target] += lax.dot_general(
            source[index_ref[k, 1]], values_ref[k], NT, preferred_element_type=F32
        )
    live = live_ref[...].astype(BF)
    for t in range(targets // width):
        at = slice(t * width, (t + 1) * width)
        tile = acc[t].astype(BF)
        agg_ref[:, at] = tile
        left[:wide, at] = tile * live[:, at]
        left[wide:, at] = source[t] * live[:, at]
    block = lax.dot_general(left[...], cot_ref[...], NT, preferred_element_type=F32)
    at = 0
    for w in range(2):
        for r in range(0, cols, 8):
            for c in range(0, cot_ref.shape[0], 128):
                rows_of = [
                    block[w * wide + j * cols + r : w * wide + j * cols + r + 8, c : c + 128]
                    for j in range(group)
                ]
                out_ref[at] = jnp.concatenate(rows_of, axis=0).astype(BF)
                at += 1


def second_kernel(agg_ref, got_ref, out_ref, weight, acts):
    group, rows, targets = got_ref.shape
    rows = rows // 2
    width = targets // 2
    for j in range(group):
        low, mid, high = 2 * rows * j, 2 * rows * j + rows, 2 * rows * (j + 1)
        weight[low:mid, :] = got_ref[j, rows:, :width]
        acts[low:mid, :] = agg_ref[j * rows : (j + 1) * rows, :]
        weight[mid:high, :] = got_ref[j, rows:, width:]
        acts[mid:high, :] = got_ref[j, :rows, :]
    total = lax.dot_general(weight[...], acts[...], TN, preferred_element_type=F32)
    n, cols, _ = out_ref.shape
    for z in range(n):
        out_ref[z] = total[z * cols : (z + 1) * cols, :].astype(BF)


def sum_kernel(mine_ref, terms_ref, out_ref):
    mine = mine_ref[0]
    total = terms_ref[0].astype(F32)
    for d in range(1, terms_ref.shape[0]):
        total = total + terms_ref[d].astype(F32)
    rows = out_ref.shape[1]
    for j in range(out_ref.shape[0]):
        out_ref[jnp.bitwise_xor(mine, j)] = total[j * rows : (j + 1) * rows, :]


def copies_kernel(p0_ref, p1_ref, p2_ref, p3_ref, late_ref, out_ref):
    del late_ref
    whole = jnp.concatenate([p0_ref[...], p1_ref[...], p2_ref[...], p3_ref[...]], axis=0)
    for d in range(out_ref.shape[0]):
        out_ref[d] = whole


def place_kernel(mine_ref, pieces_ref, neigh_ref, self_ref):
    mine = mine_ref[0]
    half = 64
    at = 0
    for out_ref in (neigh_ref, self_ref):
        for r in range(0, out_ref.shape[0], 8):
            for c in range(2):
                parts = [
                    pieces_ref[at, pl.ds(pl.multiple_of(jnp.bitwise_xor(mine, h) * 8, 8), 8), :]
                    for h in range(4)
                ]
                for e in range(2):
                    for p in range(2):
                        pair = [parts[2 * p + i][:, e * half : (e + 1) * half] for i in range(2)]
                        to = (8 * c + 4 * e + 2 * p) * half
                        out_ref[r : r + 8, to : to + 2 * half] = jnp.concatenate(pair, axis=1)
                at += 1


def out_kernel(parts_ref, bias_ref, live_ref, out_ref):
    total = parts_ref[0].astype(F32)
    for k in range(1, parts_ref.shape[0]):
        total = total + parts_ref[k].astype(F32)
    out_ref[...] = ((total + bias_ref[...]) * live_ref[...]).astype(BF)


def body(
    edge_feats,
    edge_dst,
    self_feats,
    neigh_one,
    self_one,
    bias_one,
    tile_index,
    tile_values,
    seed_live,
    neigh_two,
    self_two,
    bias_two,
    cotangent,
):
    groups = lax.axis_size("dp")
    n_feat = lax.axis_size("feat")
    edges, cols = edge_feats.shape
    targets = self_feats.shape[0]
    hid = bias_one.shape[0]
    full = neigh_one.shape[1]
    cap = 2 * edges // groups
    blocks = n_feat // GROUP
    wide = full // GROUP
    near = [[GROUP * i + j for j in range(GROUP)] for i in range(blocks)]
    far = [[i + GROUP * j for j in range(blocks)] for i in range(GROUP)]
    z = lax.axis_index("feat")
    mine = (z % GROUP).reshape(1)
    live = seed_live.reshape(1, targets).astype(F32)

    def swap(x, axis, among=None):
        return lax.all_to_all(
            x, axis, split_axis=0, concat_axis=0, tiled=True, axis_index_groups=among
        )

    def trade(x, k):
        return lax.ppermute(x, "feat", [(i, i ^ k) for i in range(n_feat)])

    def shape(*dims, dtype=BF):
        return jax.ShapeDtypeStruct(dims, dtype)

    with jax.named_scope("edges"):
        send = call(
            functools.partial(pack_kernel, groups, targets),
            shape(groups, ROWS, cap),
            2,
            scratch=[pltpu.VMEM((8 * ROWS, edges), BF)],
            flops=2 * groups * ROWS * edges * cap,
            nbytes=8 << 20,
        )(edge_feats.T, edge_dst.reshape(-1, 128))
        recv = swap(send, "dp")
    with jax.named_scope("pieces"):
        pieces, cot = call(
            first_pieces_kernel,
            (shape(GROUP, 2 * cols, targets), shape(hid, targets)),
            5,
            late=(4,),
            nbytes=2 << 20,
        )(neigh_one, self_one, self_feats.T, cotangent.T, send)
        cot = lax.all_gather(cot, "feat", axis=0, tiled=True, axis_index_groups=far)
    with jax.named_scope("mean"):
        acts = call(
            functools.partial(mean_kernel, cols),
            shape(GROUP, 3 * cols, targets),
            3,
            late=(2,),
            flops=2 * groups * ROWS * cap * targets,
            nbytes=8 << 20,
        )(recv, pieces, cot)
        acts = swap(acts, "feat", near)
    with jax.named_scope("first"):
        first = call(
            first_kernel,
            shape(blocks, hid, targets),
            1,
            scratch=[pltpu.VMEM((8 * cols, wide), BF), pltpu.VMEM((8 * cols, targets), BF)],
            flops=2 * 8 * cols * wide * targets,
            nbytes=2 << 20,
        )(acts)
        parts = swap(first, "feat", far)
    with jax.named_scope("pieces"):
        pieces = call(
            second_pieces_kernel, shape(GROUP, hid, targets), 3, late=(2,), nbytes=1 << 20
        )(neigh_two, self_two, first)
    with jax.named_scope("hidden"):
        hidden = call(hidden_kernel, shape(GROUP, 2 * hid, targets), 3, nbytes=1 << 20)(
            parts, bias_one.reshape(hid, 1), pieces
        )
        hidden = swap(hidden, "feat", near)
    with jax.named_scope("grads"):
        agg, terms = call(
            grad_kernel,
            (shape(wide, targets), shape(groups, GROUP * 8, 128)),
            5,
            scratch=[
                pltpu.VMEM((2 * wide, targets), BF),
                pltpu.VMEM((targets // 128, wide, 128), BF),
                pltpu.VMEM((targets // 128, wide, 128), F32),
            ],
            smem=(0,),
            flops=2 * 2 * wide * targets * wide,
            nbytes=4 << 20,
        )(tile_index, hidden, tile_values, live, cot)
        terms = swap(terms, "dp")
        mine_sum = call(
            sum_kernel, shape(GROUP, 8, 128, dtype=F32), 2, smem=(0,), nbytes=1 << 20
        )(mine, terms)
        sums = [mine_sum[0]] + [trade(mine_sum[k], k) for k in range(1, GROUP)]
    with jax.named_scope("second"):
        second = call(
            second_kernel,
            shape(blocks, hid, targets),
            2,
            scratch=[pltpu.VMEM((2 * wide, wide), BF), pltpu.VMEM((2 * wide, targets), BF)],
            flops=2 * 2 * wide * wide * targets,
            nbytes=2 << 20,
        )(agg, hidden)
        second = swap(second, "feat", far)
        second_out = call(out_kernel, shape(hid, targets), 3, nbytes=1 << 20)(
            second, bias_two.reshape(hid, 1), live
        ).T
    with jax.named_scope("place"):
        spread = call(
            copies_kernel, shape(groups, GROUP * 8, 128, dtype=F32), 5, late=(4,), nbytes=1 << 20
        )(*sums, second)
        spread = swap(spread, "dp")
        grad_neigh, grad_self = call(
            place_kernel,
            (shape(hid, full, dtype=F32), shape(hid, full, dtype=F32)),
            2,
            smem=(0,),
            nbytes=1 << 20,
        )(mine, spread)
    return (second_out, grad_neigh, grad_self)


def solution(mesh):
    in_specs = (
        P("dp", "feat"),
        P("dp"),
        P("dp", "feat"),
        P("feat", None),
        P("feat", None),
        P("feat"),
        P("dp", None),
        P("dp", None, None),
        P("dp"),
        P("feat", None),
        P("feat", None),
        P("feat"),
        P("dp", "feat"),
    )
    out_specs = (P("dp", "feat"), P("feat", None), P("feat", None))
    return jax.shard_map(body, mesh=mesh, in_specs=in_specs, out_specs=out_specs, check_vma=False)
```

```python
import functools

import jax
import jax.numpy as jnp
from jax import lax
from jax.experimental import pallas as pl
from jax.experimental.pallas import tpu as pltpu
from jax.sharding import PartitionSpec as P

BF = jnp.bfloat16
F32 = jnp.float32
NT = (((1,), (1,)), ((), ()))
TN = (((0,), (0,)), ((), ()))
ROWS = 64
GROUP = 4
VMEM_LIMIT = 48 * 1024 * 1024


def call(kernel, out_shape, n_in, scratch=(), smem=(), late=(), flops=0, nbytes=0):
    spaces = {i: pltpu.SMEM for i in smem} | {i: pl.ANY for i in late}
    in_specs = [pl.BlockSpec(memory_space=spaces.get(i, pltpu.VMEM)) for i in range(n_in)]
    out_specs = jax.tree.map(lambda _: pl.BlockSpec(memory_space=pltpu.VMEM), out_shape)
    return pl.pallas_call(
        kernel,
        out_shape=out_shape,
        in_specs=in_specs,
        out_specs=out_specs,
        scratch_shapes=list(scratch),
        compiler_params=pltpu.CompilerParams(vmem_limit_bytes=VMEM_LIMIT),
        cost_estimate=pl.CostEstimate(flops=flops, bytes_accessed=nbytes, transcendentals=0),
    )


def pack_kernel(groups, tgt_rows, feats_ref, dst_ref, send_ref, masked):
    cols, edges = feats_ref.shape
    cap = send_ref.shape[2]
    dst = jnp.concatenate([dst_ref[i : i + 1, :] for i in range(dst_ref.shape[0])], axis=1)
    owner = dst // tgt_rows
    local = dst - owner * tgt_rows
    half = tgt_rows // 2
    code = jnp.where(local < half, local - half, local - (half - 1)).astype(F32)
    owner_hot = lax.broadcasted_iota(jnp.int32, (groups, edges), 0) == owner
    owner_hot = owner_hot.astype(F32)
    step = 256
    before = (
        lax.broadcasted_iota(jnp.int32, (step, step), 0)
        < lax.broadcasted_iota(jnp.int32, (step, step), 1)
    ).astype(BF)
    seen = jnp.zeros((groups, 1), F32)
    ranks = []
    for i in range(edges // step):
        part = owner_hot[:, i * step : (i + 1) * step]
        prior = jnp.dot(part.astype(BF), before, preferred_element_type=F32) + seen
        ranks.append(jnp.sum(prior * part, axis=0, keepdims=True))
        seen = seen + jnp.sum(part, axis=1, keepdims=True)
    rank = jnp.concatenate(ranks, axis=1).astype(jnp.int32)
    rank_hot = (lax.broadcasted_iota(jnp.int32, (cap, edges), 0) == rank).astype(F32).astype(BF)
    extra_row = lax.broadcasted_iota(jnp.int32, (ROWS - cols, edges), 0)
    extra = jnp.where(extra_row == 0, code, jnp.where(extra_row == 1, 1.0, 0.0)).astype(BF)
    hot = owner_hot.astype(BF)
    some = masked.shape[0] // ROWS
    for g in range(groups // some):
        for j in range(some):
            o = g * some + j
            live = hot[o : o + 1, :]
            masked[j * ROWS : j * ROWS + cols, :] = feats_ref[...] * live
            masked[j * ROWS + cols : (j + 1) * ROWS, :] = extra * live
        out = lax.dot_general(masked[...], rank_hot, NT, preferred_element_type=F32).astype(BF)
        for j in range(some):
            send_ref[g * some + j] = out[j * ROWS : (j + 1) * ROWS, :]


def column_sets(weight, group):
    half = 64
    n = weight.shape[1] // half
    sets = []
    for j in range(group):
        blocks = [weight[:, b * half : (b + 1) * half] for b in range(j, n, group)]
        sets.append(jnp.concatenate(blocks, axis=1))
    return sets


def first_pieces_kernel(neigh_ref, own_ref, self_ref, cot_ref, late_ref, out_ref, cot_out_ref):
    del late_ref
    rows = neigh_ref.shape[0]
    group, _, width = out_ref.shape
    both = zip(column_sets(neigh_ref[...], group), column_sets(own_ref[...], group))
    for j, (neigh, own) in enumerate(both):
        out_ref[j, :rows, : width // 2] = neigh
        out_ref[j, :rows, width // 2 :] = own
        out_ref[j, rows:, :] = self_ref[...]
    cot_out_ref[...] = cot_ref[...]


def second_pieces_kernel(neigh_ref, own_ref, late_ref, out_ref):
    del late_ref
    group, _, width = out_ref.shape
    both = zip(column_sets(neigh_ref[...], group), column_sets(own_ref[...], group))
    for j, (neigh, own) in enumerate(both):
        out_ref[j, :, : width // 2] = neigh
        out_ref[j, :, width // 2 :] = own


def mean_kernel(cols, recv_ref, pieces_ref, cot_ref, far_ref, out_ref, cots_ref):
    groups, rows, cap = recv_ref.shape
    targets = out_ref.shape[2]
    half = targets // 2
    vertex = lax.broadcasted_iota(jnp.int32, (targets, 1), 0)
    vertex = jnp.where(vertex < half, vertex - half, vertex - (half - 1)).astype(F32)
    acc = jnp.zeros((rows, targets), F32)
    some = 8
    for g in range(groups // some):
        part = jnp.concatenate([recv_ref[g * some + j] for j in range(some)], axis=1)
        code = part[cols : cols + 1, :].astype(F32)
        hot = (vertex == code).astype(F32).astype(BF)
        acc = acc + lax.dot_general(part, hot, NT, preferred_element_type=F32)
    degree = jnp.maximum(acc[cols + 1 : cols + 2, :], 1.0)
    mean = (acc[:cols, :] / degree).astype(BF)
    for j in range(out_ref.shape[0]):
        out_ref[j, :cols, :] = mean
        out_ref[j, cols:, :] = pieces_ref[j]
    cots_ref[0] = cot_ref[...]
    cots_ref[1] = far_ref[...]


def first_kernel(got_ref, late_ref, out_ref, weight, acts):
    del late_ref
    group, rows, targets = got_ref.shape
    rows = rows // 3
    width = targets // 2
    for j in range(group):
        low, mid, high = 2 * rows * j, 2 * rows * j + rows, 2 * rows * (j + 1)
        acts[low:mid, :] = got_ref[j, :rows, :]
        weight[low:mid, :] = got_ref[j, rows : 2 * rows, :width]
        weight[mid:high, :] = got_ref[j, rows : 2 * rows, width:]
        acts[mid:high, :] = got_ref[j, 2 * rows :, :]
    total = lax.dot_general(weight[...], acts[...], TN, preferred_element_type=F32)
    cols = out_ref.shape[1]
    for z in range(out_ref.shape[0]):
        out_ref[z] = total[z * cols : (z + 1) * cols, :].astype(BF)


def hidden_kernel(parts_ref, bias_ref, pieces_ref, out_ref):
    cols = bias_ref.shape[0]
    total = parts_ref[0].astype(F32)
    for k in range(1, parts_ref.shape[0]):
        total = total + parts_ref[k].astype(F32)
    hidden = jnp.maximum(total + bias_ref[...], 0.0).astype(BF)
    for c in range(out_ref.shape[0]):
        out_ref[c, :cols, :] = hidden
        out_ref[c, cols:, :] = pieces_ref[c]


def grad_kernel(
    across_ref,
    index_ref,
    got_ref,
    values_ref,
    live_ref,
    cots_ref,
    others_ref,
    agg_ref,
    out_ref,
    left,
    source,
    acc,
    cot,
):
    group, cols, targets = got_ref.shape
    cols = cols // 2
    width = values_ref.shape[1]
    wide = group * cols
    for t in range(targets // width):
        for j in range(group):
            at = slice(j * cols, (j + 1) * cols)
            source[t, at, :] = got_ref[j, :cols, t * width : (t + 1) * width]
    across = across_ref[0]
    for k, ref in enumerate((cots_ref, others_ref, cots_ref, others_ref)):
        cot[jnp.bitwise_xor(across, k)] = ref[k // 2]
    acc[...] = jnp.zeros_like(acc)
    for k in range(values_ref.shape[0]):
        target = index_ref[k, 0]
        acc[target] += lax.dot_general(
            source[index_ref[k, 1]], values_ref[k], NT, preferred_element_type=F32
        )
    live = live_ref[...].astype(BF)
    for t in range(targets // width):
        at = slice(t * width, (t + 1) * width)
        tile = acc[t].astype(BF)
        agg_ref[:, at] = tile
        left[:wide, at] = tile * live[:, at]
        left[wide:, at] = source[t] * live[:, at]
    right = jnp.concatenate([cot[z] for z in range(cot.shape[0])], axis=0)
    block = lax.dot_general(left[...], right, NT, preferred_element_type=F32)
    at = 0
    for w in range(2):
        for r in range(0, cols, 8):
            for c in range(0, right.shape[0], 128):
                rows_of = [
                    block[w * wide + j * cols + r : w * wide + j * cols + r + 8, c : c + 128]
                    for j in range(group)
                ]
                out_ref[at] = jnp.concatenate(rows_of, axis=0).astype(BF)
                at += 1


def second_kernel(agg_ref, got_ref, out_ref, weight, acts):
    group, rows, targets = got_ref.shape
    rows = rows // 2
    width = targets // 2
    for j in range(group):
        low, mid, high = 2 * rows * j, 2 * rows * j + rows, 2 * rows * (j + 1)
        weight[low:mid, :] = got_ref[j, rows:, :width]
        acts[low:mid, :] = agg_ref[j * rows : (j + 1) * rows, :]
        weight[mid:high, :] = got_ref[j, rows:, width:]
        acts[mid:high, :] = got_ref[j, :rows, :]
    total = lax.dot_general(weight[...], acts[...], TN, preferred_element_type=F32)
    n, cols, _ = out_ref.shape
    for z in range(n):
        out_ref[z] = total[z * cols : (z + 1) * cols, :].astype(BF)


def sum_kernel(mine_ref, terms_ref, out_ref):
    mine = mine_ref[0]
    total = terms_ref[0].astype(F32)
    for d in range(1, terms_ref.shape[0]):
        total = total + terms_ref[d].astype(F32)
    rows = out_ref.shape[1]
    for j in range(out_ref.shape[0]):
        out_ref[jnp.bitwise_xor(mine, j)] = total[j * rows : (j + 1) * rows, :]


def copies_kernel(p0_ref, p1_ref, p2_ref, p3_ref, late_ref, out_ref):
    del late_ref
    whole = jnp.concatenate([p0_ref[...], p1_ref[...], p2_ref[...], p3_ref[...]], axis=0)
    for d in range(out_ref.shape[0]):
        out_ref[d] = whole


def place_kernel(mine_ref, pieces_ref, neigh_ref, self_ref):
    mine = mine_ref[0]
    half = 64
    at = 0
    for out_ref in (neigh_ref, self_ref):
        for r in range(0, out_ref.shape[0], 8):
            for c in range(2):
                parts = [
                    pieces_ref[at, pl.ds(pl.multiple_of(jnp.bitwise_xor(mine, h) * 8, 8), 8), :]
                    for h in range(4)
                ]
                for e in range(2):
                    for p in range(2):
                        pair = [parts[2 * p + i][:, e * half : (e + 1) * half] for i in range(2)]
                        to = (8 * c + 4 * e + 2 * p) * half
                        out_ref[r : r + 8, to : to + 2 * half] = jnp.concatenate(pair, axis=1)
                at += 1


def out_kernel(parts_ref, bias_ref, live_ref, out_ref):
    total = parts_ref[0].astype(F32)
    for k in range(1, parts_ref.shape[0]):
        total = total + parts_ref[k].astype(F32)
    out_ref[...] = ((total + bias_ref[...]) * live_ref[...]).astype(BF)


def body(
    edge_feats,
    edge_dst,
    self_feats,
    neigh_one,
    self_one,
    bias_one,
    tile_index,
    tile_values,
    seed_live,
    neigh_two,
    self_two,
    bias_two,
    cotangent,
):
    groups = lax.axis_size("dp")
    n_feat = lax.axis_size("feat")
    edges, cols = edge_feats.shape
    targets = self_feats.shape[0]
    hid = bias_one.shape[0]
    full = neigh_one.shape[1]
    cap = 2 * edges // groups
    blocks = n_feat // GROUP
    wide = full // GROUP
    near = [[GROUP * i + j for j in range(GROUP)] for i in range(blocks)]
    far = [[i + GROUP * j for j in range(blocks)] for i in range(GROUP)]
    z = lax.axis_index("feat")
    mine = (z % GROUP).reshape(1)
    across = (z // GROUP).reshape(1)
    live = seed_live.reshape(1, targets).astype(F32)

    def swap(x, axis, among=None):
        return lax.all_to_all(
            x, axis, split_axis=0, concat_axis=0, tiled=True, axis_index_groups=among
        )

    def trade(x, k):
        return lax.ppermute(x, "feat", [(i, i ^ k) for i in range(n_feat)])

    def shape(*dims, dtype=BF):
        return jax.ShapeDtypeStruct(dims, dtype)

    with jax.named_scope("edges"):
        send = call(
            functools.partial(pack_kernel, groups, targets),
            shape(groups, ROWS, cap),
            2,
            scratch=[pltpu.VMEM((8 * ROWS, edges), BF)],
            flops=2 * groups * ROWS * edges * cap,
            nbytes=8 << 20,
        )(edge_feats.T, edge_dst.reshape(-1, 128))
        recv = swap(send, "dp")
    with jax.named_scope("pieces"):
        pieces, cot = call(
            first_pieces_kernel,
            (shape(GROUP, 2 * cols, targets), shape(hid, targets)),
            5,
            late=(4,),
            nbytes=2 << 20,
        )(neigh_one, self_one, self_feats.T, cotangent.T, send)
        cot_far = trade(cot, 2 * GROUP)
    with jax.named_scope("mean"):
        acts, cots = call(
            functools.partial(mean_kernel, cols),
            (shape(GROUP, 3 * cols, targets), shape(2, hid, targets)),
            4,
            flops=2 * groups * ROWS * cap * targets,
            nbytes=8 << 20,
        )(recv, pieces, cot, cot_far)
        others = trade(cots, GROUP)
        acts = swap(acts, "feat", near)
    with jax.named_scope("first"):
        first = call(
            first_kernel,
            shape(blocks, hid, targets),
            2,
            late=(1,),
            scratch=[pltpu.VMEM((8 * cols, wide), BF), pltpu.VMEM((8 * cols, targets), BF)],
            flops=2 * 8 * cols * wide * targets,
            nbytes=2 << 20,
        )(acts, others)
        parts = swap(first, "feat", far)
    with jax.named_scope("pieces"):
        pieces = call(
            second_pieces_kernel, shape(GROUP, hid, targets), 3, late=(2,), nbytes=1 << 20
        )(neigh_two, self_two, first)
    with jax.named_scope("hidden"):
        hidden = call(hidden_kernel, shape(GROUP, 2 * hid, targets), 3, nbytes=1 << 20)(
            parts, bias_one.reshape(hid, 1), pieces
        )
        hidden = swap(hidden, "feat", near)
    with jax.named_scope("grads"):
        agg, terms = call(
            grad_kernel,
            (shape(wide, targets), shape(groups, GROUP * 8, 128)),
            7,
            scratch=[
                pltpu.VMEM((2 * wide, targets), BF),
                pltpu.VMEM((targets // 128, wide, 128), BF),
                pltpu.VMEM((targets // 128, wide, 128), F32),
                pltpu.VMEM((blocks, hid, targets), BF),
            ],
            smem=(0, 1),
            flops=2 * 2 * wide * targets * wide,
            nbytes=4 << 20,
        )(across, tile_index, hidden, tile_values, live, cots, others)
        terms = swap(terms, "dp")
        mine_sum = call(
            sum_kernel, shape(GROUP, 8, 128, dtype=F32), 2, smem=(0,), nbytes=1 << 20
        )(mine, terms)
        sums = [mine_sum[0]] + [trade(mine_sum[k], k) for k in range(1, GROUP)]
    with jax.named_scope("second"):
        second = call(
            second_kernel,
            shape(blocks, hid, targets),
            2,
            scratch=[pltpu.VMEM((2 * wide, wide), BF), pltpu.VMEM((2 * wide, targets), BF)],
            flops=2 * 2 * wide * wide * targets,
            nbytes=2 << 20,
        )(agg, hidden)
        second = swap(second, "feat", far)
        second_out = call(out_kernel, shape(hid, targets), 3, nbytes=1 << 20)(
            second, bias_two.reshape(hid, 1), live
        ).T
    with jax.named_scope("place"):
        spread = call(
            copies_kernel, shape(groups, GROUP * 8, 128, dtype=F32), 5, late=(4,), nbytes=1 << 20
        )(*sums, second)
        spread = swap(spread, "dp")
        grad_neigh, grad_self = call(
            place_kernel,
            (shape(hid, full, dtype=F32), shape(hid, full, dtype=F32)),
            2,
            smem=(0,),
            nbytes=1 << 20,
        )(mine, spread)
    return (second_out, grad_neigh, grad_self)


def solution(mesh):
    in_specs = (
        P("dp", "feat"),
        P("dp"),
        P("dp", "feat"),
        P("feat", None),
        P("feat", None),
        P("feat"),
        P("dp", None),
        P("dp", None, None),
        P("dp"),
        P("feat", None),
        P("feat", None),
        P("feat"),
        P("dp", "feat"),
    )
    out_specs = (P("dp", "feat"), P("feat", None), P("feat", None))
    return jax.shard_map(body, mesh=mesh, in_specs=in_specs, out_specs=out_specs, check_vma=False)
```

```python
import functools

import jax
import jax.numpy as jnp
from jax import lax
from jax.experimental import pallas as pl
from jax.experimental.pallas import tpu as pltpu
from jax.sharding import PartitionSpec as P

BF = jnp.bfloat16
F32 = jnp.float32
NT = (((1,), (1,)), ((), ()))
TN = (((0,), (0,)), ((), ()))
ROWS = 64
GROUP = 4
VMEM_LIMIT = 48 * 1024 * 1024


def call(kernel, out_shape, n_in, scratch=(), smem=(), late=(), flops=0, nbytes=0):
    spaces = {i: pltpu.SMEM for i in smem} | {i: pl.ANY for i in late}
    in_specs = [pl.BlockSpec(memory_space=spaces.get(i, pltpu.VMEM)) for i in range(n_in)]
    out_specs = jax.tree.map(lambda _: pl.BlockSpec(memory_space=pltpu.VMEM), out_shape)
    return pl.pallas_call(
        kernel,
        out_shape=out_shape,
        in_specs=in_specs,
        out_specs=out_specs,
        scratch_shapes=list(scratch),
        compiler_params=pltpu.CompilerParams(vmem_limit_bytes=VMEM_LIMIT),
        cost_estimate=pl.CostEstimate(flops=flops, bytes_accessed=nbytes, transcendentals=0),
    )


def pack_kernel(groups, tgt_rows, feats_ref, dst_ref, send_ref, masked):
    cols, edges = feats_ref.shape
    cap = send_ref.shape[2]
    dst = jnp.concatenate([dst_ref[i : i + 1, :] for i in range(dst_ref.shape[0])], axis=1)
    owner = dst // tgt_rows
    local = dst - owner * tgt_rows
    half = tgt_rows // 2
    code = jnp.where(local < half, local - half, local - (half - 1)).astype(F32)
    owner_hot = lax.broadcasted_iota(jnp.int32, (groups, edges), 0) == owner
    owner_hot = owner_hot.astype(F32)
    step = 256
    before = (
        lax.broadcasted_iota(jnp.int32, (step, step), 0)
        < lax.broadcasted_iota(jnp.int32, (step, step), 1)
    ).astype(BF)
    seen = jnp.zeros((groups, 1), F32)
    ranks = []
    for i in range(edges // step):
        part = owner_hot[:, i * step : (i + 1) * step]
        prior = jnp.dot(part.astype(BF), before, preferred_element_type=F32) + seen
        ranks.append(jnp.sum(prior * part, axis=0, keepdims=True))
        seen = seen + jnp.sum(part, axis=1, keepdims=True)
    rank = jnp.concatenate(ranks, axis=1).astype(jnp.int32)
    rank_hot = (lax.broadcasted_iota(jnp.int32, (cap, edges), 0) == rank).astype(F32).astype(BF)
    extra_row = lax.broadcasted_iota(jnp.int32, (ROWS - cols, edges), 0)
    extra = jnp.where(extra_row == 0, code, jnp.where(extra_row == 1, 1.0, 0.0)).astype(BF)
    hot = owner_hot.astype(BF)
    some = masked.shape[0] // ROWS
    for g in range(groups // some):
        for j in range(some):
            o = g * some + j
            live = hot[o : o + 1, :]
            masked[j * ROWS : j * ROWS + cols, :] = feats_ref[...] * live
            masked[j * ROWS + cols : (j + 1) * ROWS, :] = extra * live
        out = lax.dot_general(masked[...], rank_hot, NT, preferred_element_type=F32).astype(BF)
        for j in range(some):
            send_ref[g * some + j] = out[j * ROWS : (j + 1) * ROWS, :]


def column_sets(weight, group):
    half = 64
    n = weight.shape[1] // half
    sets = []
    for j in range(group):
        blocks = [weight[:, b * half : (b + 1) * half] for b in range(j, n, group)]
        sets.append(jnp.concatenate(blocks, axis=1))
    return sets


def first_pieces_kernel(mine_ref, neigh_ref, own_ref, self_ref, late_ref, out_ref):
    del late_ref
    mine = mine_ref[0]
    rows = neigh_ref.shape[0]
    group, _, width = out_ref.shape
    both = zip(column_sets(neigh_ref[...], group), column_sets(own_ref[...], group))
    for j, (neigh, own) in enumerate(both):
        to = jnp.bitwise_xor(mine, j)
        out_ref[to, :rows, :] = neigh
        out_ref[to, rows : 2 * rows, :] = own
        out_ref[to, 2 * rows : 3 * rows, :] = self_ref[:, :width]
        out_ref[to, 3 * rows :, :] = self_ref[:, width:]


def second_pieces_kernel(neigh_ref, own_ref, late_ref, out_ref):
    del late_ref
    group, _, width = out_ref.shape
    both = zip(column_sets(neigh_ref[...], group), column_sets(own_ref[...], group))
    for j, (neigh, own) in enumerate(both):
        out_ref[j, :, : width // 2] = neigh
        out_ref[j, :, width // 2 :] = own


def mean_kernel(cols, recv_ref, late1_ref, late2_ref, late3_ref, out_ref):
    del late1_ref, late2_ref, late3_ref
    groups, rows, cap = recv_ref.shape
    targets = out_ref.shape[2]
    half = targets // 2
    vertex = lax.broadcasted_iota(jnp.int32, (targets, 1), 0)
    vertex = jnp.where(vertex < half, vertex - half, vertex - (half - 1)).astype(F32)
    acc = jnp.zeros((rows, targets), F32)
    some = 8
    for g in range(groups // some):
        part = jnp.concatenate([recv_ref[g * some + j] for j in range(some)], axis=1)
        code = part[cols : cols + 1, :].astype(F32)
        hot = (vertex == code).astype(F32).astype(BF)
        acc = acc + lax.dot_general(part, hot, NT, preferred_element_type=F32)
    degree = jnp.maximum(acc[cols + 1 : cols + 2, :], 1.0)
    mean = (acc[:cols, :] / degree).astype(BF)
    for j in range(out_ref.shape[0]):
        out_ref[j] = mean


def first_kernel(
    mine_ref, mean_ref, p0_ref, p1_ref, p2_ref, p3_ref, out_ref, weight, acts
):
    mine = mine_ref[0]
    group, rows, targets = mean_ref.shape
    width = targets // 2
    for k, piece in enumerate((p0_ref, p1_ref, p2_ref, p3_ref)):
        at = slice(2 * rows * k, 2 * rows * (k + 1))
        mid = 2 * rows * k + rows
        weight[at, :] = piece[: 2 * rows, :]
        acts[2 * rows * k : mid, :] = mean_ref[jnp.bitwise_xor(mine, k)]
        acts[mid : mid + rows, :width] = piece[2 * rows : 3 * rows, :]
        acts[mid : mid + rows, width:] = piece[3 * rows :, :]
    total = lax.dot_general(weight[...], acts[...], TN, preferred_element_type=F32)
    cols = out_ref.shape[1]
    for z in range(out_ref.shape[0]):
        out_ref[z] = total[z * cols : (z + 1) * cols, :].astype(BF)


def hidden_kernel(
    parts_ref, bias_ref, index_ref, values_ref, live_ref, pieces_ref, pay_ref, left_ref, source, acc
):
    cols, targets = bias_ref.shape[0], live_ref.shape[1]
    width = values_ref.shape[1]
    total = parts_ref[0].astype(F32)
    for k in range(1, parts_ref.shape[0]):
        total = total + parts_ref[k].astype(F32)
    hidden = jnp.maximum(total + bias_ref[...], 0.0).astype(BF)
    for k in range(pay_ref.shape[0]):
        pay_ref[k, :cols, :] = hidden
        pay_ref[k, cols:, :] = pieces_ref[k]
    live = live_ref[...].astype(BF)
    for t in range(targets // width):
        source[t] = hidden[:, t * width : (t + 1) * width]
    acc[...] = jnp.zeros_like(acc)
    for k in range(values_ref.shape[0]):
        target = index_ref[k, 0]
        acc[target] += lax.dot_general(
            source[index_ref[k, 1]], values_ref[k], NT, preferred_element_type=F32
        )
    for t in range(targets // width):
        at = slice(t * width, (t + 1) * width)
        left_ref[:cols, at] = acc[t].astype(BF) * live[:, at]
    left_ref[cols:, :] = hidden * live


def grad_kernel(left_ref, cot_ref, late_ref, out_ref):
    del late_ref
    pieces, piece_rows, piece_cols = out_ref.shape
    quarters = left_ref.shape[0] // piece_rows
    for c in range(pieces // quarters):
        cot = cot_ref[c * piece_cols : (c + 1) * piece_cols, :]
        block = lax.dot_general(left_ref[...], cot, NT, preferred_element_type=F32).astype(BF)
        for q in range(quarters):
            out_ref[c * quarters + q] = block[q * piece_rows : (q + 1) * piece_rows, :]


def second_kernel(
    across_ref, index_ref, values_ref, got_ref, out_ref, weight, acts, source, acc
):
    across = across_ref[0]
    group, cols, targets = got_ref.shape
    cols = cols // 2
    half = targets // 2
    width = values_ref.shape[1]
    wide = group * cols
    for j in range(group):
        mine = slice(j * cols, (j + 1) * cols)
        acts[mine, :] = got_ref[j, :cols, :]
        weight[mine, :] = got_ref[j, cols:, half:]
        weight[wide + j * cols : wide + (j + 1) * cols, :] = got_ref[j, cols:, :half]
        for t in range(targets // width):
            source[t, mine, :] = got_ref[j, :cols, t * width : (t + 1) * width]
    acc[...] = jnp.zeros_like(acc)
    for k in range(values_ref.shape[0]):
        target = index_ref[k, 0]
        acc[target] += lax.dot_general(
            source[index_ref[k, 1]], values_ref[k], NT, preferred_element_type=F32
        )
    for t in range(targets // width):
        acts[wide:, t * width : (t + 1) * width] = acc[t].astype(BF)
    total = lax.dot_general(weight[...], acts[...], TN, preferred_element_type=F32)
    for z in range(out_ref.shape[0]):
        out_ref[jnp.bitwise_xor(across, z)] = total[z * cols : (z + 1) * cols, :].astype(BF)


def copies_kernel(terms_ref, late_ref, out_ref):
    del late_ref
    total = terms_ref[0].astype(F32)
    for d in range(1, terms_ref.shape[0]):
        total = total + terms_ref[d].astype(F32)
    for d in range(out_ref.shape[0]):
        out_ref[d] = total


def place_kernel(pieces_ref, neigh_ref, self_ref):
    pieces, rows, cols = pieces_ref.shape
    halves = neigh_ref.shape[0] // rows
    quarters = 2 * halves
    for i, out_ref in enumerate((neigh_ref, self_ref)):
        for c in range(pieces // quarters):
            for h in range(halves):
                out_ref[h * rows : (h + 1) * rows, c * cols : (c + 1) * cols] = pieces_ref[
                    c * quarters + i * halves + h
                ]


def out_kernel(p0_ref, p1_ref, p2_ref, p3_ref, bias_ref, live_ref, out_ref):
    total = p0_ref[...].astype(F32) + p1_ref[...].astype(F32)
    total = total + (p2_ref[...].astype(F32) + p3_ref[...].astype(F32))
    out_ref[...] = ((total + bias_ref[...]) * live_ref[...]).astype(BF)


def body(
    edge_feats,
    edge_dst,
    self_feats,
    neigh_one,
    self_one,
    bias_one,
    tile_index,
    tile_values,
    seed_live,
    neigh_two,
    self_two,
    bias_two,
    cotangent,
):
    groups = lax.axis_size("dp")
    n_feat = lax.axis_size("feat")
    edges, cols = edge_feats.shape
    targets = self_feats.shape[0]
    hid = bias_one.shape[0]
    full = neigh_one.shape[1]
    cap = 2 * edges // groups
    blocks = n_feat // GROUP
    wide = full // GROUP
    near = [[GROUP * i + j for j in range(GROUP)] for i in range(blocks)]
    far = [[i + GROUP * j for j in range(blocks)] for i in range(GROUP)]
    z = lax.axis_index("feat")
    mine = (z % GROUP).reshape(1)
    across = (z // GROUP).reshape(1)
    live = seed_live.reshape(1, targets).astype(F32)

    def swap(x, axis, among=None):
        return lax.all_to_all(
            x, axis, split_axis=0, concat_axis=0, tiled=True, axis_index_groups=among
        )

    def trade(x, k):
        return lax.ppermute(x, "feat", [(i, i ^ k) for i in range(n_feat)])

    def shape(*dims, dtype=BF):
        return jax.ShapeDtypeStruct(dims, dtype)

    with jax.named_scope("cotangent"):
        cot = lax.all_gather(cotangent.T, "feat", axis=0, tiled=True)
    with jax.named_scope("edges"):
        send = call(
            functools.partial(pack_kernel, groups, targets),
            shape(groups, ROWS, cap),
            2,
            scratch=[pltpu.VMEM((8 * ROWS, edges), BF)],
            flops=2 * groups * ROWS * edges * cap,
            nbytes=8 << 20,
        )(edge_feats.T, edge_dst.reshape(-1, 128))
        recv = swap(send, "dp")
    with jax.named_scope("pieces"):
        pieces = call(
            first_pieces_kernel,
            shape(GROUP, 4 * cols, wide),
            5,
            smem=(0,),
            late=(4,),
            nbytes=2 << 20,
        )(mine, neigh_one, self_one, self_feats.T, send)
        got = [trade(pieces[k], k) for k in range(1, GROUP)]
    with jax.named_scope("mean"):
        mean = call(
            functools.partial(mean_kernel, cols),
            shape(GROUP, cols, targets),
            4,
            late=(1, 2, 3),
            flops=2 * groups * ROWS * cap * targets,
            nbytes=8 << 20,
        )(recv, *got)
        mean = swap(mean, "feat", near)
    with jax.named_scope("first"):
        first = call(
            first_kernel,
            shape(blocks, hid, targets),
            6,
            scratch=[pltpu.VMEM((8 * cols, wide), BF), pltpu.VMEM((8 * cols, targets), BF)],
            smem=(0,),
            flops=2 * 8 * cols * wide * targets,
            nbytes=2 << 20,
        )(mine, mean, pieces[0], *got)
        parts = swap(first, "feat", far)
    with jax.named_scope("pieces"):
        pieces = call(
            second_pieces_kernel, shape(GROUP, hid, targets), 3, late=(2,), nbytes=1 << 20
        )(neigh_two, self_two, first)
    with jax.named_scope("hidden"):
        pay, left = call(
            hidden_kernel,
            (shape(GROUP, 2 * hid, targets), shape(2 * hid, targets)),
            6,
            scratch=[
                pltpu.VMEM((targets // 128, hid, 128), BF),
                pltpu.VMEM((targets // 128, hid, 128), F32),
            ],
            smem=(2,),
            nbytes=1 << 20,
        )(parts, bias_one.reshape(hid, 1), tile_index, tile_values, live, pieces)
        pay = swap(pay, "feat", near)
    with jax.named_scope("grads"):
        piece_rows = 2 * hid * full // 128 // groups
        terms = call(
            grad_kernel,
            shape(groups, piece_rows, 128),
            3,
            late=(2,),
            flops=2 * 2 * hid * targets * full,
            nbytes=2 << 20,
        )(left, cot, pay)
        terms = swap(terms, "dp")
    with jax.named_scope("second"):
        second = call(
            second_kernel,
            shape(blocks, hid, targets),
            4,
            scratch=[
                pltpu.VMEM((2 * wide, wide), BF),
                pltpu.VMEM((2 * wide, targets), BF),
                pltpu.VMEM((targets // 128, wide, 128), BF),
                pltpu.VMEM((targets // 128, wide, 128), F32),
            ],
            smem=(0, 1),
            flops=2 * 2 * wide * wide * targets,
            nbytes=2 << 20,
        )(across, tile_index, tile_values, pay)
        sums = [second[0]] + [trade(second[k], GROUP * k) for k in range(1, blocks)]
        second_out = call(out_kernel, shape(hid, targets), 6, nbytes=1 << 20)(
            *sums, bias_two.reshape(hid, 1), live
        ).T
    with jax.named_scope("spread"):
        spread = call(
            copies_kernel,
            shape(groups, piece_rows, 128, dtype=F32),
            2,
            late=(1,),
            nbytes=1 << 20,
        )(terms, sums[1])
        spread = swap(spread, "dp")
        grad_neigh, grad_self = call(
            place_kernel,
            (shape(hid, full, dtype=F32), shape(hid, full, dtype=F32)),
            1,
            nbytes=1 << 20,
        )(spread)
    return (second_out, grad_neigh, grad_self)


def solution(mesh):
    in_specs = (
        P("dp", "feat"),
        P("dp"),
        P("dp", "feat"),
        P("feat", None),
        P("feat", None),
        P("feat"),
        P("dp", None),
        P("dp", None, None),
        P("dp"),
        P("feat", None),
        P("feat", None),
        P("feat"),
        P("dp", "feat"),
    )
    out_specs = (P("dp", "feat"), P("feat", None), P("feat", None))
    return jax.shard_map(body, mesh=mesh, in_specs=in_specs, out_specs=out_specs, check_vma=False)
```

```python
import functools

import jax
import jax.numpy as jnp
from jax import lax
from jax.experimental import pallas as pl
from jax.experimental.pallas import tpu as pltpu
from jax.sharding import PartitionSpec as P

BF = jnp.bfloat16
F32 = jnp.float32
NT = (((1,), (1,)), ((), ()))
TN = (((0,), (0,)), ((), ()))
ROWS = 64
GROUP = 4
VMEM_LIMIT = 48 * 1024 * 1024


def call(kernel, out_shape, n_in, scratch=(), smem=(), late=(), flops=0, nbytes=0):
    spaces = {i: pltpu.SMEM for i in smem} | {i: pl.ANY for i in late}
    in_specs = [pl.BlockSpec(memory_space=spaces.get(i, pltpu.VMEM)) for i in range(n_in)]
    out_specs = jax.tree.map(lambda _: pl.BlockSpec(memory_space=pltpu.VMEM), out_shape)
    return pl.pallas_call(
        kernel,
        out_shape=out_shape,
        in_specs=in_specs,
        out_specs=out_specs,
        scratch_shapes=list(scratch),
        compiler_params=pltpu.CompilerParams(vmem_limit_bytes=VMEM_LIMIT),
        cost_estimate=pl.CostEstimate(flops=flops, bytes_accessed=nbytes, transcendentals=0),
    )


def pack_kernel(groups, tgt_rows, feats_ref, dst_ref, send_ref, masked):
    cols, edges = feats_ref.shape
    cap = send_ref.shape[2]
    dst = jnp.concatenate([dst_ref[i : i + 1, :] for i in range(dst_ref.shape[0])], axis=1)
    owner = dst // tgt_rows
    local = dst - owner * tgt_rows
    half = tgt_rows // 2
    code = jnp.where(local < half, local - half, local - (half - 1)).astype(F32)
    owner_hot = lax.broadcasted_iota(jnp.int32, (groups, edges), 0) == owner
    owner_hot = owner_hot.astype(F32)
    step = 256
    before = (
        lax.broadcasted_iota(jnp.int32, (step, step), 0)
        < lax.broadcasted_iota(jnp.int32, (step, step), 1)
    ).astype(BF)
    seen = jnp.zeros((groups, 1), F32)
    ranks = []
    for i in range(edges // step):
        part = owner_hot[:, i * step : (i + 1) * step]
        prior = jnp.dot(part.astype(BF), before, preferred_element_type=F32) + seen
        ranks.append(jnp.sum(prior * part, axis=0, keepdims=True))
        seen = seen + jnp.sum(part, axis=1, keepdims=True)
    rank = jnp.concatenate(ranks, axis=1).astype(jnp.int32)
    rank_hot = (lax.broadcasted_iota(jnp.int32, (cap, edges), 0) == rank).astype(F32).astype(BF)
    extra_row = lax.broadcasted_iota(jnp.int32, (ROWS - cols, edges), 0)
    extra = jnp.where(extra_row == 0, code, jnp.where(extra_row == 1, 1.0, 0.0)).astype(BF)
    hot = owner_hot.astype(BF)
    some = masked.shape[0] // ROWS
    for g in range(groups // some):
        for j in range(some):
            o = g * some + j
            live = hot[o : o + 1, :]
            masked[j * ROWS : j * ROWS + cols, :] = feats_ref[...] * live
            masked[j * ROWS + cols : (j + 1) * ROWS, :] = extra * live
        out = lax.dot_general(masked[...], rank_hot, NT, preferred_element_type=F32).astype(BF)
        for j in range(some):
            send_ref[g * some + j] = out[j * ROWS : (j + 1) * ROWS, :]


def far_place(block, column):
    return (block + column) % GROUP


def column_sets(weight, group):
    half = 64
    n = weight.shape[1] // half
    sets = []
    for h in range(group):
        at = [group * i + far_place(i, h) for i in range(n // group)]
        sets.append(jnp.concatenate([weight[:, b * half : (b + 1) * half] for b in at], axis=1))
    return sets


def first_pieces_kernel(
    block_ref, neigh_ref, own_ref, self_ref, cot_ref, late_ref, out_ref, cot_out_ref
):
    del late_ref
    rows = neigh_ref.shape[0]
    group, _, width = out_ref.shape
    both = zip(column_sets(neigh_ref[...], group), column_sets(own_ref[...], group))
    for h, (neigh, own) in enumerate(both):
        to = far_place(block_ref[0], h)
        out_ref[to, :rows, : width // 2] = neigh
        out_ref[to, :rows, width // 2 :] = own
        out_ref[to, rows:, :] = self_ref[...]
    cot_out_ref[...] = cot_ref[...]


def second_pieces_kernel(block_ref, neigh_ref, own_ref, late_ref, out_ref):
    del late_ref
    group, _, width = out_ref.shape
    both = zip(column_sets(neigh_ref[...], group), column_sets(own_ref[...], group))
    for h, (neigh, own) in enumerate(both):
        to = far_place(block_ref[0], h)
        out_ref[to, :, : width // 2] = neigh
        out_ref[to, :, width // 2 :] = own


def mean_kernel(cols, recv_ref, pieces_ref, late_ref, out_ref):
    del late_ref
    groups, rows, cap = recv_ref.shape
    targets = out_ref.shape[2]
    half = targets // 2
    vertex = lax.broadcasted_iota(jnp.int32, (targets, 1), 0)
    vertex = jnp.where(vertex < half, vertex - half, vertex - (half - 1)).astype(F32)
    acc = jnp.zeros((rows, targets), F32)
    some = 8
    for g in range(groups // some):
        part = jnp.concatenate([recv_ref[g * some + j] for j in range(some)], axis=1)
        code = part[cols : cols + 1, :].astype(F32)
        hot = (vertex == code).astype(F32).astype(BF)
        acc = acc + lax.dot_general(part, hot, NT, preferred_element_type=F32)
    degree = jnp.maximum(acc[cols + 1 : cols + 2, :], 1.0)
    mean = (acc[:cols, :] / degree).astype(BF)
    for j in range(out_ref.shape[0]):
        out_ref[j, :cols, :] = mean
        out_ref[j, cols:, :] = pieces_ref[j]


def first_kernel(got_ref, out_ref, weight, acts):
    group, rows, targets = got_ref.shape
    rows = rows // 3
    width = targets // 2
    for j in range(group):
        low, mid, high = 2 * rows * j, 2 * rows * j + rows, 2 * rows * (j + 1)
        acts[low:mid, :] = got_ref[j, :rows, :]
        weight[low:mid, :] = got_ref[j, rows : 2 * rows, :width]
        weight[mid:high, :] = got_ref[j, rows : 2 * rows, width:]
        acts[mid:high, :] = got_ref[j, 2 * rows :, :]
    total = lax.dot_general(weight[...], acts[...], TN, preferred_element_type=F32)
    cols = out_ref.shape[1]
    for z in range(out_ref.shape[0]):
        out_ref[z] = total[z * cols : (z + 1) * cols, :].astype(BF)


def hidden_kernel(parts_ref, bias_ref, pieces_ref, out_ref):
    cols = bias_ref.shape[0]
    total = parts_ref[0].astype(F32)
    for k in range(1, parts_ref.shape[0]):
        total = total + parts_ref[k].astype(F32)
    hidden = jnp.maximum(total + bias_ref[...], 0.0).astype(BF)
    for c in range(out_ref.shape[0]):
        out_ref[c, :cols, :] = hidden
        out_ref[c, cols:, :] = pieces_ref[c]


def grad_kernel(
    index_ref, got_ref, values_ref, live_ref, cot_ref, agg_ref, out_ref, left, source, acc
):
    group, cols, targets = got_ref.shape
    cols = cols // 2
    width = values_ref.shape[1]
    wide = group * cols
    for t in range(targets // width):
        for j in range(group):
            at = slice(j * cols, (j + 1) * cols)
            source[t, at, :] = got_ref[j, :cols, t * width : (t + 1) * width]
    acc[...] = jnp.zeros_like(acc)
    for k in range(values_ref.shape[0]):
        target = index_ref[k, 0]
        acc[target] += lax.dot_general(
            source[index_ref[k, 1]], values_ref[k], NT, preferred_element_type=F32
        )
    live = live_ref[...].astype(BF)
    for t in range(targets // width):
        at = slice(t * width, (t + 1) * width)
        tile = acc[t].astype(BF)
        agg_ref[:, at] = tile
        left[:wide, at] = tile * live[:, at]
        left[wide:, at] = source[t] * live[:, at]
    block = lax.dot_general(left[...], cot_ref[...], NT, preferred_element_type=F32)
    at = 0
    for w in range(2):
        for r in range(0, cols, 8):
            for c in range(0, cot_ref.shape[0], 128):
                rows_of = [
                    block[w * wide + j * cols + r : w * wide + j * cols + r + 8, c : c + 128]
                    for j in range(group)
                ]
                out_ref[at] = jnp.concatenate(rows_of, axis=0).astype(BF)
                at += 1


def second_kernel(agg_ref, got_ref, out_ref, weight, acts):
    group, rows, targets = got_ref.shape
    rows = rows // 2
    width = targets // 2
    for j in range(group):
        low, mid, high = 2 * rows * j, 2 * rows * j + rows, 2 * rows * (j + 1)
        weight[low:mid, :] = got_ref[j, rows:, :width]
        acts[low:mid, :] = agg_ref[j * rows : (j + 1) * rows, :]
        weight[mid:high, :] = got_ref[j, rows:, width:]
        acts[mid:high, :] = got_ref[j, :rows, :]
    total = lax.dot_general(weight[...], acts[...], TN, preferred_element_type=F32)
    n, cols, _ = out_ref.shape
    for z in range(n):
        out_ref[z] = total[z * cols : (z + 1) * cols, :].astype(BF)


def sum_kernel(mine_ref, terms_ref, out_ref):
    mine = mine_ref[0]
    total = terms_ref[0].astype(F32)
    for d in range(1, terms_ref.shape[0]):
        total = total + terms_ref[d].astype(F32)
    rows = out_ref.shape[1]
    for j in range(out_ref.shape[0]):
        out_ref[jnp.bitwise_xor(mine, j)] = total[j * rows : (j + 1) * rows, :]


def copies_kernel(p0_ref, p1_ref, p2_ref, p3_ref, late_ref, out_ref):
    del late_ref
    whole = jnp.concatenate([p0_ref[...], p1_ref[...], p2_ref[...], p3_ref[...]], axis=0)
    for d in range(out_ref.shape[0]):
        out_ref[d] = whole


def place_kernel(mine_ref, block_ref, pieces_ref, neigh_ref, self_ref):
    half = 64
    starts = []
    for h in range(GROUP):
        from_me = jnp.bitwise_xor(mine_ref[0], far_place(block_ref[0], h))
        starts.append(pl.multiple_of(from_me * 8, 8))
    at = 0
    for out_ref in (neigh_ref, self_ref):
        for r in range(0, out_ref.shape[0], 8):
            for c in range(2):
                parts = [pieces_ref[at, pl.ds(start, 8), :] for start in starts]
                for e in range(2):
                    block = 2 * c + e
                    for p in range(0, GROUP, 2):
                        pair = [
                            parts[(p + i - block) % GROUP][:, e * half : (e + 1) * half]
                            for i in range(2)
                        ]
                        to = (GROUP * block + p) * half
                        out_ref[r : r + 8, to : to + 2 * half] = jnp.concatenate(pair, axis=1)
                at += 1


def out_kernel(parts_ref, bias_ref, live_ref, out_ref):
    total = parts_ref[0].astype(F32)
    for k in range(1, parts_ref.shape[0]):
        total = total + parts_ref[k].astype(F32)
    out_ref[...] = ((total + bias_ref[...]) * live_ref[...]).astype(BF)


def body(
    edge_feats,
    edge_dst,
    self_feats,
    neigh_one,
    self_one,
    bias_one,
    tile_index,
    tile_values,
    seed_live,
    neigh_two,
    self_two,
    bias_two,
    cotangent,
):
    groups = lax.axis_size("dp")
    n_feat = lax.axis_size("feat")
    edges, cols = edge_feats.shape
    targets = self_feats.shape[0]
    hid = bias_one.shape[0]
    full = neigh_one.shape[1]
    cap = 2 * edges // groups
    blocks = n_feat // GROUP
    wide = full // GROUP
    near = [[GROUP * i + j for j in range(GROUP)] for i in range(blocks)]
    far = [[GROUP * i + far_place(i, h) for i in range(blocks)] for h in range(GROUP)]
    z = lax.axis_index("feat")
    mine = (z % GROUP).reshape(1)
    block = (z // GROUP).reshape(1)
    live = seed_live.reshape(1, targets).astype(F32)

    def swap(x, axis, among=None):
        return lax.all_to_all(
            x, axis, split_axis=0, concat_axis=0, tiled=True, axis_index_groups=among
        )

    def trade(x, k):
        return lax.ppermute(x, "feat", [(i, i ^ k) for i in range(n_feat)])

    def shape(*dims, dtype=BF):
        return jax.ShapeDtypeStruct(dims, dtype)

    with jax.named_scope("edges"):
        send = call(
            functools.partial(pack_kernel, groups, targets),
            shape(groups, ROWS, cap),
            2,
            scratch=[pltpu.VMEM((8 * ROWS, edges), BF)],
            flops=2 * groups * ROWS * edges * cap,
            nbytes=8 << 20,
        )(edge_feats.T, edge_dst.reshape(-1, 128))
        recv = swap(send, "dp")
    with jax.named_scope("pieces"):
        pieces, cot = call(
            first_pieces_kernel,
            (shape(GROUP, 2 * cols, targets), shape(hid, targets)),
            6,
            smem=(0,),
            late=(5,),
            nbytes=2 << 20,
        )(block, neigh_one, self_one, self_feats.T, cotangent.T, send)
        cot = lax.all_gather(cot, "feat", axis=0, tiled=True, axis_index_groups=far)
    with jax.named_scope("mean"):
        acts = call(
            functools.partial(mean_kernel, cols),
            shape(GROUP, 3 * cols, targets),
            3,
            late=(2,),
            flops=2 * groups * ROWS * cap * targets,
            nbytes=8 << 20,
        )(recv, pieces, cot)
        acts = swap(acts, "feat", near)
    with jax.named_scope("first"):
        first = call(
            first_kernel,
            shape(blocks, hid, targets),
            1,
            scratch=[pltpu.VMEM((8 * cols, wide), BF), pltpu.VMEM((8 * cols, targets), BF)],
            flops=2 * 8 * cols * wide * targets,
            nbytes=2 << 20,
        )(acts)
        parts = swap(first, "feat", far)
    with jax.named_scope("pieces"):
        pieces = call(
            second_pieces_kernel,
            shape(GROUP, hid, targets),
            4,
            smem=(0,),
            late=(3,),
            nbytes=1 << 20,
        )(block, neigh_two, self_two, first)
    with jax.named_scope("hidden"):
        hidden = call(hidden_kernel, shape(GROUP, 2 * hid, targets), 3, nbytes=1 << 20)(
            parts, bias_one.reshape(hid, 1), pieces
        )
        hidden = swap(hidden, "feat", near)
    with jax.named_scope("grads"):
        agg, terms = call(
            grad_kernel,
            (shape(wide, targets), shape(groups, GROUP * 8, 128)),
            5,
            scratch=[
                pltpu.VMEM((2 * wide, targets), BF),
                pltpu.VMEM((targets // 128, wide, 128), BF),
                pltpu.VMEM((targets // 128, wide, 128), F32),
            ],
            smem=(0,),
            flops=2 * 2 * wide * targets * wide,
            nbytes=4 << 20,
        )(tile_index, hidden, tile_values, live, cot)
        terms = swap(terms, "dp")
        mine_sum = call(
            sum_kernel, shape(GROUP, 8, 128, dtype=F32), 2, smem=(0,), nbytes=1 << 20
        )(mine, terms)
        sums = [mine_sum[0]] + [trade(mine_sum[k], k) for k in range(1, GROUP)]
    with jax.named_scope("second"):
        second = call(
            second_kernel,
            shape(blocks, hid, targets),
            2,
            scratch=[pltpu.VMEM((2 * wide, wide), BF), pltpu.VMEM((2 * wide, targets), BF)],
            flops=2 * 2 * wide * wide * targets,
            nbytes=2 << 20,
        )(agg, hidden)
        second = swap(second, "feat", far)
        second_out = call(out_kernel, shape(hid, targets), 3, nbytes=1 << 20)(
            second, bias_two.reshape(hid, 1), live
        ).T
    with jax.named_scope("place"):
        spread = call(
            copies_kernel, shape(groups, GROUP * 8, 128, dtype=F32), 5, late=(4,), nbytes=1 << 20
        )(*sums, second)
        spread = swap(spread, "dp")
        grad_neigh, grad_self = call(
            place_kernel,
            (shape(hid, full, dtype=F32), shape(hid, full, dtype=F32)),
            3,
            smem=(0, 1),
            nbytes=1 << 20,
        )(mine, block, spread)
    return (second_out, grad_neigh, grad_self)


def solution(mesh):
    in_specs = (
        P("dp", "feat"),
        P("dp"),
        P("dp", "feat"),
        P("feat", None),
        P("feat", None),
        P("feat"),
        P("dp", None),
        P("dp", None, None),
        P("dp"),
        P("feat", None),
        P("feat", None),
        P("feat"),
        P("dp", "feat"),
    )
    out_specs = (P("dp", "feat"), P("feat", None), P("feat", None))
    return jax.shard_map(body, mesh=mesh, in_specs=in_specs, out_specs=out_specs, check_vma=False)
```

```python
import functools

import jax
import jax.numpy as jnp
from jax import lax
from jax.experimental import pallas as pl
from jax.experimental.pallas import tpu as pltpu
from jax.sharding import Mesh
from jax.sharding import PartitionSpec as P

BF = jnp.bfloat16
F32 = jnp.float32
NT = (((1,), (1,)), ((), ()))
TN = (((0,), (0,)), ((), ()))
ROWS = 64
GROUP = 4
FEAT = ("blk", "mem")
VMEM_LIMIT = 48 * 1024 * 1024


def call(kernel, out_shape, n_in, scratch=(), smem=(), late=(), flops=0, nbytes=0):
    spaces = {i: pltpu.SMEM for i in smem} | {i: pl.ANY for i in late}
    in_specs = [pl.BlockSpec(memory_space=spaces.get(i, pltpu.VMEM)) for i in range(n_in)]
    out_specs = jax.tree.map(lambda _: pl.BlockSpec(memory_space=pltpu.VMEM), out_shape)
    return pl.pallas_call(
        kernel,
        out_shape=out_shape,
        in_specs=in_specs,
        out_specs=out_specs,
        scratch_shapes=list(scratch),
        compiler_params=pltpu.CompilerParams(vmem_limit_bytes=VMEM_LIMIT),
        cost_estimate=pl.CostEstimate(flops=flops, bytes_accessed=nbytes, transcendentals=0),
    )


def pack_kernel(groups, tgt_rows, feats_ref, dst_ref, send_ref, masked):
    cols, edges = feats_ref.shape
    cap = send_ref.shape[2]
    dst = jnp.concatenate([dst_ref[i : i + 1, :] for i in range(dst_ref.shape[0])], axis=1)
    owner = dst // tgt_rows
    local = dst - owner * tgt_rows
    half = tgt_rows // 2
    code = jnp.where(local < half, local - half, local - (half - 1)).astype(F32)
    owner_hot = lax.broadcasted_iota(jnp.int32, (groups, edges), 0) == owner
    owner_hot = owner_hot.astype(F32)
    step = 256
    before = (
        lax.broadcasted_iota(jnp.int32, (step, step), 0)
        < lax.broadcasted_iota(jnp.int32, (step, step), 1)
    ).astype(BF)
    seen = jnp.zeros((groups, 1), F32)
    ranks = []
    for i in range(edges // step):
        part = owner_hot[:, i * step : (i + 1) * step]
        prior = jnp.dot(part.astype(BF), before, preferred_element_type=F32) + seen
        ranks.append(jnp.sum(prior * part, axis=0, keepdims=True))
        seen = seen + jnp.sum(part, axis=1, keepdims=True)
    rank = jnp.concatenate(ranks, axis=1).astype(jnp.int32)
    rank_hot = (lax.broadcasted_iota(jnp.int32, (cap, edges), 0) == rank).astype(F32).astype(BF)
    extra_row = lax.broadcasted_iota(jnp.int32, (ROWS - cols, edges), 0)
    extra = jnp.where(extra_row == 0, code, jnp.where(extra_row == 1, 1.0, 0.0)).astype(BF)
    hot = owner_hot.astype(BF)
    some = masked.shape[0] // ROWS
    for g in range(groups // some):
        for j in range(some):
            o = g * some + j
            live = hot[o : o + 1, :]
            masked[j * ROWS : j * ROWS + cols, :] = feats_ref[...] * live
            masked[j * ROWS + cols : (j + 1) * ROWS, :] = extra * live
        out = lax.dot_general(masked[...], rank_hot, NT, preferred_element_type=F32).astype(BF)
        for j in range(some):
            send_ref[g * some + j] = out[j * ROWS : (j + 1) * ROWS, :]


def far_place(block, column):
    return (block + column) % GROUP


def column_sets(weight, group):
    half = 64
    n = weight.shape[1] // half
    sets = []
    for h in range(group):
        at = [group * i + far_place(i, h) for i in range(n // group)]
        sets.append(jnp.concatenate([weight[:, b * half : (b + 1) * half] for b in at], axis=1))
    return sets


def first_pieces_kernel(block_ref, neigh_ref, own_ref, self_ref, late_ref, out_ref):
    del late_ref
    rows = neigh_ref.shape[0]
    group, _, width = out_ref.shape
    both = zip(column_sets(neigh_ref[...], group), column_sets(own_ref[...], group))
    for h, (neigh, own) in enumerate(both):
        to = far_place(block_ref[0], h)
        out_ref[to, :rows, : width // 2] = neigh
        out_ref[to, :rows, width // 2 :] = own
        out_ref[to, rows:, :] = self_ref[...]


def second_pieces_kernel(block_ref, neigh_ref, own_ref, late_ref, out_ref):
    del late_ref
    group, _, width = out_ref.shape
    both = zip(column_sets(neigh_ref[...], group), column_sets(own_ref[...], group))
    for h, (neigh, own) in enumerate(both):
        to = far_place(block_ref[0], h)
        out_ref[to, :, : width // 2] = neigh
        out_ref[to, :, width // 2 :] = own


def mean_kernel(cols, recv_ref, pieces_ref, out_ref):
    groups, rows, cap = recv_ref.shape
    targets = out_ref.shape[2]
    half = targets // 2
    vertex = lax.broadcasted_iota(jnp.int32, (targets, 1), 0)
    vertex = jnp.where(vertex < half, vertex - half, vertex - (half - 1)).astype(F32)
    acc = jnp.zeros((rows, targets), F32)
    some = 8
    for g in range(groups // some):
        part = jnp.concatenate([recv_ref[g * some + j] for j in range(some)], axis=1)
        code = part[cols : cols + 1, :].astype(F32)
        hot = (vertex == code).astype(F32).astype(BF)
        acc = acc + lax.dot_general(part, hot, NT, preferred_element_type=F32)
    degree = jnp.maximum(acc[cols + 1 : cols + 2, :], 1.0)
    mean = (acc[:cols, :] / degree).astype(BF)
    for j in range(out_ref.shape[0]):
        out_ref[j, :cols, :] = mean
        out_ref[j, cols:, :] = pieces_ref[j]


def first_kernel(got_ref, cot_ref, out_ref, weight, acts):
    group, rows, targets = got_ref.shape
    rows = rows // 3
    width = targets // 2
    for j in range(group):
        low, mid, high = 2 * rows * j, 2 * rows * j + rows, 2 * rows * (j + 1)
        acts[low:mid, :] = got_ref[j, :rows, :]
        weight[low:mid, :] = got_ref[j, rows : 2 * rows, :width]
        weight[mid:high, :] = got_ref[j, rows : 2 * rows, width:]
        acts[mid:high, :] = got_ref[j, 2 * rows :, :]
    total = lax.dot_general(weight[...], acts[...], TN, preferred_element_type=F32)
    cols = cot_ref.shape[0]
    for z in range(out_ref.shape[0]):
        out_ref[z, :cols, :] = total[z * cols : (z + 1) * cols, :].astype(BF)
        out_ref[z, cols:, :] = cot_ref[...]


def hidden_kernel(parts_ref, bias_ref, pieces_ref, out_ref):
    cols = bias_ref.shape[0]
    total = parts_ref[0, :cols, :].astype(F32)
    for k in range(1, parts_ref.shape[0]):
        total = total + parts_ref[k, :cols, :].astype(F32)
    hidden = jnp.maximum(total + bias_ref[...], 0.0).astype(BF)
    for c in range(out_ref.shape[0]):
        out_ref[c, :cols, :] = hidden
        out_ref[c, cols:, :] = pieces_ref[c]


def grad_kernel(
    index_ref, got_ref, values_ref, live_ref, parts_ref, agg_ref, out_ref, left, source, acc
):
    group, cols, targets = got_ref.shape
    cols = cols // 2
    width = values_ref.shape[1]
    wide = group * cols
    for t in range(targets // width):
        for j in range(group):
            at = slice(j * cols, (j + 1) * cols)
            source[t, at, :] = got_ref[j, :cols, t * width : (t + 1) * width]
    acc[...] = jnp.zeros_like(acc)
    for k in range(values_ref.shape[0]):
        target = index_ref[k, 0]
        acc[target] += lax.dot_general(
            source[index_ref[k, 1]], values_ref[k], NT, preferred_element_type=F32
        )
    live = live_ref[...].astype(BF)
    for t in range(targets // width):
        at = slice(t * width, (t + 1) * width)
        tile = acc[t].astype(BF)
        agg_ref[:, at] = tile
        left[:wide, at] = tile * live[:, at]
        left[wide:, at] = source[t] * live[:, at]
    right = jnp.concatenate([parts_ref[z, cols:, :] for z in range(parts_ref.shape[0])], axis=0)
    block = lax.dot_general(left[...], right, NT, preferred_element_type=F32)
    at = 0
    for w in range(2):
        for r in range(0, cols, 8):
            for c in range(0, right.shape[0], 128):
                rows_of = [
                    block[w * wide + j * cols + r : w * wide + j * cols + r + 8, c : c + 128]
                    for j in range(group)
                ]
                out_ref[at] = jnp.concatenate(rows_of, axis=0).astype(BF)
                at += 1


def second_kernel(agg_ref, got_ref, out_ref, weight, acts):
    group, rows, targets = got_ref.shape
    rows = rows // 2
    width = targets // 2
    for j in range(group):
        low, mid, high = 2 * rows * j, 2 * rows * j + rows, 2 * rows * (j + 1)
        weight[low:mid, :] = got_ref[j, rows:, :width]
        acts[low:mid, :] = agg_ref[j * rows : (j + 1) * rows, :]
        weight[mid:high, :] = got_ref[j, rows:, width:]
        acts[mid:high, :] = got_ref[j, :rows, :]
    total = lax.dot_general(weight[...], acts[...], TN, preferred_element_type=F32)
    n, cols, _ = out_ref.shape
    for z in range(n):
        out_ref[z] = total[z * cols : (z + 1) * cols, :].astype(BF)


def sum_kernel(terms_ref, out_ref):
    total = terms_ref[0].astype(F32)
    for d in range(1, terms_ref.shape[0]):
        total = total + terms_ref[d].astype(F32)
    out_ref[...] = total


def place_kernel(block_ref, pieces_ref, neigh_ref, self_ref):
    half = 64
    starts = []
    for h in range(GROUP):
        starts.append(pl.multiple_of(far_place(block_ref[0], h) * 8, 8))
    at = 0
    for out_ref in (neigh_ref, self_ref):
        for r in range(0, out_ref.shape[0], 8):
            for c in range(2):
                parts = [pieces_ref[at, pl.ds(start, 8), :] for start in starts]
                for e in range(2):
                    block = 2 * c + e
                    for p in range(0, GROUP, 2):
                        pair = [
                            parts[(p + i - block) % GROUP][:, e * half : (e + 1) * half]
                            for i in range(2)
                        ]
                        to = (GROUP * block + p) * half
                        out_ref[r : r + 8, to : to + 2 * half] = jnp.concatenate(pair, axis=1)
                at += 1


def out_kernel(parts_ref, bias_ref, live_ref, out_ref):
    total = parts_ref[0].astype(F32)
    for k in range(1, parts_ref.shape[0]):
        total = total + parts_ref[k].astype(F32)
    out_ref[...] = ((total + bias_ref[...]) * live_ref[...]).astype(BF)


def body(
    edge_feats,
    edge_dst,
    self_feats,
    neigh_one,
    self_one,
    bias_one,
    tile_index,
    tile_values,
    seed_live,
    neigh_two,
    self_two,
    bias_two,
    cotangent,
):
    groups = lax.axis_size("dp")
    blocks = lax.axis_size("blk")
    edges, cols = edge_feats.shape
    targets = self_feats.shape[0]
    hid = bias_one.shape[0]
    full = neigh_one.shape[1]
    cap = 2 * edges // groups
    wide = full // GROUP
    far = [[GROUP * i + far_place(i, h) for i in range(blocks)] for h in range(GROUP)]
    block = lax.axis_index("blk").reshape(1)
    live = seed_live.reshape(1, targets).astype(F32)

    def swap(x, axis, among=None):
        return lax.all_to_all(
            x, axis, split_axis=0, concat_axis=0, tiled=True, axis_index_groups=among
        )

    def shape(*dims, dtype=BF):
        return jax.ShapeDtypeStruct(dims, dtype)

    with jax.named_scope("edges"):
        send = call(
            functools.partial(pack_kernel, groups, targets),
            shape(groups, ROWS, cap),
            2,
            scratch=[pltpu.VMEM((8 * ROWS, edges), BF)],
            flops=2 * groups * ROWS * edges * cap,
            nbytes=8 << 20,
        )(edge_feats.T, edge_dst.reshape(-1, 128))
        recv = swap(send, "dp")
    with jax.named_scope("pieces"):
        pieces = call(
            first_pieces_kernel,
            shape(GROUP, 2 * cols, targets),
            5,
            smem=(0,),
            late=(4,),
            nbytes=2 << 20,
        )(block, neigh_one, self_one, self_feats.T, send)
    with jax.named_scope("mean"):
        acts = call(
            functools.partial(mean_kernel, cols),
            shape(GROUP, 3 * cols, targets),
            2,
            flops=2 * groups * ROWS * cap * targets,
            nbytes=8 << 20,
        )(recv, pieces)
        acts = swap(acts, "mem")
    with jax.named_scope("first"):
        first = call(
            first_kernel,
            shape(blocks, 2 * hid, targets),
            2,
            scratch=[pltpu.VMEM((8 * cols, wide), BF), pltpu.VMEM((8 * cols, targets), BF)],
            flops=2 * 8 * cols * wide * targets,
            nbytes=2 << 20,
        )(acts, cotangent.T)
        parts = swap(first, FEAT, far)
    with jax.named_scope("pieces"):
        pieces = call(
            second_pieces_kernel,
            shape(GROUP, hid, targets),
            4,
            smem=(0,),
            late=(3,),
            nbytes=1 << 20,
        )(block, neigh_two, self_two, first)
    with jax.named_scope("hidden"):
        hidden = call(hidden_kernel, shape(GROUP, 2 * hid, targets), 3, nbytes=1 << 20)(
            parts, bias_one.reshape(hid, 1), pieces
        )
        hidden = swap(hidden, "mem")
    with jax.named_scope("grads"):
        agg, terms = call(
            grad_kernel,
            (shape(wide, targets), shape(groups, GROUP * 8, 128)),
            5,
            scratch=[
                pltpu.VMEM((2 * wide, targets), BF),
                pltpu.VMEM((targets // 128, wide, 128), BF),
                pltpu.VMEM((targets // 128, wide, 128), F32),
            ],
            smem=(0,),
            flops=2 * 2 * wide * targets * wide,
            nbytes=4 << 20,
        )(tile_index, hidden, tile_values, live, parts)
        terms = swap(terms.reshape(GROUP * groups, 8, 128), ("dp", "mem"))
        mine = call(sum_kernel, shape(GROUP * 8, 128, dtype=F32), 1, nbytes=1 << 20)(
            terms.reshape(groups, GROUP * 8, 128)
        )
    with jax.named_scope("second"):
        second = call(
            second_kernel,
            shape(blocks, hid, targets),
            2,
            scratch=[pltpu.VMEM((2 * wide, wide), BF), pltpu.VMEM((2 * wide, targets), BF)],
            flops=2 * 2 * wide * wide * targets,
            nbytes=2 << 20,
        )(agg, hidden)
        second = swap(second, FEAT, far)
        second_out = call(out_kernel, shape(hid, targets), 3, nbytes=1 << 20)(
            second, bias_two.reshape(hid, 1), live
        ).T
    with jax.named_scope("place"):
        spread = lax.all_gather(mine, "dp", axis=0)
        grad_neigh, grad_self = call(
            place_kernel,
            (shape(hid, full, dtype=F32), shape(hid, full, dtype=F32)),
            2,
            smem=(0,),
            nbytes=1 << 20,
        )(block, spread)
    return (second_out, grad_neigh, grad_self)


def solution(mesh):
    shards = mesh.devices.shape
    blocks = mesh.devices.reshape(shards[0], shards[1] // GROUP, GROUP)
    mesh = Mesh(blocks, ("dp",) + FEAT)
    in_specs = (
        P("dp", FEAT),
        P("dp"),
        P("dp", FEAT),
        P(FEAT, None),
        P(FEAT, None),
        P(FEAT),
        P("dp", None),
        P("dp", None, None),
        P("dp"),
        P(FEAT, None),
        P(FEAT, None),
        P(FEAT),
        P("dp", FEAT),
    )
    out_specs = (P("dp", FEAT), P(FEAT, None), P(FEAT, None))
    return jax.shard_map(body, mesh=mesh, in_specs=in_specs, out_specs=out_specs, check_vma=False)
```

```python
import functools

import jax
import jax.numpy as jnp
from jax import lax
from jax.experimental import pallas as pl
from jax.experimental.pallas import tpu as pltpu
from jax.sharding import PartitionSpec as P

BF = jnp.bfloat16
F32 = jnp.float32
NT = (((1,), (1,)), ((), ()))
TN = (((0,), (0,)), ((), ()))
ROWS = 64
GROUP = 4
VMEM_LIMIT = 48 * 1024 * 1024


def call(kernel, out_shape, n_in, scratch=(), smem=(), late=(), flops=0, nbytes=0):
    spaces = {i: pltpu.SMEM for i in smem} | {i: pl.ANY for i in late}
    in_specs = [pl.BlockSpec(memory_space=spaces.get(i, pltpu.VMEM)) for i in range(n_in)]
    out_specs = jax.tree.map(lambda _: pl.BlockSpec(memory_space=pltpu.VMEM), out_shape)
    return pl.pallas_call(
        kernel,
        out_shape=out_shape,
        in_specs=in_specs,
        out_specs=out_specs,
        scratch_shapes=list(scratch),
        compiler_params=pltpu.CompilerParams(vmem_limit_bytes=VMEM_LIMIT),
        cost_estimate=pl.CostEstimate(flops=flops, bytes_accessed=nbytes, transcendentals=0),
    )


def pack_kernel(groups, tgt_rows, feats_ref, dst_ref, send_ref, masked):
    cols, edges = feats_ref.shape
    cap = send_ref.shape[2]
    dst = jnp.concatenate([dst_ref[i : i + 1, :] for i in range(dst_ref.shape[0])], axis=1)
    owner = dst // tgt_rows
    local = dst - owner * tgt_rows
    half = tgt_rows // 2
    code = jnp.where(local < half, local - half, local - (half - 1)).astype(F32)
    owner_hot = lax.broadcasted_iota(jnp.int32, (groups, edges), 0) == owner
    owner_hot = owner_hot.astype(F32)
    step = 256
    before = (
        lax.broadcasted_iota(jnp.int32, (step, step), 0)
        < lax.broadcasted_iota(jnp.int32, (step, step), 1)
    ).astype(BF)
    seen = jnp.zeros((groups, 1), F32)
    ranks = []
    for i in range(edges // step):
        part = owner_hot[:, i * step : (i + 1) * step]
        prior = jnp.dot(part.astype(BF), before, preferred_element_type=F32) + seen
        ranks.append(jnp.sum(prior * part, axis=0, keepdims=True))
        seen = seen + jnp.sum(part, axis=1, keepdims=True)
    rank = jnp.concatenate(ranks, axis=1).astype(jnp.int32)
    rank_hot = (lax.broadcasted_iota(jnp.int32, (cap, edges), 0) == rank).astype(F32).astype(BF)
    extra_row = lax.broadcasted_iota(jnp.int32, (ROWS - cols, edges), 0)
    extra = jnp.where(extra_row == 0, code, jnp.where(extra_row == 1, 1.0, 0.0)).astype(BF)
    hot = owner_hot.astype(BF)
    some = masked.shape[0] // ROWS
    for g in range(groups // some):
        for j in range(some):
            o = g * some + j
            live = hot[o : o + 1, :]
            masked[j * ROWS : j * ROWS + cols, :] = feats_ref[...] * live
            masked[j * ROWS + cols : (j + 1) * ROWS, :] = extra * live
        out = lax.dot_general(masked[...], rank_hot, NT, preferred_element_type=F32).astype(BF)
        for j in range(some):
            send_ref[g * some + j] = out[j * ROWS : (j + 1) * ROWS, :]


def far_place(block, column):
    return (block + column) % GROUP


def column_sets(weight, group):
    half = 64
    n = weight.shape[1] // half
    sets = []
    for h in range(group):
        at = [group * i + far_place(i, h) for i in range(n // group)]
        sets.append(jnp.concatenate([weight[:, b * half : (b + 1) * half] for b in at], axis=1))
    return sets


def first_pieces_kernel(mine_ref, block_ref, neigh_ref, own_ref, self_ref, late_ref, out_ref):
    del late_ref
    mine = mine_ref[0]
    rows = neigh_ref.shape[0]
    group, _, width = out_ref.shape
    both = zip(column_sets(neigh_ref[...], group), column_sets(own_ref[...], group))
    for h, (neigh, own) in enumerate(both):
        to = jnp.bitwise_xor(mine, far_place(block_ref[0], h))
        out_ref[to, :rows, :] = neigh
        out_ref[to, rows : 2 * rows, :] = own
        out_ref[to, 2 * rows : 3 * rows, :] = self_ref[:, :width]
        out_ref[to, 3 * rows :, :] = self_ref[:, width:]


def second_pieces_kernel(mine_ref, block_ref, neigh_ref, own_ref, late_ref, out_ref):
    del late_ref
    mine = mine_ref[0]
    rows = neigh_ref.shape[0]
    both = zip(column_sets(neigh_ref[...], out_ref.shape[0]), column_sets(own_ref[...], out_ref.shape[0]))
    for h, (neigh, own) in enumerate(both):
        to = jnp.bitwise_xor(mine, far_place(block_ref[0], h))
        out_ref[to, :rows, :] = neigh
        out_ref[to, rows:, :] = own


def mean_kernel(cols, recv_ref, late1_ref, late2_ref, late3_ref, out_ref):
    del late1_ref, late2_ref, late3_ref
    groups, rows, cap = recv_ref.shape
    targets = out_ref.shape[2]
    half = targets // 2
    vertex = lax.broadcasted_iota(jnp.int32, (targets, 1), 0)
    vertex = jnp.where(vertex < half, vertex - half, vertex - (half - 1)).astype(F32)
    acc = jnp.zeros((rows, targets), F32)
    some = 8
    for g in range(groups // some):
        part = jnp.concatenate([recv_ref[g * some + j] for j in range(some)], axis=1)
        code = part[cols : cols + 1, :].astype(F32)
        hot = (vertex == code).astype(F32).astype(BF)
        acc = acc + lax.dot_general(part, hot, NT, preferred_element_type=F32)
    degree = jnp.maximum(acc[cols + 1 : cols + 2, :], 1.0)
    mean = (acc[:cols, :] / degree).astype(BF)
    for j in range(out_ref.shape[0]):
        out_ref[j] = mean


def first_kernel(
    mine_ref, mean_ref, p0_ref, p1_ref, p2_ref, p3_ref, out_ref, weight, acts
):
    mine = mine_ref[0]
    group, rows, targets = mean_ref.shape
    width = targets // 2
    for k, piece in enumerate((p0_ref, p1_ref, p2_ref, p3_ref)):
        at = slice(2 * rows * k, 2 * rows * (k + 1))
        mid = 2 * rows * k + rows
        weight[at, :] = piece[: 2 * rows, :]
        acts[2 * rows * k : mid, :] = mean_ref[jnp.bitwise_xor(mine, k)]
        acts[mid : mid + rows, :width] = piece[2 * rows : 3 * rows, :]
        acts[mid : mid + rows, width:] = piece[3 * rows :, :]
    total = lax.dot_general(weight[...], acts[...], TN, preferred_element_type=F32)
    cols = out_ref.shape[1]
    for z in range(out_ref.shape[0]):
        out_ref[z] = total[z * cols : (z + 1) * cols, :].astype(BF)


def hidden_kernel(
    parts_ref, bias_ref, index_ref, values_ref, live_ref, pieces_ref, pay_ref, left_ref, source, acc
):
    cols, targets = bias_ref.shape[0], live_ref.shape[1]
    width = values_ref.shape[1]
    wide = pay_ref.shape[2]
    total = parts_ref[0].astype(F32)
    for k in range(1, parts_ref.shape[0]):
        total = total + parts_ref[k].astype(F32)
    hidden = jnp.maximum(total + bias_ref[...], 0.0).astype(BF)
    for k in range(pay_ref.shape[0]):
        pay_ref[k, :cols, :] = hidden[:, :wide]
        pay_ref[k, cols : 2 * cols, :] = hidden[:, wide:]
        pay_ref[k, 2 * cols :, :] = pieces_ref[k]
    live = live_ref[...].astype(BF)
    for t in range(targets // width):
        source[t] = hidden[:, t * width : (t + 1) * width]
    acc[...] = jnp.zeros_like(acc)
    for k in range(values_ref.shape[0]):
        target = index_ref[k, 0]
        acc[target] += lax.dot_general(
            source[index_ref[k, 1]], values_ref[k], NT, preferred_element_type=F32
        )
    for t in range(targets // width):
        at = slice(t * width, (t + 1) * width)
        left_ref[:cols, at] = acc[t].astype(BF) * live[:, at]
    left_ref[cols:, :] = hidden * live


def grad_kernel(left_ref, cot_ref, late1_ref, late2_ref, late3_ref, out_ref):
    del late1_ref, late2_ref, late3_ref
    pieces, piece_rows, piece_cols = out_ref.shape
    quarters = left_ref.shape[0] // piece_rows
    for c in range(pieces // quarters):
        cot = cot_ref[c * piece_cols : (c + 1) * piece_cols, :]
        block = lax.dot_general(left_ref[...], cot, NT, preferred_element_type=F32).astype(BF)
        for q in range(quarters):
            out_ref[c * quarters + q] = block[q * piece_rows : (q + 1) * piece_rows, :]


def second_kernel(
    across_ref, index_ref, values_ref, p0_ref, p1_ref, p2_ref, p3_ref, out_ref, weight, acts, source, acc
):
    across = across_ref[0]
    n, cols, targets = out_ref.shape
    wide = p0_ref.shape[1]
    width = values_ref.shape[1]
    group = 4
    for k, ref in enumerate((p0_ref, p1_ref, p2_ref, p3_ref)):
        mine = slice(k * cols, (k + 1) * cols)
        acts[mine, :wide] = ref[:cols, :]
        acts[mine, wide:] = ref[cols : 2 * cols, :]
        weight[mine, :] = ref[3 * cols :, :]
        weight[(group + k) * cols : (group + k + 1) * cols, :] = ref[2 * cols : 3 * cols, :]
        for t in range(targets // width):
            half, at = divmod(t * width, wide)
            source[t, mine, :] = ref[half * cols : (half + 1) * cols, at : at + width]
    acc[...] = jnp.zeros_like(acc)
    for k in range(values_ref.shape[0]):
        target = index_ref[k, 0]
        acc[target] += lax.dot_general(
            source[index_ref[k, 1]], values_ref[k], NT, preferred_element_type=F32
        )
    for t in range(targets // width):
        acts[group * cols :, t * width : (t + 1) * width] = acc[t].astype(BF)
    total = lax.dot_general(weight[...], acts[...], TN, preferred_element_type=F32)
    for z in range(n):
        out_ref[jnp.bitwise_xor(across, z)] = total[z * cols : (z + 1) * cols, :].astype(BF)


def copies_kernel(terms_ref, late_ref, out_ref):
    del late_ref
    total = terms_ref[0].astype(F32)
    for d in range(1, terms_ref.shape[0]):
        total = total + terms_ref[d].astype(F32)
    for d in range(out_ref.shape[0]):
        out_ref[d] = total


def place_kernel(pieces_ref, neigh_ref, self_ref):
    pieces, rows, cols = pieces_ref.shape
    halves = neigh_ref.shape[0] // rows
    quarters = 2 * halves
    for i, out_ref in enumerate((neigh_ref, self_ref)):
        for c in range(pieces // quarters):
            for h in range(halves):
                out_ref[h * rows : (h + 1) * rows, c * cols : (c + 1) * cols] = pieces_ref[
                    c * quarters + i * halves + h
                ]


def out_kernel(p0_ref, p1_ref, p2_ref, p3_ref, bias_ref, live_ref, out_ref):
    total = p0_ref[...].astype(F32) + p1_ref[...].astype(F32)
    total = total + (p2_ref[...].astype(F32) + p3_ref[...].astype(F32))
    out_ref[...] = ((total + bias_ref[...]) * live_ref[...]).astype(BF)


def body(
    edge_feats,
    edge_dst,
    self_feats,
    neigh_one,
    self_one,
    bias_one,
    tile_index,
    tile_values,
    seed_live,
    neigh_two,
    self_two,
    bias_two,
    cotangent,
):
    groups = lax.axis_size("dp")
    n_feat = lax.axis_size("feat")
    edges, cols = edge_feats.shape
    targets = self_feats.shape[0]
    hid = bias_one.shape[0]
    full = neigh_one.shape[1]
    cap = 2 * edges // groups
    blocks = n_feat // GROUP
    wide = full // GROUP
    near = [[GROUP * i + j for j in range(GROUP)] for i in range(blocks)]
    far = [[GROUP * i + far_place(i, h) for i in range(blocks)] for h in range(GROUP)]
    z = lax.axis_index("feat")
    mine = (z % GROUP).reshape(1)
    block = (z // GROUP).reshape(1)
    live = seed_live.reshape(1, targets).astype(F32)

    def swap(x, axis, among=None):
        return lax.all_to_all(
            x, axis, split_axis=0, concat_axis=0, tiled=True, axis_index_groups=among
        )

    def trade(x, k):
        return lax.ppermute(x, "feat", [(i, i ^ k) for i in range(n_feat)])

    def trade_far(x, k):
        pairs = [(group[i], group[i ^ k]) for group in far for i in range(blocks)]
        return lax.ppermute(x, "feat", pairs)

    def shape(*dims, dtype=BF):
        return jax.ShapeDtypeStruct(dims, dtype)

    with jax.named_scope("cotangent"):
        cot = lax.all_gather(cotangent.T, "feat", axis=0, tiled=True)
    with jax.named_scope("edges"):
        send = call(
            functools.partial(pack_kernel, groups, targets),
            shape(groups, ROWS, cap),
            2,
            scratch=[pltpu.VMEM((8 * ROWS, edges), BF)],
            flops=2 * groups * ROWS * edges * cap,
            nbytes=8 << 20,
        )(edge_feats.T, edge_dst.reshape(-1, 128))
        recv = swap(send, "dp")
    with jax.named_scope("pieces"):
        pieces = call(
            first_pieces_kernel,
            shape(GROUP, 4 * cols, wide),
            6,
            smem=(0, 1),
            late=(5,),
            nbytes=2 << 20,
        )(mine, block, neigh_one, self_one, self_feats.T, send)
        got = [trade(pieces[k], k) for k in range(1, GROUP)]
    with jax.named_scope("mean"):
        mean = call(
            functools.partial(mean_kernel, cols),
            shape(GROUP, cols, targets),
            4,
            late=(1, 2, 3),
            flops=2 * groups * ROWS * cap * targets,
            nbytes=8 << 20,
        )(recv, *got)
        mean = swap(mean, "feat", near)
    with jax.named_scope("first"):
        first = call(
            first_kernel,
            shape(blocks, hid, targets),
            6,
            scratch=[pltpu.VMEM((8 * cols, wide), BF), pltpu.VMEM((8 * cols, targets), BF)],
            smem=(0,),
            flops=2 * 8 * cols * wide * targets,
            nbytes=2 << 20,
        )(mine, mean, pieces[0], *got)
        parts = swap(first, "feat", far)
    with jax.named_scope("pieces"):
        pieces = call(
            second_pieces_kernel,
            shape(GROUP, 2 * hid, wide),
            5,
            smem=(0, 1),
            late=(4,),
            nbytes=1 << 20,
        )(mine, block, neigh_two, self_two, first)
    with jax.named_scope("hidden"):
        pay, left = call(
            hidden_kernel,
            (shape(GROUP, 4 * hid, wide), shape(2 * hid, targets)),
            6,
            scratch=[
                pltpu.VMEM((targets // 128, hid, 128), BF),
                pltpu.VMEM((targets // 128, hid, 128), F32),
            ],
            smem=(2,),
            nbytes=1 << 20,
        )(parts, bias_one.reshape(hid, 1), tile_index, tile_values, live, pieces)
        got = [trade(pay[k], k) for k in range(1, GROUP)]
    with jax.named_scope("grads"):
        piece_rows = 2 * hid * full // 128 // groups
        terms = call(
            grad_kernel,
            shape(groups, piece_rows, 128),
            5,
            late=(2, 3, 4),
            flops=2 * 2 * hid * targets * full,
            nbytes=2 << 20,
        )(left, cot, *got)
        terms = swap(terms, "dp")
    with jax.named_scope("second"):
        second = call(
            second_kernel,
            shape(blocks, hid, targets),
            7,
            scratch=[
                pltpu.VMEM((2 * wide, wide), BF),
                pltpu.VMEM((2 * wide, targets), BF),
                pltpu.VMEM((targets // 128, wide, 128), BF),
                pltpu.VMEM((targets // 128, wide, 128), F32),
            ],
            smem=(0, 1),
            flops=2 * 2 * wide * wide * targets,
            nbytes=2 << 20,
        )(block, tile_index, tile_values, pay[0], *got)
        sums = [second[0]] + [trade_far(second[k], k) for k in range(1, blocks)]
        second_out = call(out_kernel, shape(hid, targets), 6, nbytes=1 << 20)(
            *sums, bias_two.reshape(hid, 1), live
        ).T
    with jax.named_scope("spread"):
        spread = call(
            copies_kernel,
            shape(groups, piece_rows, 128, dtype=F32),
            2,
            late=(1,),
            nbytes=1 << 20,
        )(terms, second)
        spread = swap(spread, "dp")
        grad_neigh, grad_self = call(
            place_kernel,
            (shape(hid, full, dtype=F32), shape(hid, full, dtype=F32)),
            1,
            nbytes=1 << 20,
        )(spread)
    return (second_out, grad_neigh, grad_self)


def solution(mesh):
    in_specs = (
        P("dp", "feat"),
        P("dp"),
        P("dp", "feat"),
        P("feat", None),
        P("feat", None),
        P("feat"),
        P("dp", None),
        P("dp", None, None),
        P("dp"),
        P("feat", None),
        P("feat", None),
        P("feat"),
        P("dp", "feat"),
    )
    out_specs = (P("dp", "feat"), P("feat", None), P("feat", None))
    return jax.shard_map(body, mesh=mesh, in_specs=in_specs, out_specs=out_specs, check_vma=False)
```

```python
import functools

import jax
import jax.numpy as jnp
from jax import lax
from jax.experimental import pallas as pl
from jax.experimental.pallas import tpu as pltpu
from jax.sharding import PartitionSpec as P

BF = jnp.bfloat16
F32 = jnp.float32
NT = (((1,), (1,)), ((), ()))
TN = (((0,), (0,)), ((), ()))
ROWS = 64
GROUP = 4
VMEM_LIMIT = 48 * 1024 * 1024


def call(kernel, out_shape, n_in, scratch=(), smem=(), late=(), flops=0, nbytes=0):
    spaces = {i: pltpu.SMEM for i in smem} | {i: pl.ANY for i in late}
    in_specs = [pl.BlockSpec(memory_space=spaces.get(i, pltpu.VMEM)) for i in range(n_in)]
    out_specs = jax.tree.map(lambda _: pl.BlockSpec(memory_space=pltpu.VMEM), out_shape)
    return pl.pallas_call(
        kernel,
        out_shape=out_shape,
        in_specs=in_specs,
        out_specs=out_specs,
        scratch_shapes=list(scratch),
        compiler_params=pltpu.CompilerParams(vmem_limit_bytes=VMEM_LIMIT),
        cost_estimate=pl.CostEstimate(flops=flops, bytes_accessed=nbytes, transcendentals=0),
    )


def pack_kernel(groups, tgt_rows, feats_ref, dst_ref, send_ref, masked):
    cols, edges = feats_ref.shape
    cap = send_ref.shape[2]
    dst = jnp.concatenate([dst_ref[i : i + 1, :] for i in range(dst_ref.shape[0])], axis=1)
    owner = dst // tgt_rows
    local = dst - owner * tgt_rows
    half = tgt_rows // 2
    code = jnp.where(local < half, local - half, local - (half - 1)).astype(F32)
    owner_hot = lax.broadcasted_iota(jnp.int32, (groups, edges), 0) == owner
    owner_hot = owner_hot.astype(F32)
    step = 256
    before = (
        lax.broadcasted_iota(jnp.int32, (step, step), 0)
        < lax.broadcasted_iota(jnp.int32, (step, step), 1)
    ).astype(BF)
    seen = jnp.zeros((groups, 1), F32)
    ranks = []
    for i in range(edges // step):
        part = owner_hot[:, i * step : (i + 1) * step]
        prior = jnp.dot(part.astype(BF), before, preferred_element_type=F32) + seen
        ranks.append(jnp.sum(prior * part, axis=0, keepdims=True))
        seen = seen + jnp.sum(part, axis=1, keepdims=True)
    rank = jnp.concatenate(ranks, axis=1).astype(jnp.int32)
    rank_hot = (lax.broadcasted_iota(jnp.int32, (cap, edges), 0) == rank).astype(F32).astype(BF)
    extra_row = lax.broadcasted_iota(jnp.int32, (ROWS - cols, edges), 0)
    extra = jnp.where(extra_row == 0, code, jnp.where(extra_row == 1, 1.0, 0.0)).astype(BF)
    hot = owner_hot.astype(BF)
    some = masked.shape[0] // ROWS
    for g in range(groups // some):
        for j in range(some):
            o = g * some + j
            live = hot[o : o + 1, :]
            masked[j * ROWS : j * ROWS + cols, :] = feats_ref[...] * live
            masked[j * ROWS + cols : (j + 1) * ROWS, :] = extra * live
        out = lax.dot_general(masked[...], rank_hot, NT, preferred_element_type=F32).astype(BF)
        for j in range(some):
            send_ref[g * some + j] = out[j * ROWS : (j + 1) * ROWS, :]


def far_place(block, column):
    return (block + column) % GROUP


def column_sets(weight, group):
    half = 64
    n = weight.shape[1] // half
    sets = []
    for h in range(group):
        at = [group * i + far_place(i, h) for i in range(n // group)]
        sets.append(jnp.concatenate([weight[:, b * half : (b + 1) * half] for b in at], axis=1))
    return sets


def first_pieces_kernel(mine_ref, block_ref, neigh_ref, own_ref, self_ref, late_ref, out_ref):
    del late_ref
    mine = mine_ref[0]
    rows = neigh_ref.shape[0]
    group, _, width = out_ref.shape
    both = zip(column_sets(neigh_ref[...], group), column_sets(own_ref[...], group))
    for h, (neigh, own) in enumerate(both):
        to = jnp.bitwise_xor(mine, far_place(block_ref[0], h))
        out_ref[to, :rows, :] = neigh
        out_ref[to, rows : 2 * rows, :] = own
        out_ref[to, 2 * rows : 3 * rows, :] = self_ref[:, :width]
        out_ref[to, 3 * rows :, :] = self_ref[:, width:]


def second_pieces_kernel(mine_ref, block_ref, neigh_ref, own_ref, late_ref, out_ref):
    del late_ref
    mine = mine_ref[0]
    rows = neigh_ref.shape[0]
    both = zip(column_sets(neigh_ref[...], out_ref.shape[0]), column_sets(own_ref[...], out_ref.shape[0]))
    for h, (neigh, own) in enumerate(both):
        to = jnp.bitwise_xor(mine, far_place(block_ref[0], h))
        out_ref[to, :rows, :] = neigh
        out_ref[to, rows:, :] = own


def mean_kernel(cols, recv_ref, late1_ref, late2_ref, late3_ref, out_ref):
    del late1_ref, late2_ref, late3_ref
    groups, rows, cap = recv_ref.shape
    targets = out_ref.shape[1]
    half = targets // 2
    vertex = lax.broadcasted_iota(jnp.int32, (targets, 1), 0)
    vertex = jnp.where(vertex < half, vertex - half, vertex - (half - 1)).astype(F32)
    acc = jnp.zeros((rows, targets), F32)
    some = 8
    for g in range(groups // some):
        part = jnp.concatenate([recv_ref[g * some + j] for j in range(some)], axis=1)
        code = part[cols : cols + 1, :].astype(F32)
        hot = (vertex == code).astype(F32).astype(BF)
        acc = acc + lax.dot_general(part, hot, NT, preferred_element_type=F32)
    degree = jnp.maximum(acc[cols + 1 : cols + 2, :], 1.0)
    out_ref[...] = (acc[:cols, :] / degree).astype(BF)


def first_kernel(
    m0_ref, m1_ref, m2_ref, m3_ref, p0_ref, p1_ref, p2_ref, p3_ref, out_ref, weight, acts
):
    rows, targets = m0_ref.shape
    width = targets // 2
    means = (m0_ref, m1_ref, m2_ref, m3_ref)
    for k, (mean, piece) in enumerate(zip(means, (p0_ref, p1_ref, p2_ref, p3_ref))):
        low, mid, high = 2 * rows * k, 2 * rows * k + rows, 2 * rows * (k + 1)
        weight[low:high, :] = piece[: 2 * rows, :]
        acts[low:mid, :] = mean[...]
        acts[mid:high, :width] = piece[2 * rows : 3 * rows, :]
        acts[mid:high, width:] = piece[3 * rows :, :]
    total = lax.dot_general(weight[...], acts[...], TN, preferred_element_type=F32)
    cols = out_ref.shape[1]
    for z in range(out_ref.shape[0]):
        out_ref[z] = total[z * cols : (z + 1) * cols, :].astype(BF)


def hidden_kernel(
    parts_ref, bias_ref, index_ref, values_ref, live_ref, pieces_ref, pay_ref, left_ref, source, acc
):
    cols, targets = bias_ref.shape[0], live_ref.shape[1]
    width = values_ref.shape[1]
    wide = pay_ref.shape[2]
    total = parts_ref[0].astype(F32)
    for k in range(1, parts_ref.shape[0]):
        total = total + parts_ref[k].astype(F32)
    hidden = jnp.maximum(total + bias_ref[...], 0.0).astype(BF)
    for k in range(pay_ref.shape[0]):
        pay_ref[k, :cols, :] = hidden[:, :wide]
        pay_ref[k, cols : 2 * cols, :] = hidden[:, wide:]
        pay_ref[k, 2 * cols :, :] = pieces_ref[k]
    live = live_ref[...].astype(BF)
    for t in range(targets // width):
        source[t] = hidden[:, t * width : (t + 1) * width]
    acc[...] = jnp.zeros_like(acc)
    for k in range(values_ref.shape[0]):
        target = index_ref[k, 0]
        acc[target] += lax.dot_general(
            source[index_ref[k, 1]], values_ref[k], NT, preferred_element_type=F32
        )
    for t in range(targets // width):
        at = slice(t * width, (t + 1) * width)
        left_ref[:cols, at] = acc[t].astype(BF) * live[:, at]
    left_ref[cols:, :] = hidden * live


def grad_kernel(left_ref, cot_ref, late1_ref, late2_ref, late3_ref, out_ref):
    del late1_ref, late2_ref, late3_ref
    pieces, piece_rows, piece_cols = out_ref.shape
    quarters = left_ref.shape[0] // piece_rows
    for c in range(pieces // quarters):
        cot = cot_ref[c * piece_cols : (c + 1) * piece_cols, :]
        block = lax.dot_general(left_ref[...], cot, NT, preferred_element_type=F32).astype(BF)
        for q in range(quarters):
            out_ref[c * quarters + q] = block[q * piece_rows : (q + 1) * piece_rows, :]


def second_kernel(
    across_ref, index_ref, values_ref, p0_ref, p1_ref, p2_ref, p3_ref, out_ref, weight, acts, source, acc
):
    across = across_ref[0]
    n, cols, targets = out_ref.shape
    wide = p0_ref.shape[1]
    width = values_ref.shape[1]
    group = 4
    for k, ref in enumerate((p0_ref, p1_ref, p2_ref, p3_ref)):
        mine = slice(k * cols, (k + 1) * cols)
        acts[mine, :wide] = ref[:cols, :]
        acts[mine, wide:] = ref[cols : 2 * cols, :]
        weight[mine, :] = ref[3 * cols :, :]
        weight[(group + k) * cols : (group + k + 1) * cols, :] = ref[2 * cols : 3 * cols, :]
        for t in range(targets // width):
            half, at = divmod(t * width, wide)
            source[t, mine, :] = ref[half * cols : (half + 1) * cols, at : at + width]
    acc[...] = jnp.zeros_like(acc)
    for k in range(values_ref.shape[0]):
        target = index_ref[k, 0]
        acc[target] += lax.dot_general(
            source[index_ref[k, 1]], values_ref[k], NT, preferred_element_type=F32
        )
    for t in range(targets // width):
        acts[group * cols :, t * width : (t + 1) * width] = acc[t].astype(BF)
    total = lax.dot_general(weight[...], acts[...], TN, preferred_element_type=F32)
    for z in range(n):
        out_ref[jnp.bitwise_xor(across, z)] = total[z * cols : (z + 1) * cols, :].astype(BF)


def copies_kernel(terms_ref, late_ref, out_ref):
    del late_ref
    total = terms_ref[0].astype(F32)
    for d in range(1, terms_ref.shape[0]):
        total = total + terms_ref[d].astype(F32)
    for d in range(out_ref.shape[0]):
        out_ref[d] = total


def place_kernel(pieces_ref, neigh_ref, self_ref):
    pieces, rows, cols = pieces_ref.shape
    halves = neigh_ref.shape[0] // rows
    quarters = 2 * halves
    for i, out_ref in enumerate((neigh_ref, self_ref)):
        for c in range(pieces // quarters):
            for h in range(halves):
                out_ref[h * rows : (h + 1) * rows, c * cols : (c + 1) * cols] = pieces_ref[
                    c * quarters + i * halves + h
                ]


def out_kernel(p0_ref, p1_ref, p2_ref, p3_ref, bias_ref, live_ref, out_ref):
    total = p0_ref[...].astype(F32) + p1_ref[...].astype(F32)
    total = total + (p2_ref[...].astype(F32) + p3_ref[...].astype(F32))
    out_ref[...] = ((total + bias_ref[...]) * live_ref[...]).astype(BF)


def body(
    edge_feats,
    edge_dst,
    self_feats,
    neigh_one,
    self_one,
    bias_one,
    tile_index,
    tile_values,
    seed_live,
    neigh_two,
    self_two,
    bias_two,
    cotangent,
):
    groups = lax.axis_size("dp")
    n_feat = lax.axis_size("feat")
    edges, cols = edge_feats.shape
    targets = self_feats.shape[0]
    hid = bias_one.shape[0]
    full = neigh_one.shape[1]
    cap = 2 * edges // groups
    blocks = n_feat // GROUP
    wide = full // GROUP
    far = [[GROUP * i + far_place(i, h) for i in range(blocks)] for h in range(GROUP)]
    z = lax.axis_index("feat")
    mine = (z % GROUP).reshape(1)
    block = (z // GROUP).reshape(1)
    live = seed_live.reshape(1, targets).astype(F32)

    def swap(x, axis, among=None):
        return lax.all_to_all(
            x, axis, split_axis=0, concat_axis=0, tiled=True, axis_index_groups=among
        )

    def trade(x, k):
        return lax.ppermute(x, "feat", [(i, i ^ k) for i in range(n_feat)])

    def trade_far(x, k):
        pairs = [(group[i], group[i ^ k]) for group in far for i in range(blocks)]
        return lax.ppermute(x, "feat", pairs)

    def shape(*dims, dtype=BF):
        return jax.ShapeDtypeStruct(dims, dtype)

    with jax.named_scope("cotangent"):
        cot = lax.all_gather(cotangent.T, "feat", axis=0, tiled=True)
    with jax.named_scope("edges"):
        send = call(
            functools.partial(pack_kernel, groups, targets),
            shape(groups, ROWS, cap),
            2,
            scratch=[pltpu.VMEM((8 * ROWS, edges), BF)],
            flops=2 * groups * ROWS * edges * cap,
            nbytes=8 << 20,
        )(edge_feats.T, edge_dst.reshape(-1, 128))
        recv = swap(send, "dp")
    with jax.named_scope("pieces"):
        pieces = call(
            first_pieces_kernel,
            shape(GROUP, 4 * cols, wide),
            6,
            smem=(0, 1),
            late=(5,),
            nbytes=2 << 20,
        )(mine, block, neigh_one, self_one, self_feats.T, send)
        got = [trade(pieces[k], k) for k in range(1, GROUP)]
    with jax.named_scope("mean"):
        mean = call(
            functools.partial(mean_kernel, cols),
            shape(cols, targets),
            4,
            late=(1, 2, 3),
            flops=2 * groups * ROWS * cap * targets,
            nbytes=8 << 20,
        )(recv, *got)
        means = [mean] + [trade(mean, k) for k in range(1, GROUP)]
    with jax.named_scope("first"):
        first = call(
            first_kernel,
            shape(blocks, hid, targets),
            8,
            scratch=[pltpu.VMEM((8 * cols, wide), BF), pltpu.VMEM((8 * cols, targets), BF)],
            flops=2 * 8 * cols * wide * targets,
            nbytes=2 << 20,
        )(*means, pieces[0], *got)
        parts = swap(first, "feat", far)
    with jax.named_scope("pieces"):
        pieces = call(
            second_pieces_kernel,
            shape(GROUP, 2 * hid, wide),
            5,
            smem=(0, 1),
            late=(4,),
            nbytes=1 << 20,
        )(mine, block, neigh_two, self_two, first)
    with jax.named_scope("hidden"):
        pay, left = call(
            hidden_kernel,
            (shape(GROUP, 4 * hid, wide), shape(2 * hid, targets)),
            6,
            scratch=[
                pltpu.VMEM((targets // 128, hid, 128), BF),
                pltpu.VMEM((targets // 128, hid, 128), F32),
            ],
            smem=(2,),
            nbytes=1 << 20,
        )(parts, bias_one.reshape(hid, 1), tile_index, tile_values, live, pieces)
        got = [trade(pay[k], k) for k in range(1, GROUP)]
    with jax.named_scope("grads"):
        piece_rows = 2 * hid * full // 128 // groups
        terms = call(
            grad_kernel,
            shape(groups, piece_rows, 128),
            5,
            late=(2, 3, 4),
            flops=2 * 2 * hid * targets * full,
            nbytes=2 << 20,
        )(left, cot, *got)
        terms = swap(terms, "dp")
    with jax.named_scope("second"):
        second = call(
            second_kernel,
            shape(blocks, hid, targets),
            7,
            scratch=[
                pltpu.VMEM((2 * wide, wide), BF),
                pltpu.VMEM((2 * wide, targets), BF),
                pltpu.VMEM((targets // 128, wide, 128), BF),
                pltpu.VMEM((targets // 128, wide, 128), F32),
            ],
            smem=(0, 1),
            flops=2 * 2 * wide * wide * targets,
            nbytes=2 << 20,
        )(block, tile_index, tile_values, pay[0], *got)
        sums = [second[0]] + [trade_far(second[k], k) for k in range(1, blocks)]
        second_out = call(out_kernel, shape(hid, targets), 6, nbytes=1 << 20)(
            *sums, bias_two.reshape(hid, 1), live
        ).T
    with jax.named_scope("spread"):
        spread = call(
            copies_kernel,
            shape(groups, piece_rows, 128, dtype=F32),
            2,
            late=(1,),
            nbytes=1 << 20,
        )(terms, second)
        spread = swap(spread, "dp")
        grad_neigh, grad_self = call(
            place_kernel,
            (shape(hid, full, dtype=F32), shape(hid, full, dtype=F32)),
            1,
            nbytes=1 << 20,
        )(spread)
    return (second_out, grad_neigh, grad_self)


def solution(mesh):
    in_specs = (
        P("dp", "feat"),
        P("dp"),
        P("dp", "feat"),
        P("feat", None),
        P("feat", None),
        P("feat"),
        P("dp", None),
        P("dp", None, None),
        P("dp"),
        P("feat", None),
        P("feat", None),
        P("feat"),
        P("dp", "feat"),
    )
    out_specs = (P("dp", "feat"), P("feat", None), P("feat", None))
    return jax.shard_map(body, mesh=mesh, in_specs=in_specs, out_specs=out_specs, check_vma=False)
```

```python
import functools

import jax
import jax.numpy as jnp
from jax import lax
from jax.experimental import pallas as pl
from jax.experimental.pallas import tpu as pltpu
from jax.sharding import Mesh
from jax.sharding import PartitionSpec as P

BF = jnp.bfloat16
F32 = jnp.float32
NT = (((1,), (1,)), ((), ()))
TN = (((0,), (0,)), ((), ()))
ROWS = 64
GROUP = 4
FEAT = ("blk", "mem")
VMEM_LIMIT = 48 * 1024 * 1024


def call(kernel, out_shape, n_in, scratch=(), smem=(), late=(), flops=0, nbytes=0):
    spaces = {i: pltpu.SMEM for i in smem} | {i: pl.ANY for i in late}
    in_specs = [pl.BlockSpec(memory_space=spaces.get(i, pltpu.VMEM)) for i in range(n_in)]
    out_specs = jax.tree.map(lambda _: pl.BlockSpec(memory_space=pltpu.VMEM), out_shape)
    return pl.pallas_call(
        kernel,
        out_shape=out_shape,
        in_specs=in_specs,
        out_specs=out_specs,
        scratch_shapes=list(scratch),
        compiler_params=pltpu.CompilerParams(vmem_limit_bytes=VMEM_LIMIT),
        cost_estimate=pl.CostEstimate(flops=flops, bytes_accessed=nbytes, transcendentals=0),
    )


def pack_kernel(groups, tgt_rows, feats_ref, dst_ref, send_ref, masked):
    cols, edges = feats_ref.shape
    cap = send_ref.shape[2]
    dst = jnp.concatenate([dst_ref[i : i + 1, :] for i in range(dst_ref.shape[0])], axis=1)
    owner = dst // tgt_rows
    local = dst - owner * tgt_rows
    half = tgt_rows // 2
    code = jnp.where(local < half, local - half, local - (half - 1)).astype(F32)
    owner_hot = lax.broadcasted_iota(jnp.int32, (groups, edges), 0) == owner
    owner_hot = owner_hot.astype(F32)
    step = 256
    before = (
        lax.broadcasted_iota(jnp.int32, (step, step), 0)
        < lax.broadcasted_iota(jnp.int32, (step, step), 1)
    ).astype(BF)
    seen = jnp.zeros((groups, 1), F32)
    ranks = []
    for i in range(edges // step):
        part = owner_hot[:, i * step : (i + 1) * step]
        prior = jnp.dot(part.astype(BF), before, preferred_element_type=F32) + seen
        ranks.append(jnp.sum(prior * part, axis=0, keepdims=True))
        seen = seen + jnp.sum(part, axis=1, keepdims=True)
    rank = jnp.concatenate(ranks, axis=1).astype(jnp.int32)
    rank_hot = (lax.broadcasted_iota(jnp.int32, (cap, edges), 0) == rank).astype(F32).astype(BF)
    extra_row = lax.broadcasted_iota(jnp.int32, (ROWS - cols, edges), 0)
    extra = jnp.where(extra_row == 0, code, jnp.where(extra_row == 1, 1.0, 0.0)).astype(BF)
    hot = owner_hot.astype(BF)
    some = masked.shape[0] // ROWS
    for g in range(groups // some):
        for j in range(some):
            o = g * some + j
            live = hot[o : o + 1, :]
            masked[j * ROWS : j * ROWS + cols, :] = feats_ref[...] * live
            masked[j * ROWS + cols : (j + 1) * ROWS, :] = extra * live
        out = lax.dot_general(masked[...], rank_hot, NT, preferred_element_type=F32).astype(BF)
        for j in range(some):
            send_ref[g * some + j] = out[j * ROWS : (j + 1) * ROWS, :]


def far_place(block, column):
    return (block + column) % GROUP


def column_sets(weight, group):
    half = 64
    n = weight.shape[1] // half
    sets = []
    for h in range(group):
        at = [group * i + far_place(i, h) for i in range(n // group)]
        sets.append(jnp.concatenate([weight[:, b * half : (b + 1) * half] for b in at], axis=1))
    return sets


def first_pieces_kernel(
    block_ref, neigh_ref, own_ref, self_ref, cot_ref, late_ref, out_ref, cot_out_ref
):
    del late_ref
    rows = neigh_ref.shape[0]
    group, _, width = out_ref.shape
    both = zip(column_sets(neigh_ref[...], group), column_sets(own_ref[...], group))
    for h, (neigh, own) in enumerate(both):
        to = far_place(block_ref[0], h)
        out_ref[to, :rows, : width // 2] = neigh
        out_ref[to, :rows, width // 2 :] = own
        out_ref[to, rows:, :] = self_ref[...]
    cot_out_ref[...] = cot_ref[...]


def second_pieces_kernel(block_ref, neigh_ref, own_ref, late_ref, out_ref):
    del late_ref
    group, _, width = out_ref.shape
    both = zip(column_sets(neigh_ref[...], group), column_sets(own_ref[...], group))
    for h, (neigh, own) in enumerate(both):
        to = far_place(block_ref[0], h)
        out_ref[to, :, : width // 2] = neigh
        out_ref[to, :, width // 2 :] = own


def mean_kernel(cols, recv_ref, pieces_ref, late_ref, out_ref):
    del late_ref
    groups, rows, cap = recv_ref.shape
    targets = out_ref.shape[2]
    half = targets // 2
    vertex = lax.broadcasted_iota(jnp.int32, (targets, 1), 0)
    vertex = jnp.where(vertex < half, vertex - half, vertex - (half - 1)).astype(F32)
    acc = jnp.zeros((rows, targets), F32)
    some = 8
    for g in range(groups // some):
        part = jnp.concatenate([recv_ref[g * some + j] for j in range(some)], axis=1)
        code = part[cols : cols + 1, :].astype(F32)
        hot = (vertex == code).astype(F32).astype(BF)
        acc = acc + lax.dot_general(part, hot, NT, preferred_element_type=F32)
    degree = jnp.maximum(acc[cols + 1 : cols + 2, :], 1.0)
    mean = (acc[:cols, :] / degree).astype(BF)
    for j in range(out_ref.shape[0]):
        out_ref[j, :cols, :] = mean
        out_ref[j, cols:, :] = pieces_ref[j]


def first_kernel(got_ref, out_ref, weight, acts):
    group, rows, targets = got_ref.shape
    rows = rows // 3
    width = targets // 2
    for j in range(group):
        low, mid, high = 2 * rows * j, 2 * rows * j + rows, 2 * rows * (j + 1)
        acts[low:mid, :] = got_ref[j, :rows, :]
        weight[low:mid, :] = got_ref[j, rows : 2 * rows, :width]
        weight[mid:high, :] = got_ref[j, rows : 2 * rows, width:]
        acts[mid:high, :] = got_ref[j, 2 * rows :, :]
    total = lax.dot_general(weight[...], acts[...], TN, preferred_element_type=F32)
    cols = out_ref.shape[1]
    for z in range(out_ref.shape[0]):
        out_ref[z] = total[z * cols : (z + 1) * cols, :].astype(BF)


def hidden_kernel(parts_ref, bias_ref, pieces_ref, out_ref):
    cols = bias_ref.shape[0]
    total = parts_ref[0].astype(F32)
    for k in range(1, parts_ref.shape[0]):
        total = total + parts_ref[k].astype(F32)
    hidden = jnp.maximum(total + bias_ref[...], 0.0).astype(BF)
    for c in range(out_ref.shape[0]):
        out_ref[c, :cols, :] = hidden
        out_ref[c, cols:, :] = pieces_ref[c]


def grad_kernel(
    index_ref, got_ref, values_ref, live_ref, cot_ref, agg_ref, out_ref, left, source, acc
):
    group, cols, targets = got_ref.shape
    cols = cols // 2
    width = values_ref.shape[1]
    wide = group * cols
    for t in range(targets // width):
        for j in range(group):
            at = slice(j * cols, (j + 1) * cols)
            source[t, at, :] = got_ref[j, :cols, t * width : (t + 1) * width]
    acc[...] = jnp.zeros_like(acc)
    for k in range(values_ref.shape[0]):
        target = index_ref[k, 0]
        acc[target] += lax.dot_general(
            source[index_ref[k, 1]], values_ref[k], NT, preferred_element_type=F32
        )
    live = live_ref[...].astype(BF)
    for t in range(targets // width):
        at = slice(t * width, (t + 1) * width)
        tile = acc[t].astype(BF)
        agg_ref[:, at] = tile
        left[:wide, at] = tile * live[:, at]
        left[wide:, at] = source[t] * live[:, at]
    block = lax.dot_general(left[...], cot_ref[...], NT, preferred_element_type=F32)
    at = 0
    for w in range(2):
        for r in range(0, cols, 8):
            for c in range(0, cot_ref.shape[0], 128):
                rows_of = [
                    block[w * wide + j * cols + r : w * wide + j * cols + r + 8, c : c + 128]
                    for j in range(group)
                ]
                out_ref[at] = jnp.concatenate(rows_of, axis=0).astype(BF)
                at += 1


def second_kernel(block_ref, agg_ref, got_ref, out_ref, weight, acts):
    group, rows, targets = got_ref.shape
    rows = rows // 2
    width = targets // 2
    for j in range(group):
        low, mid, high = 2 * rows * j, 2 * rows * j + rows, 2 * rows * (j + 1)
        weight[low:mid, :] = got_ref[j, rows:, :width]
        acts[low:mid, :] = agg_ref[j * rows : (j + 1) * rows, :]
        weight[mid:high, :] = got_ref[j, rows:, width:]
        acts[mid:high, :] = got_ref[j, :rows, :]
    total = lax.dot_general(weight[...], acts[...], TN, preferred_element_type=F32)
    n, cols, _ = out_ref.shape
    for z in range(n):
        out_ref[jnp.bitwise_xor(block_ref[0], z)] = total[z * cols : (z + 1) * cols, :].astype(BF)


def copies_kernel(terms_ref, late1_ref, late2_ref, out_ref):
    del late1_ref, late2_ref
    total = terms_ref[0].astype(F32)
    for d in range(1, terms_ref.shape[0]):
        total = total + terms_ref[d].astype(F32)
    for d in range(out_ref.shape[0]):
        out_ref[d] = total


def place_kernel(block_ref, pieces_ref, neigh_ref, self_ref):
    half = 64
    starts = []
    for h in range(GROUP):
        starts.append(pl.multiple_of(far_place(block_ref[0], h) * 8, 8))
    at = 0
    for out_ref in (neigh_ref, self_ref):
        for r in range(0, out_ref.shape[0], 8):
            for c in range(2):
                parts = [pieces_ref[at, pl.ds(start, 8), :] for start in starts]
                for e in range(2):
                    block = 2 * c + e
                    for p in range(0, GROUP, 2):
                        pair = [
                            parts[(p + i - block) % GROUP][:, e * half : (e + 1) * half]
                            for i in range(2)
                        ]
                        to = (GROUP * block + p) * half
                        out_ref[r : r + 8, to : to + 2 * half] = jnp.concatenate(pair, axis=1)
                at += 1


def out_kernel(p0_ref, p1_ref, p2_ref, p3_ref, bias_ref, live_ref, out_ref):
    total = p0_ref[...].astype(F32) + p1_ref[...].astype(F32)
    total = total + (p2_ref[...].astype(F32) + p3_ref[...].astype(F32))
    out_ref[...] = ((total + bias_ref[...]) * live_ref[...]).astype(BF)


def body(
    edge_feats,
    edge_dst,
    self_feats,
    neigh_one,
    self_one,
    bias_one,
    tile_index,
    tile_values,
    seed_live,
    neigh_two,
    self_two,
    bias_two,
    cotangent,
):
    groups = lax.axis_size("dp")
    blocks = lax.axis_size("blk")
    edges, cols = edge_feats.shape
    targets = self_feats.shape[0]
    hid = bias_one.shape[0]
    full = neigh_one.shape[1]
    cap = 2 * edges // groups
    wide = full // GROUP
    far = [[GROUP * i + far_place(i, h) for i in range(blocks)] for h in range(GROUP)]
    block = lax.axis_index("blk").reshape(1)
    live = seed_live.reshape(1, targets).astype(F32)

    def swap(x, axis, among=None):
        return lax.all_to_all(
            x, axis, split_axis=0, concat_axis=0, tiled=True, axis_index_groups=among
        )

    def trade_far(x, k):
        pairs = [(group[i], group[i ^ k]) for group in far for i in range(blocks)]
        return lax.ppermute(x, FEAT, pairs)

    def shape(*dims, dtype=BF):
        return jax.ShapeDtypeStruct(dims, dtype)

    with jax.named_scope("edges"):
        send = call(
            functools.partial(pack_kernel, groups, targets),
            shape(groups, ROWS, cap),
            2,
            scratch=[pltpu.VMEM((8 * ROWS, edges), BF)],
            flops=2 * groups * ROWS * edges * cap,
            nbytes=8 << 20,
        )(edge_feats.T, edge_dst.reshape(-1, 128))
        recv = swap(send, "dp")
    with jax.named_scope("pieces"):
        pieces, cot = call(
            first_pieces_kernel,
            (shape(GROUP, 2 * cols, targets), shape(hid, targets)),
            6,
            smem=(0,),
            late=(5,),
            nbytes=2 << 20,
        )(block, neigh_one, self_one, self_feats.T, cotangent.T, send)
        cot = lax.all_gather(cot, FEAT, axis=0, tiled=True, axis_index_groups=far)
    with jax.named_scope("mean"):
        acts = call(
            functools.partial(mean_kernel, cols),
            shape(GROUP, 3 * cols, targets),
            3,
            late=(2,),
            flops=2 * groups * ROWS * cap * targets,
            nbytes=8 << 20,
        )(recv, pieces, cot)
        acts = swap(acts, "mem")
    with jax.named_scope("first"):
        first = call(
            first_kernel,
            shape(blocks, hid, targets),
            1,
            scratch=[pltpu.VMEM((8 * cols, wide), BF), pltpu.VMEM((8 * cols, targets), BF)],
            flops=2 * 8 * cols * wide * targets,
            nbytes=2 << 20,
        )(acts)
        parts = swap(first, FEAT, far)
    with jax.named_scope("pieces"):
        pieces = call(
            second_pieces_kernel,
            shape(GROUP, hid, targets),
            4,
            smem=(0,),
            late=(3,),
            nbytes=1 << 20,
        )(block, neigh_two, self_two, first)
    with jax.named_scope("hidden"):
        hidden = call(hidden_kernel, shape(GROUP, 2 * hid, targets), 3, nbytes=1 << 20)(
            parts, bias_one.reshape(hid, 1), pieces
        )
        hidden = swap(hidden, "mem")
    with jax.named_scope("grads"):
        agg, terms = call(
            grad_kernel,
            (shape(wide, targets), shape(groups, GROUP * 8, 128)),
            5,
            scratch=[
                pltpu.VMEM((2 * wide, targets), BF),
                pltpu.VMEM((targets // 128, wide, 128), BF),
                pltpu.VMEM((targets // 128, wide, 128), F32),
            ],
            smem=(0,),
            flops=2 * 2 * wide * targets * wide,
            nbytes=4 << 20,
        )(tile_index, hidden, tile_values, live, cot)
        terms = swap(terms.reshape(GROUP * groups, 8, 128), ("dp", "mem"))
    with jax.named_scope("second"):
        second = call(
            second_kernel,
            shape(blocks, hid, targets),
            3,
            scratch=[pltpu.VMEM((2 * wide, wide), BF), pltpu.VMEM((2 * wide, targets), BF)],
            smem=(0,),
            flops=2 * 2 * wide * wide * targets,
            nbytes=2 << 20,
        )(block, agg, hidden)
        sums = [second[0]] + [trade_far(second[k], k) for k in range(1, blocks)]
        second_out = call(out_kernel, shape(hid, targets), 6, nbytes=1 << 20)(
            *sums, bias_two.reshape(hid, 1), live
        ).T
    with jax.named_scope("place"):
        spread = call(
            copies_kernel,
            shape(groups, GROUP * 8, 128, dtype=F32),
            3,
            late=(1, 2),
            nbytes=1 << 20,
        )(terms.reshape(groups, GROUP * 8, 128), second, sums[1])
        spread = swap(spread, "dp")
        grad_neigh, grad_self = call(
            place_kernel,
            (shape(hid, full, dtype=F32), shape(hid, full, dtype=F32)),
            2,
            smem=(0,),
            nbytes=1 << 20,
        )(block, spread)
    return (second_out, grad_neigh, grad_self)


def solution(mesh):
    shards = mesh.devices.shape
    blocks = mesh.devices.reshape(shards[0], shards[1] // GROUP, GROUP)
    mesh = Mesh(blocks, ("dp",) + FEAT)
    in_specs = (
        P("dp", FEAT),
        P("dp"),
        P("dp", FEAT),
        P(FEAT, None),
        P(FEAT, None),
        P(FEAT),
        P("dp", None),
        P("dp", None, None),
        P("dp"),
        P(FEAT, None),
        P(FEAT, None),
        P(FEAT),
        P("dp", FEAT),
    )
    out_specs = (P("dp", FEAT), P(FEAT, None), P(FEAT, None))
    return jax.shard_map(body, mesh=mesh, in_specs=in_specs, out_specs=out_specs, check_vma=False)
```

```python
import functools

import jax
import jax.numpy as jnp
from jax import lax
from jax.experimental import pallas as pl
from jax.experimental.pallas import tpu as pltpu
from jax.sharding import Mesh
from jax.sharding import PartitionSpec as P

BF = jnp.bfloat16
F32 = jnp.float32
NT = (((1,), (1,)), ((), ()))
TN = (((0,), (0,)), ((), ()))
ROWS = 64
GROUP = 4
FEAT = ("blk", "mem")
VMEM_LIMIT = 48 * 1024 * 1024


def call(kernel, out_shape, n_in, scratch=(), smem=(), late=(), flops=0, nbytes=0):
    spaces = {i: pltpu.SMEM for i in smem} | {i: pl.ANY for i in late}
    in_specs = [pl.BlockSpec(memory_space=spaces.get(i, pltpu.VMEM)) for i in range(n_in)]
    out_specs = jax.tree.map(lambda _: pl.BlockSpec(memory_space=pltpu.VMEM), out_shape)
    return pl.pallas_call(
        kernel,
        out_shape=out_shape,
        in_specs=in_specs,
        out_specs=out_specs,
        scratch_shapes=list(scratch),
        compiler_params=pltpu.CompilerParams(vmem_limit_bytes=VMEM_LIMIT),
        cost_estimate=pl.CostEstimate(flops=flops, bytes_accessed=nbytes, transcendentals=0),
    )


def pack_kernel(groups, tgt_rows, feats_ref, dst_ref, send_ref, masked):
    cols, edges = feats_ref.shape
    cap = send_ref.shape[2]
    dst = jnp.concatenate([dst_ref[i : i + 1, :] for i in range(dst_ref.shape[0])], axis=1)
    owner = dst // tgt_rows
    local = dst - owner * tgt_rows
    half = tgt_rows // 2
    code = jnp.where(local < half, local - half, local - (half - 1)).astype(F32)
    owner_hot = lax.broadcasted_iota(jnp.int32, (groups, edges), 0) == owner
    owner_hot = owner_hot.astype(F32)
    step = 256
    before = (
        lax.broadcasted_iota(jnp.int32, (step, step), 0)
        < lax.broadcasted_iota(jnp.int32, (step, step), 1)
    ).astype(BF)
    seen = jnp.zeros((groups, 1), F32)
    ranks = []
    for i in range(edges // step):
        part = owner_hot[:, i * step : (i + 1) * step]
        prior = jnp.dot(part.astype(BF), before, preferred_element_type=F32) + seen
        ranks.append(jnp.sum(prior * part, axis=0, keepdims=True))
        seen = seen + jnp.sum(part, axis=1, keepdims=True)
    rank = jnp.concatenate(ranks, axis=1).astype(jnp.int32)
    rank_hot = (lax.broadcasted_iota(jnp.int32, (cap, edges), 0) == rank).astype(F32).astype(BF)
    extra_row = lax.broadcasted_iota(jnp.int32, (ROWS - cols, edges), 0)
    extra = jnp.where(extra_row == 0, code, jnp.where(extra_row == 1, 1.0, 0.0)).astype(BF)
    hot = owner_hot.astype(BF)
    some = masked.shape[0] // ROWS
    for g in range(groups // some):
        for j in range(some):
            o = g * some + j
            live = hot[o : o + 1, :]
            masked[j * ROWS : j * ROWS + cols, :] = feats_ref[...] * live
            masked[j * ROWS + cols : (j + 1) * ROWS, :] = extra * live
        out = lax.dot_general(masked[...], rank_hot, NT, preferred_element_type=F32).astype(BF)
        for j in range(some):
            send_ref[g * some + j] = out[j * ROWS : (j + 1) * ROWS, :]


def far_place(block, column):
    return (block + column) % GROUP


def column_sets(weight, group):
    half = 64
    n = weight.shape[1] // half
    sets = []
    for h in range(group):
        at = [group * i + far_place(i, h) for i in range(n // group)]
        sets.append(jnp.concatenate([weight[:, b * half : (b + 1) * half] for b in at], axis=1))
    return sets


def first_pieces_kernel(block_ref, neigh_ref, own_ref, self_ref, late_ref, out_ref):
    del late_ref
    rows = neigh_ref.shape[0]
    group, _, width = out_ref.shape
    both = zip(column_sets(neigh_ref[...], group), column_sets(own_ref[...], group))
    for h, (neigh, own) in enumerate(both):
        to = far_place(block_ref[0], h)
        out_ref[to, :rows, : width // 2] = neigh
        out_ref[to, :rows, width // 2 :] = own
        out_ref[to, rows:, :] = self_ref[...]


def second_pieces_kernel(block_ref, neigh_ref, own_ref, late_ref, out_ref):
    del late_ref
    group, _, width = out_ref.shape
    both = zip(column_sets(neigh_ref[...], group), column_sets(own_ref[...], group))
    for h, (neigh, own) in enumerate(both):
        to = far_place(block_ref[0], h)
        out_ref[to, :, : width // 2] = neigh
        out_ref[to, :, width // 2 :] = own


def mean_kernel(cols, recv_ref, pieces_ref, out_ref):
    groups, rows, cap = recv_ref.shape
    targets = out_ref.shape[2]
    half = targets // 2
    vertex = lax.broadcasted_iota(jnp.int32, (targets, 1), 0)
    vertex = jnp.where(vertex < half, vertex - half, vertex - (half - 1)).astype(F32)
    acc = jnp.zeros((rows, targets), F32)
    some = 8
    for g in range(groups // some):
        part = jnp.concatenate([recv_ref[g * some + j] for j in range(some)], axis=1)
        code = part[cols : cols + 1, :].astype(F32)
        hot = (vertex == code).astype(F32).astype(BF)
        acc = acc + lax.dot_general(part, hot, NT, preferred_element_type=F32)
    degree = jnp.maximum(acc[cols + 1 : cols + 2, :], 1.0)
    mean = (acc[:cols, :] / degree).astype(BF)
    for j in range(out_ref.shape[0]):
        out_ref[j, :cols, :] = mean
        out_ref[j, cols:, :] = pieces_ref[j]


def first_kernel(got_ref, out_ref, weight, acts):
    group, rows, targets = got_ref.shape
    rows = rows // 3
    width = targets // 2
    for j in range(group):
        low, mid, high = 2 * rows * j, 2 * rows * j + rows, 2 * rows * (j + 1)
        acts[low:mid, :] = got_ref[j, :rows, :]
        weight[low:mid, :] = got_ref[j, rows : 2 * rows, :width]
        weight[mid:high, :] = got_ref[j, rows : 2 * rows, width:]
        acts[mid:high, :] = got_ref[j, 2 * rows :, :]
    total = lax.dot_general(weight[...], acts[...], TN, preferred_element_type=F32)
    cols = out_ref.shape[1]
    for z in range(out_ref.shape[0]):
        out_ref[z] = total[z * cols : (z + 1) * cols, :].astype(BF)


def hidden_kernel(parts_ref, bias_ref, pieces_ref, out_ref):
    cols = bias_ref.shape[0]
    total = parts_ref[0].astype(F32)
    for k in range(1, parts_ref.shape[0]):
        total = total + parts_ref[k].astype(F32)
    hidden = jnp.maximum(total + bias_ref[...], 0.0).astype(BF)
    for c in range(out_ref.shape[0]):
        out_ref[c, :cols, :] = hidden
        out_ref[c, cols:, :] = pieces_ref[c]


def grad_kernel(
    index_ref, got_ref, values_ref, live_ref, cot_ref, agg_ref, out_ref, left, source, acc
):
    group, cols, targets = got_ref.shape
    cols = cols // 2
    width = values_ref.shape[1]
    wide = group * cols
    for t in range(targets // width):
        for j in range(group):
            at = slice(j * cols, (j + 1) * cols)
            source[t, at, :] = got_ref[j, :cols, t * width : (t + 1) * width]
    acc[...] = jnp.zeros_like(acc)
    for k in range(values_ref.shape[0]):
        target = index_ref[k, 0]
        acc[target] += lax.dot_general(
            source[index_ref[k, 1]], values_ref[k], NT, preferred_element_type=F32
        )
    live = live_ref[...].astype(BF)
    for t in range(targets // width):
        at = slice(t * width, (t + 1) * width)
        tile = acc[t].astype(BF)
        agg_ref[:, at] = tile
        left[:wide, at] = tile * live[:, at]
        left[wide:, at] = source[t] * live[:, at]
    block = lax.dot_general(left[...], cot_ref[...], NT, preferred_element_type=F32)
    at = 0
    for w in range(2):
        for r in range(0, cols, 8):
            for c in range(0, cot_ref.shape[0], 128):
                rows_of = [
                    block[w * wide + j * cols + r : w * wide + j * cols + r + 8, c : c + 128]
                    for j in range(group)
                ]
                out_ref[at] = jnp.concatenate(rows_of, axis=0).astype(BF)
                at += 1


def second_kernel(block_ref, agg_ref, got_ref, out_ref, weight, acts):
    group, rows, targets = got_ref.shape
    rows = rows // 2
    width = targets // 2
    for j in range(group):
        low, mid, high = 2 * rows * j, 2 * rows * j + rows, 2 * rows * (j + 1)
        weight[low:mid, :] = got_ref[j, rows:, :width]
        acts[low:mid, :] = agg_ref[j * rows : (j + 1) * rows, :]
        weight[mid:high, :] = got_ref[j, rows:, width:]
        acts[mid:high, :] = got_ref[j, :rows, :]
    total = lax.dot_general(weight[...], acts[...], TN, preferred_element_type=F32)
    n, cols, _ = out_ref.shape
    for z in range(n):
        out_ref[jnp.bitwise_xor(block_ref[0], z)] = total[z * cols : (z + 1) * cols, :].astype(BF)


def copies_kernel(terms_ref, late1_ref, late2_ref, out_ref):
    del late1_ref, late2_ref
    total = terms_ref[0].astype(F32)
    for d in range(1, terms_ref.shape[0]):
        total = total + terms_ref[d].astype(F32)
    for d in range(out_ref.shape[0]):
        out_ref[d] = total


def place_kernel(block_ref, pieces_ref, neigh_ref, self_ref):
    half = 64
    starts = []
    for h in range(GROUP):
        starts.append(pl.multiple_of(far_place(block_ref[0], h) * 8, 8))
    at = 0
    for out_ref in (neigh_ref, self_ref):
        for r in range(0, out_ref.shape[0], 8):
            for c in range(2):
                parts = [pieces_ref[at, pl.ds(start, 8), :] for start in starts]
                for e in range(2):
                    block = 2 * c + e
                    for p in range(0, GROUP, 2):
                        pair = [
                            parts[(p + i - block) % GROUP][:, e * half : (e + 1) * half]
                            for i in range(2)
                        ]
                        to = (GROUP * block + p) * half
                        out_ref[r : r + 8, to : to + 2 * half] = jnp.concatenate(pair, axis=1)
                at += 1


def out_kernel(p0_ref, p1_ref, p2_ref, p3_ref, bias_ref, live_ref, out_ref):
    total = p0_ref[...].astype(F32) + p1_ref[...].astype(F32)
    total = total + (p2_ref[...].astype(F32) + p3_ref[...].astype(F32))
    out_ref[...] = ((total + bias_ref[...]) * live_ref[...]).astype(BF)


def body(
    edge_feats,
    edge_dst,
    self_feats,
    neigh_one,
    self_one,
    bias_one,
    tile_index,
    tile_values,
    seed_live,
    neigh_two,
    self_two,
    bias_two,
    cotangent,
):
    groups = lax.axis_size("dp")
    blocks = lax.axis_size("blk")
    edges, cols = edge_feats.shape
    targets = self_feats.shape[0]
    hid = bias_one.shape[0]
    full = neigh_one.shape[1]
    cap = 2 * edges // groups
    wide = full // GROUP
    far = [[GROUP * i + far_place(i, h) for i in range(blocks)] for h in range(GROUP)]
    block = lax.axis_index("blk").reshape(1)
    live = seed_live.reshape(1, targets).astype(F32)

    def swap(x, axis, among=None):
        return lax.all_to_all(
            x, axis, split_axis=0, concat_axis=0, tiled=True, axis_index_groups=among
        )

    def trade_far(x, k):
        pairs = [(group[i], group[i ^ k]) for group in far for i in range(blocks)]
        return lax.ppermute(x, FEAT, pairs)

    def shape(*dims, dtype=BF):
        return jax.ShapeDtypeStruct(dims, dtype)

    with jax.named_scope("edges"):
        send = call(
            functools.partial(pack_kernel, groups, targets),
            shape(groups, ROWS, cap),
            2,
            scratch=[pltpu.VMEM((8 * ROWS, edges), BF)],
            flops=2 * groups * ROWS * edges * cap,
            nbytes=8 << 20,
        )(edge_feats.T, edge_dst.reshape(-1, 128))
        recv = swap(send, "dp")
    with jax.named_scope("pieces"):
        pieces = call(
            first_pieces_kernel,
            shape(GROUP, 2 * cols, targets),
            5,
            smem=(0,),
            late=(4,),
            nbytes=2 << 20,
        )(block, neigh_one, self_one, self_feats.T, send)
    with jax.named_scope("mean"):
        acts = call(
            functools.partial(mean_kernel, cols),
            shape(GROUP, 3 * cols, targets),
            2,
            flops=2 * groups * ROWS * cap * targets,
            nbytes=8 << 20,
        )(recv, pieces)
        acts = swap(acts, "mem")
    with jax.named_scope("first"):
        first = call(
            first_kernel,
            shape(blocks, hid, targets),
            1,
            scratch=[pltpu.VMEM((8 * cols, wide), BF), pltpu.VMEM((8 * cols, targets), BF)],
            flops=2 * 8 * cols * wide * targets,
            nbytes=2 << 20,
        )(acts)
        parts = swap(first, FEAT, far)
    with jax.named_scope("pieces"):
        pieces = call(
            second_pieces_kernel,
            shape(GROUP, hid, targets),
            4,
            smem=(0,),
            late=(3,),
            nbytes=1 << 20,
        )(block, neigh_two, self_two, first)
    with jax.named_scope("hidden"):
        hidden = call(hidden_kernel, shape(GROUP, 2 * hid, targets), 3, nbytes=1 << 20)(
            parts, bias_one.reshape(hid, 1), pieces
        )
        hidden = swap(hidden, "mem")
    with jax.named_scope("cotangent"):
        cot = lax.all_gather(cotangent.T, FEAT, axis=0, tiled=True, axis_index_groups=far)
    with jax.named_scope("grads"):
        agg, terms = call(
            grad_kernel,
            (shape(wide, targets), shape(groups, GROUP * 8, 128)),
            5,
            scratch=[
                pltpu.VMEM((2 * wide, targets), BF),
                pltpu.VMEM((targets // 128, wide, 128), BF),
                pltpu.VMEM((targets // 128, wide, 128), F32),
            ],
            smem=(0,),
            flops=2 * 2 * wide * targets * wide,
            nbytes=4 << 20,
        )(tile_index, hidden, tile_values, live, cot)
        terms = swap(terms.reshape(GROUP * groups, 8, 128), ("dp", "mem"))
    with jax.named_scope("second"):
        second = call(
            second_kernel,
            shape(blocks, hid, targets),
            3,
            scratch=[pltpu.VMEM((2 * wide, wide), BF), pltpu.VMEM((2 * wide, targets), BF)],
            smem=(0,),
            flops=2 * 2 * wide * wide * targets,
            nbytes=2 << 20,
        )(block, agg, hidden)
        sums = [second[0]] + [trade_far(second[k], k) for k in range(1, blocks)]
        second_out = call(out_kernel, shape(hid, targets), 6, nbytes=1 << 20)(
            *sums, bias_two.reshape(hid, 1), live
        ).T
    with jax.named_scope("place"):
        spread = call(
            copies_kernel,
            shape(groups, GROUP * 8, 128, dtype=F32),
            3,
            late=(1, 2),
            nbytes=1 << 20,
        )(terms.reshape(groups, GROUP * 8, 128), second, sums[1])
        spread = swap(spread, "dp")
        grad_neigh, grad_self = call(
            place_kernel,
            (shape(hid, full, dtype=F32), shape(hid, full, dtype=F32)),
            2,
            smem=(0,),
            nbytes=1 << 20,
        )(block, spread)
    return (second_out, grad_neigh, grad_self)


def solution(mesh):
    shards = mesh.devices.shape
    blocks = mesh.devices.reshape(shards[0], shards[1] // GROUP, GROUP)
    mesh = Mesh(blocks, ("dp",) + FEAT)
    in_specs = (
        P("dp", FEAT),
        P("dp"),
        P("dp", FEAT),
        P(FEAT, None),
        P(FEAT, None),
        P(FEAT),
        P("dp", None),
        P("dp", None, None),
        P("dp"),
        P(FEAT, None),
        P(FEAT, None),
        P(FEAT),
        P("dp", FEAT),
    )
    out_specs = (P("dp", FEAT), P(FEAT, None), P(FEAT, None))
    return jax.shard_map(body, mesh=mesh, in_specs=in_specs, out_specs=out_specs, check_vma=False)
```

```python
import functools

import jax
import jax.numpy as jnp
from jax import lax
from jax.experimental import pallas as pl
from jax.experimental.pallas import tpu as pltpu
from jax.sharding import Mesh
from jax.sharding import PartitionSpec as P

BF = jnp.bfloat16
F32 = jnp.float32
NT = (((1,), (1,)), ((), ()))
TN = (((0,), (0,)), ((), ()))
ROWS = 64
GROUP = 4
FEAT = ("blk", "mem")
VMEM_LIMIT = 48 * 1024 * 1024


def call(kernel, out_shape, n_in, scratch=(), smem=(), late=(), flops=0, nbytes=0):
    spaces = {i: pltpu.SMEM for i in smem} | {i: pl.ANY for i in late}
    in_specs = [pl.BlockSpec(memory_space=spaces.get(i, pltpu.VMEM)) for i in range(n_in)]
    out_specs = jax.tree.map(lambda _: pl.BlockSpec(memory_space=pltpu.VMEM), out_shape)
    return pl.pallas_call(
        kernel,
        out_shape=out_shape,
        in_specs=in_specs,
        out_specs=out_specs,
        scratch_shapes=list(scratch),
        compiler_params=pltpu.CompilerParams(vmem_limit_bytes=VMEM_LIMIT),
        cost_estimate=pl.CostEstimate(flops=flops, bytes_accessed=nbytes, transcendentals=0),
    )


def pack_kernel(groups, tgt_rows, feats_ref, dst_ref, send_ref, masked):
    cols, edges = feats_ref.shape
    cap = send_ref.shape[2]
    dst = jnp.concatenate([dst_ref[i : i + 1, :] for i in range(dst_ref.shape[0])], axis=1)
    owner = dst // tgt_rows
    local = dst - owner * tgt_rows
    half = tgt_rows // 2
    code = jnp.where(local < half, local - half, local - (half - 1)).astype(F32)
    owner_hot = lax.broadcasted_iota(jnp.int32, (groups, edges), 0) == owner
    owner_hot = owner_hot.astype(F32)
    step = 256
    before = (
        lax.broadcasted_iota(jnp.int32, (step, step), 0)
        < lax.broadcasted_iota(jnp.int32, (step, step), 1)
    ).astype(BF)
    seen = jnp.zeros((groups, 1), F32)
    ranks = []
    for i in range(edges // step):
        part = owner_hot[:, i * step : (i + 1) * step]
        prior = jnp.dot(part.astype(BF), before, preferred_element_type=F32) + seen
        ranks.append(jnp.sum(prior * part, axis=0, keepdims=True))
        seen = seen + jnp.sum(part, axis=1, keepdims=True)
    rank = jnp.concatenate(ranks, axis=1).astype(jnp.int32)
    rank_hot = (lax.broadcasted_iota(jnp.int32, (cap, edges), 0) == rank).astype(F32).astype(BF)
    extra_row = lax.broadcasted_iota(jnp.int32, (ROWS - cols, edges), 0)
    extra = jnp.where(extra_row == 0, code, jnp.where(extra_row == 1, 1.0, 0.0)).astype(BF)
    hot = owner_hot.astype(BF)
    some = masked.shape[0] // ROWS
    for g in range(groups // some):
        for j in range(some):
            o = g * some + j
            live = hot[o : o + 1, :]
            masked[j * ROWS : j * ROWS + cols, :] = feats_ref[...] * live
            masked[j * ROWS + cols : (j + 1) * ROWS, :] = extra * live
        out = lax.dot_general(masked[...], rank_hot, NT, preferred_element_type=F32).astype(BF)
        for j in range(some):
            send_ref[g * some + j] = out[j * ROWS : (j + 1) * ROWS, :]


def far_place(block, column):
    return (block + column) % GROUP


def column_sets(weight, group):
    half = 64
    n = weight.shape[1] // half
    sets = []
    for h in range(group):
        at = [group * i + far_place(i, h) for i in range(n // group)]
        sets.append(jnp.concatenate([weight[:, b * half : (b + 1) * half] for b in at], axis=1))
    return sets


def first_pieces_kernel(
    block_ref, neigh_ref, own_ref, self_ref, cot_ref, late_ref, out_ref, cot_out_ref
):
    del late_ref
    rows = neigh_ref.shape[0]
    group, _, width = out_ref.shape
    both = zip(column_sets(neigh_ref[...], group), column_sets(own_ref[...], group))
    for h, (neigh, own) in enumerate(both):
        to = far_place(block_ref[0], h)
        out_ref[to, :rows, : width // 2] = neigh
        out_ref[to, :rows, width // 2 :] = own
        out_ref[to, rows:, :] = self_ref[...]
    cot_out_ref[...] = cot_ref[...]


def second_pieces_kernel(block_ref, neigh_ref, own_ref, late_ref, out_ref):
    del late_ref
    group, _, width = out_ref.shape
    both = zip(column_sets(neigh_ref[...], group), column_sets(own_ref[...], group))
    for h, (neigh, own) in enumerate(both):
        to = far_place(block_ref[0], h)
        out_ref[to, :, : width // 2] = neigh
        out_ref[to, :, width // 2 :] = own


def mean_kernel(cols, recv_ref, pieces_ref, late_ref, out_ref):
    del late_ref
    groups, rows, cap = recv_ref.shape
    targets = out_ref.shape[2]
    half = targets // 2
    vertex = lax.broadcasted_iota(jnp.int32, (targets, 1), 0)
    vertex = jnp.where(vertex < half, vertex - half, vertex - (half - 1)).astype(F32)
    acc = jnp.zeros((rows, targets), F32)
    some = 8
    for g in range(groups // some):
        part = jnp.concatenate([recv_ref[g * some + j] for j in range(some)], axis=1)
        code = part[cols : cols + 1, :].astype(F32)
        hot = (vertex == code).astype(F32).astype(BF)
        acc = acc + lax.dot_general(part, hot, NT, preferred_element_type=F32)
    degree = jnp.maximum(acc[cols + 1 : cols + 2, :], 1.0)
    mean = (acc[:cols, :] / degree).astype(BF)
    for j in range(out_ref.shape[0]):
        out_ref[j, :cols, :] = mean
        out_ref[j, cols:, :] = pieces_ref[j]


def first_kernel(got_ref, out_ref, weight, acts):
    group, rows, targets = got_ref.shape
    rows = rows // 3
    width = targets // 2
    for j in range(group):
        low, mid, high = 2 * rows * j, 2 * rows * j + rows, 2 * rows * (j + 1)
        acts[low:mid, :] = got_ref[j, :rows, :]
        weight[low:mid, :] = got_ref[j, rows : 2 * rows, :width]
        weight[mid:high, :] = got_ref[j, rows : 2 * rows, width:]
        acts[mid:high, :] = got_ref[j, 2 * rows :, :]
    total = lax.dot_general(weight[...], acts[...], TN, preferred_element_type=F32)
    cols = out_ref.shape[1]
    for z in range(out_ref.shape[0]):
        out_ref[z] = total[z * cols : (z + 1) * cols, :].astype(BF)


def hidden_kernel(parts_ref, bias_ref, pieces_ref, out_ref):
    cols = bias_ref.shape[0]
    total = parts_ref[0].astype(F32)
    for k in range(1, parts_ref.shape[0]):
        total = total + parts_ref[k].astype(F32)
    hidden = jnp.maximum(total + bias_ref[...], 0.0).astype(BF)
    for c in range(out_ref.shape[0]):
        out_ref[c, :cols, :] = hidden
        out_ref[c, cols:, :] = pieces_ref[c]


def grad_kernel(
    index_ref, got_ref, values_ref, live_ref, cot_ref, agg_ref, out_ref, left, source, acc
):
    group, cols, targets = got_ref.shape
    cols = cols // 2
    width = values_ref.shape[1]
    wide = group * cols
    for t in range(targets // width):
        for j in range(group):
            at = slice(j * cols, (j + 1) * cols)
            source[t, at, :] = got_ref[j, :cols, t * width : (t + 1) * width]
    acc[...] = jnp.zeros_like(acc)
    for k in range(values_ref.shape[0]):
        target = index_ref[k, 0]
        acc[target] += lax.dot_general(
            source[index_ref[k, 1]], values_ref[k], NT, preferred_element_type=F32
        )
    live = live_ref[...].astype(BF)
    for t in range(targets // width):
        at = slice(t * width, (t + 1) * width)
        tile = acc[t].astype(BF)
        agg_ref[:, at] = tile
        left[:wide, at] = tile * live[:, at]
        left[wide:, at] = source[t] * live[:, at]
    block = lax.dot_general(left[...], cot_ref[...], NT, preferred_element_type=F32)
    at = 0
    for w in range(2):
        for r in range(0, cols, 8):
            for c in range(0, cot_ref.shape[0], 128):
                rows_of = [
                    block[w * wide + j * cols + r : w * wide + j * cols + r + 8, c : c + 128]
                    for j in range(group)
                ]
                out_ref[at] = jnp.concatenate(rows_of, axis=0).astype(BF)
                at += 1


def second_kernel(block_ref, agg_ref, got_ref, out_ref, weight, acts):
    group, rows, targets = got_ref.shape
    rows = rows // 2
    width = targets // 2
    for j in range(group):
        low, mid, high = 2 * rows * j, 2 * rows * j + rows, 2 * rows * (j + 1)
        weight[low:mid, :] = got_ref[j, rows:, :width]
        acts[low:mid, :] = agg_ref[j * rows : (j + 1) * rows, :]
        weight[mid:high, :] = got_ref[j, rows:, width:]
        acts[mid:high, :] = got_ref[j, :rows, :]
    total = lax.dot_general(weight[...], acts[...], TN, preferred_element_type=F32)
    n, cols, _ = out_ref.shape
    for z in range(n):
        out_ref[jnp.bitwise_xor(block_ref[0], z)] = total[z * cols : (z + 1) * cols, :].astype(BF)


def copies_kernel(terms_ref, late1_ref, late2_ref, late3_ref, out_ref):
    del late1_ref, late2_ref, late3_ref
    total = terms_ref[0].astype(F32)
    for d in range(1, terms_ref.shape[0]):
        total = total + terms_ref[d].astype(F32)
    for d in range(out_ref.shape[0]):
        out_ref[d] = total


def place_kernel(block_ref, pieces_ref, neigh_ref, self_ref):
    half = 64
    starts = []
    for h in range(GROUP):
        starts.append(pl.multiple_of(far_place(block_ref[0], h) * 8, 8))
    at = 0
    for out_ref in (neigh_ref, self_ref):
        for r in range(0, out_ref.shape[0], 8):
            for c in range(2):
                parts = [pieces_ref[at, pl.ds(start, 8), :] for start in starts]
                for e in range(2):
                    block = 2 * c + e
                    for p in range(0, GROUP, 2):
                        pair = [
                            parts[(p + i - block) % GROUP][:, e * half : (e + 1) * half]
                            for i in range(2)
                        ]
                        to = (GROUP * block + p) * half
                        out_ref[r : r + 8, to : to + 2 * half] = jnp.concatenate(pair, axis=1)
                at += 1


def out_kernel(p0_ref, p1_ref, p2_ref, p3_ref, bias_ref, live_ref, out_ref):
    total = p0_ref[...].astype(F32) + p1_ref[...].astype(F32)
    total = total + (p2_ref[...].astype(F32) + p3_ref[...].astype(F32))
    out_ref[...] = ((total + bias_ref[...]) * live_ref[...]).astype(BF)


def body(
    edge_feats,
    edge_dst,
    self_feats,
    neigh_one,
    self_one,
    bias_one,
    tile_index,
    tile_values,
    seed_live,
    neigh_two,
    self_two,
    bias_two,
    cotangent,
):
    groups = lax.axis_size("dp")
    blocks = lax.axis_size("blk")
    edges, cols = edge_feats.shape
    targets = self_feats.shape[0]
    hid = bias_one.shape[0]
    full = neigh_one.shape[1]
    cap = 2 * edges // groups
    wide = full // GROUP
    far = [[GROUP * i + far_place(i, h) for i in range(blocks)] for h in range(GROUP)]
    block = lax.axis_index("blk").reshape(1)
    live = seed_live.reshape(1, targets).astype(F32)

    def swap(x, axis, among=None):
        return lax.all_to_all(
            x, axis, split_axis=0, concat_axis=0, tiled=True, axis_index_groups=among
        )

    def trade_far(x, k):
        pairs = [(group[i], group[i ^ k]) for group in far for i in range(blocks)]
        return lax.ppermute(x, FEAT, pairs)

    def shape(*dims, dtype=BF):
        return jax.ShapeDtypeStruct(dims, dtype)

    with jax.named_scope("edges"):
        send = call(
            functools.partial(pack_kernel, groups, targets),
            shape(groups, ROWS, cap),
            2,
            scratch=[pltpu.VMEM((8 * ROWS, edges), BF)],
            flops=2 * groups * ROWS * edges * cap,
            nbytes=8 << 20,
        )(edge_feats.T, edge_dst.reshape(-1, 128))
        recv = swap(send, "dp")
    with jax.named_scope("pieces"):
        pieces, cot = call(
            first_pieces_kernel,
            (shape(GROUP, 2 * cols, targets), shape(hid, targets)),
            6,
            smem=(0,),
            late=(5,),
            nbytes=2 << 20,
        )(block, neigh_one, self_one, self_feats.T, cotangent.T, send)
        cot = lax.all_gather(cot, FEAT, axis=0, tiled=True, axis_index_groups=far)
    with jax.named_scope("mean"):
        acts = call(
            functools.partial(mean_kernel, cols),
            shape(GROUP, 3 * cols, targets),
            3,
            late=(2,),
            flops=2 * groups * ROWS * cap * targets,
            nbytes=8 << 20,
        )(recv, pieces, cot)
        acts = swap(acts, "mem")
    with jax.named_scope("first"):
        first = call(
            first_kernel,
            shape(blocks, hid, targets),
            1,
            scratch=[pltpu.VMEM((8 * cols, wide), BF), pltpu.VMEM((8 * cols, targets), BF)],
            flops=2 * 8 * cols * wide * targets,
            nbytes=2 << 20,
        )(acts)
        parts = swap(first, FEAT, far)
    with jax.named_scope("pieces"):
        pieces = call(
            second_pieces_kernel,
            shape(GROUP, hid, targets),
            4,
            smem=(0,),
            late=(3,),
            nbytes=1 << 20,
        )(block, neigh_two, self_two, first)
    with jax.named_scope("hidden"):
        hidden = call(hidden_kernel, shape(GROUP, 2 * hid, targets), 3, nbytes=1 << 20)(
            parts, bias_one.reshape(hid, 1), pieces
        )
        hidden = swap(hidden, "mem")
    with jax.named_scope("grads"):
        agg, terms = call(
            grad_kernel,
            (shape(wide, targets), shape(groups, GROUP * 8, 128)),
            5,
            scratch=[
                pltpu.VMEM((2 * wide, targets), BF),
                pltpu.VMEM((targets // 128, wide, 128), BF),
                pltpu.VMEM((targets // 128, wide, 128), F32),
            ],
            smem=(0,),
            flops=2 * 2 * wide * targets * wide,
            nbytes=4 << 20,
        )(tile_index, hidden, tile_values, live, cot)
        terms = swap(terms.reshape(GROUP * groups, 8, 128), ("dp", "mem"))
    with jax.named_scope("second"):
        second = call(
            second_kernel,
            shape(blocks, hid, targets),
            3,
            scratch=[pltpu.VMEM((2 * wide, wide), BF), pltpu.VMEM((2 * wide, targets), BF)],
            smem=(0,),
            flops=2 * 2 * wide * wide * targets,
            nbytes=2 << 20,
        )(block, agg, hidden)
        sums = [second[0]] + [trade_far(second[k], k) for k in range(1, blocks)]
        second_out = call(out_kernel, shape(hid, targets), 6, nbytes=1 << 20)(
            *sums, bias_two.reshape(hid, 1), live
        ).T
    with jax.named_scope("place"):
        spread = call(
            copies_kernel,
            shape(groups, GROUP * 8, 128, dtype=F32),
            4,
            late=(1, 2, 3),
            nbytes=1 << 20,
        )(terms.reshape(groups, GROUP * 8, 128), second, sums[1], sums[2])
        spread = swap(spread, "dp")
        grad_neigh, grad_self = call(
            place_kernel,
            (shape(hid, full, dtype=F32), shape(hid, full, dtype=F32)),
            2,
            smem=(0,),
            nbytes=1 << 20,
        )(block, spread)
    return (second_out, grad_neigh, grad_self)


def solution(mesh):
    shards = mesh.devices.shape
    blocks = mesh.devices.reshape(shards[0], shards[1] // GROUP, GROUP)
    mesh = Mesh(blocks, ("dp",) + FEAT)
    in_specs = (
        P("dp", FEAT),
        P("dp"),
        P("dp", FEAT),
        P(FEAT, None),
        P(FEAT, None),
        P(FEAT),
        P("dp", None),
        P("dp", None, None),
        P("dp"),
        P(FEAT, None),
        P(FEAT, None),
        P(FEAT),
        P("dp", FEAT),
    )
    out_specs = (P("dp", FEAT), P(FEAT, None), P(FEAT, None))
    return jax.shard_map(body, mesh=mesh, in_specs=in_specs, out_specs=out_specs, check_vma=False)
```

```python
import functools

import jax
import jax.numpy as jnp
from jax import lax
from jax.experimental import pallas as pl
from jax.experimental.pallas import tpu as pltpu
from jax.sharding import Mesh
from jax.sharding import PartitionSpec as P

BF = jnp.bfloat16
F32 = jnp.float32
NT = (((1,), (1,)), ((), ()))
TN = (((0,), (0,)), ((), ()))
ROWS = 64
GROUP = 4
FEAT = ("blk", "mem")
VMEM_LIMIT = 48 * 1024 * 1024


def call(kernel, out_shape, n_in, scratch=(), smem=(), late=(), flops=0, nbytes=0):
    spaces = {i: pltpu.SMEM for i in smem} | {i: pl.ANY for i in late}
    in_specs = [pl.BlockSpec(memory_space=spaces.get(i, pltpu.VMEM)) for i in range(n_in)]
    out_specs = jax.tree.map(lambda _: pl.BlockSpec(memory_space=pltpu.VMEM), out_shape)
    return pl.pallas_call(
        kernel,
        out_shape=out_shape,
        in_specs=in_specs,
        out_specs=out_specs,
        scratch_shapes=list(scratch),
        compiler_params=pltpu.CompilerParams(vmem_limit_bytes=VMEM_LIMIT),
        cost_estimate=pl.CostEstimate(flops=flops, bytes_accessed=nbytes, transcendentals=0),
    )


def pack_kernel(groups, tgt_rows, feats_ref, dst_ref, send_ref, masked):
    cols, edges = feats_ref.shape
    cap = send_ref.shape[2]
    dst = jnp.concatenate([dst_ref[i : i + 1, :] for i in range(dst_ref.shape[0])], axis=1)
    owner = dst // tgt_rows
    local = dst - owner * tgt_rows
    half = tgt_rows // 2
    code = jnp.where(local < half, local - half, local - (half - 1)).astype(F32)
    owner_hot = lax.broadcasted_iota(jnp.int32, (groups, edges), 0) == owner
    owner_hot = owner_hot.astype(F32)
    step = 256
    before = (
        lax.broadcasted_iota(jnp.int32, (step, step), 0)
        < lax.broadcasted_iota(jnp.int32, (step, step), 1)
    ).astype(BF)
    seen = jnp.zeros((groups, 1), F32)
    ranks = []
    for i in range(edges // step):
        part = owner_hot[:, i * step : (i + 1) * step]
        prior = jnp.dot(part.astype(BF), before, preferred_element_type=F32) + seen
        ranks.append(jnp.sum(prior * part, axis=0, keepdims=True))
        seen = seen + jnp.sum(part, axis=1, keepdims=True)
    rank = jnp.concatenate(ranks, axis=1).astype(jnp.int32)
    rank_hot = (lax.broadcasted_iota(jnp.int32, (cap, edges), 0) == rank).astype(F32).astype(BF)
    extra_row = lax.broadcasted_iota(jnp.int32, (ROWS - cols, edges), 0)
    extra = jnp.where(extra_row == 0, code, jnp.where(extra_row == 1, 1.0, 0.0)).astype(BF)
    hot = owner_hot.astype(BF)
    some = masked.shape[0] // ROWS
    for g in range(groups // some):
        for j in range(some):
            o = g * some + j
            live = hot[o : o + 1, :]
            masked[j * ROWS : j * ROWS + cols, :] = feats_ref[...] * live
            masked[j * ROWS + cols : (j + 1) * ROWS, :] = extra * live
        out = lax.dot_general(masked[...], rank_hot, NT, preferred_element_type=F32).astype(BF)
        for j in range(some):
            send_ref[g * some + j] = out[j * ROWS : (j + 1) * ROWS, :]


def far_place(block, column):
    return (block + column) % GROUP


def column_sets(weight, group):
    half = 64
    n = weight.shape[1] // half
    sets = []
    for h in range(group):
        at = [group * i + far_place(i, h) for i in range(n // group)]
        sets.append(jnp.concatenate([weight[:, b * half : (b + 1) * half] for b in at], axis=1))
    return sets


def first_pieces_kernel(
    block_ref, neigh_ref, own_ref, self_ref, cot_ref, late_ref, out_ref, cot_out_ref
):
    del late_ref
    rows = neigh_ref.shape[0]
    group, _, width = out_ref.shape
    both = zip(column_sets(neigh_ref[...], group), column_sets(own_ref[...], group))
    for h, (neigh, own) in enumerate(both):
        to = far_place(block_ref[0], h)
        out_ref[to, :rows, : width // 2] = neigh
        out_ref[to, :rows, width // 2 :] = own
        out_ref[to, rows:, :] = self_ref[...]
    cot_out_ref[...] = cot_ref[...]


def second_pieces_kernel(block_ref, neigh_ref, own_ref, late_ref, out_ref):
    del late_ref
    group, _, width = out_ref.shape
    both = zip(column_sets(neigh_ref[...], group), column_sets(own_ref[...], group))
    for h, (neigh, own) in enumerate(both):
        to = far_place(block_ref[0], h)
        out_ref[to, :, : width // 2] = neigh
        out_ref[to, :, width // 2 :] = own


def mean_kernel(cols, recv_ref, pieces_ref, late_ref, out_ref):
    del late_ref
    groups, rows, cap = recv_ref.shape
    targets = out_ref.shape[2]
    half = targets // 2
    vertex = lax.broadcasted_iota(jnp.int32, (targets, 1), 0)
    vertex = jnp.where(vertex < half, vertex - half, vertex - (half - 1)).astype(F32)
    acc = jnp.zeros((rows, targets), F32)
    some = 8
    for g in range(groups // some):
        part = jnp.concatenate([recv_ref[g * some + j] for j in range(some)], axis=1)
        code = part[cols : cols + 1, :].astype(F32)
        hot = (vertex == code).astype(F32).astype(BF)
        acc = acc + lax.dot_general(part, hot, NT, preferred_element_type=F32)
    degree = jnp.maximum(acc[cols + 1 : cols + 2, :], 1.0)
    mean = (acc[:cols, :] / degree).astype(BF)
    for j in range(out_ref.shape[0]):
        out_ref[j, :cols, :] = mean
        out_ref[j, cols:, :] = pieces_ref[j]


def first_kernel(got_ref, out_ref, weight, acts):
    group, rows, targets = got_ref.shape
    rows = rows // 3
    width = targets // 2
    for j in range(group):
        low, mid, high = 2 * rows * j, 2 * rows * j + rows, 2 * rows * (j + 1)
        acts[low:mid, :] = got_ref[j, :rows, :]
        weight[low:mid, :] = got_ref[j, rows : 2 * rows, :width]
        weight[mid:high, :] = got_ref[j, rows : 2 * rows, width:]
        acts[mid:high, :] = got_ref[j, 2 * rows :, :]
    total = lax.dot_general(weight[...], acts[...], TN, preferred_element_type=F32)
    cols = out_ref.shape[1]
    for z in range(out_ref.shape[0]):
        out_ref[z] = total[z * cols : (z + 1) * cols, :].astype(BF)


def hidden_kernel(parts_ref, bias_ref, pieces_ref, out_ref):
    cols = bias_ref.shape[0]
    total = parts_ref[0].astype(F32)
    for k in range(1, parts_ref.shape[0]):
        total = total + parts_ref[k].astype(F32)
    hidden = jnp.maximum(total + bias_ref[...], 0.0).astype(BF)
    for c in range(out_ref.shape[0]):
        out_ref[c, :cols, :] = hidden
        out_ref[c, cols:, :] = pieces_ref[c]


def grad_kernel(
    index_ref, got_ref, values_ref, live_ref, cot_ref, agg_ref, out_ref, left, source, acc
):
    group, cols, targets = got_ref.shape
    cols = cols // 2
    width = values_ref.shape[1]
    wide = group * cols
    for t in range(targets // width):
        for j in range(group):
            at = slice(j * cols, (j + 1) * cols)
            source[t, at, :] = got_ref[j, :cols, t * width : (t + 1) * width]
    acc[...] = jnp.zeros_like(acc)
    for k in range(values_ref.shape[0]):
        target = index_ref[k, 0]
        acc[target] += lax.dot_general(
            source[index_ref[k, 1]], values_ref[k], NT, preferred_element_type=F32
        )
    live = live_ref[...].astype(BF)
    for t in range(targets // width):
        at = slice(t * width, (t + 1) * width)
        tile = acc[t].astype(BF)
        agg_ref[:, at] = tile
        left[:wide, at] = tile * live[:, at]
        left[wide:, at] = source[t] * live[:, at]
    block = lax.dot_general(left[...], cot_ref[...], NT, preferred_element_type=F32)
    at = 0
    for w in range(2):
        for r in range(0, cols, 8):
            for c in range(0, cot_ref.shape[0], 128):
                rows_of = [
                    block[w * wide + j * cols + r : w * wide + j * cols + r + 8, c : c + 128]
                    for j in range(group)
                ]
                out_ref[at] = jnp.concatenate(rows_of, axis=0).astype(BF)
                at += 1


def second_kernel(block_ref, agg_ref, got_ref, out_ref, weight, acts):
    group, rows, targets = got_ref.shape
    rows = rows // 2
    width = targets // 2
    for j in range(group):
        low, mid, high = 2 * rows * j, 2 * rows * j + rows, 2 * rows * (j + 1)
        weight[low:mid, :] = got_ref[j, rows:, :width]
        acts[low:mid, :] = agg_ref[j * rows : (j + 1) * rows, :]
        weight[mid:high, :] = got_ref[j, rows:, width:]
        acts[mid:high, :] = got_ref[j, :rows, :]
    total = lax.dot_general(weight[...], acts[...], TN, preferred_element_type=F32)
    n, cols, _ = out_ref.shape
    for z in range(n):
        out_ref[jnp.bitwise_xor(block_ref[0], z)] = total[z * cols : (z + 1) * cols, :].astype(BF)


def copies_kernel(terms_ref, late1_ref, late2_ref, late3_ref, late4_ref, out_ref):
    del late1_ref, late2_ref, late3_ref, late4_ref
    total = terms_ref[0].astype(F32)
    for d in range(1, terms_ref.shape[0]):
        total = total + terms_ref[d].astype(F32)
    total = total.astype(BF)
    for d in range(out_ref.shape[0]):
        out_ref[d] = total


def place_kernel(block_ref, pieces_ref, neigh_ref, self_ref, wide):
    half = 64
    wide[...] = pieces_ref[...].astype(F32)
    starts = []
    for h in range(GROUP):
        starts.append(pl.multiple_of(far_place(block_ref[0], h) * 8, 8))
    at = 0
    for out_ref in (neigh_ref, self_ref):
        for r in range(0, out_ref.shape[0], 8):
            for c in range(2):
                parts = [wide[at, pl.ds(start, 8), :] for start in starts]
                for e in range(2):
                    block = 2 * c + e
                    for p in range(0, GROUP, 2):
                        pair = [
                            parts[(p + i - block) % GROUP][:, e * half : (e + 1) * half]
                            for i in range(2)
                        ]
                        to = (GROUP * block + p) * half
                        out_ref[r : r + 8, to : to + 2 * half] = jnp.concatenate(pair, axis=1)
                at += 1


def out_kernel(p0_ref, p1_ref, p2_ref, p3_ref, bias_ref, live_ref, out_ref):
    total = p0_ref[...].astype(F32) + p1_ref[...].astype(F32)
    total = total + (p2_ref[...].astype(F32) + p3_ref[...].astype(F32))
    out_ref[...] = ((total + bias_ref[...]) * live_ref[...]).astype(BF)


def body(
    edge_feats,
    edge_dst,
    self_feats,
    neigh_one,
    self_one,
    bias_one,
    tile_index,
    tile_values,
    seed_live,
    neigh_two,
    self_two,
    bias_two,
    cotangent,
):
    groups = lax.axis_size("dp")
    blocks = lax.axis_size("blk")
    edges, cols = edge_feats.shape
    targets = self_feats.shape[0]
    hid = bias_one.shape[0]
    full = neigh_one.shape[1]
    cap = 2 * edges // groups
    wide = full // GROUP
    far = [[GROUP * i + far_place(i, h) for i in range(blocks)] for h in range(GROUP)]
    block = lax.axis_index("blk").reshape(1)
    live = seed_live.reshape(1, targets).astype(F32)

    def swap(x, axis, among=None):
        return lax.all_to_all(
            x, axis, split_axis=0, concat_axis=0, tiled=True, axis_index_groups=among
        )

    def trade_far(x, k):
        pairs = [(group[i], group[i ^ k]) for group in far for i in range(blocks)]
        return lax.ppermute(x, FEAT, pairs)

    def shape(*dims, dtype=BF):
        return jax.ShapeDtypeStruct(dims, dtype)

    with jax.named_scope("edges"):
        send = call(
            functools.partial(pack_kernel, groups, targets),
            shape(groups, ROWS, cap),
            2,
            scratch=[pltpu.VMEM((8 * ROWS, edges), BF)],
            flops=2 * groups * ROWS * edges * cap,
            nbytes=8 << 20,
        )(edge_feats.T, edge_dst.reshape(-1, 128))
        recv = swap(send, "dp")
    with jax.named_scope("pieces"):
        pieces, cot = call(
            first_pieces_kernel,
            (shape(GROUP, 2 * cols, targets), shape(hid, targets)),
            6,
            smem=(0,),
            late=(5,),
            nbytes=2 << 20,
        )(block, neigh_one, self_one, self_feats.T, cotangent.T, send)
        cot = lax.all_gather(cot, FEAT, axis=0, tiled=True, axis_index_groups=far)
    with jax.named_scope("mean"):
        acts = call(
            functools.partial(mean_kernel, cols),
            shape(GROUP, 3 * cols, targets),
            3,
            late=(2,),
            flops=2 * groups * ROWS * cap * targets,
            nbytes=8 << 20,
        )(recv, pieces, cot)
        acts = swap(acts, "mem")
    with jax.named_scope("first"):
        first = call(
            first_kernel,
            shape(blocks, hid, targets),
            1,
            scratch=[pltpu.VMEM((8 * cols, wide), BF), pltpu.VMEM((8 * cols, targets), BF)],
            flops=2 * 8 * cols * wide * targets,
            nbytes=2 << 20,
        )(acts)
        parts = swap(first, FEAT, far)
    with jax.named_scope("pieces"):
        pieces = call(
            second_pieces_kernel,
            shape(GROUP, hid, targets),
            4,
            smem=(0,),
            late=(3,),
            nbytes=1 << 20,
        )(block, neigh_two, self_two, first)
    with jax.named_scope("hidden"):
        hidden = call(hidden_kernel, shape(GROUP, 2 * hid, targets), 3, nbytes=1 << 20)(
            parts, bias_one.reshape(hid, 1), pieces
        )
        hidden = swap(hidden, "mem")
    with jax.named_scope("grads"):
        agg, terms = call(
            grad_kernel,
            (shape(wide, targets), shape(groups, GROUP * 8, 128)),
            5,
            scratch=[
                pltpu.VMEM((2 * wide, targets), BF),
                pltpu.VMEM((targets // 128, wide, 128), BF),
                pltpu.VMEM((targets // 128, wide, 128), F32),
            ],
            smem=(0,),
            flops=2 * 2 * wide * targets * wide,
            nbytes=4 << 20,
        )(tile_index, hidden, tile_values, live, cot)
        terms = swap(terms.reshape(GROUP * groups, 8, 128), ("dp", "mem"))
    with jax.named_scope("second"):
        second = call(
            second_kernel,
            shape(blocks, hid, targets),
            3,
            scratch=[pltpu.VMEM((2 * wide, wide), BF), pltpu.VMEM((2 * wide, targets), BF)],
            smem=(0,),
            flops=2 * 2 * wide * wide * targets,
            nbytes=2 << 20,
        )(block, agg, hidden)
        sums = [second[0]] + [trade_far(second[k], k) for k in range(1, blocks)]
        second_out = call(out_kernel, shape(hid, targets), 6, nbytes=1 << 20)(
            *sums, bias_two.reshape(hid, 1), live
        ).T
    with jax.named_scope("place"):
        spread = call(
            copies_kernel,
            shape(groups, GROUP * 8, 128),
            5,
            late=(1, 2, 3, 4),
            nbytes=1 << 20,
        )(terms.reshape(groups, GROUP * 8, 128), second, *sums[1:])
        spread = swap(spread, "dp")
        grad_neigh, grad_self = call(
            place_kernel,
            (shape(hid, full, dtype=F32), shape(hid, full, dtype=F32)),
            2,
            scratch=[pltpu.VMEM((groups, GROUP * 8, 128), F32)],
            smem=(0,),
            nbytes=1 << 20,
        )(block, spread)
    return (second_out, grad_neigh, grad_self)


def solution(mesh):
    shards = mesh.devices.shape
    blocks = mesh.devices.reshape(shards[0], shards[1] // GROUP, GROUP)
    mesh = Mesh(blocks, ("dp",) + FEAT)
    in_specs = (
        P("dp", FEAT),
        P("dp"),
        P("dp", FEAT),
        P(FEAT, None),
        P(FEAT, None),
        P(FEAT),
        P("dp", None),
        P("dp", None, None),
        P("dp"),
        P(FEAT, None),
        P(FEAT, None),
        P(FEAT),
        P("dp", FEAT),
    )
    out_specs = (P("dp", FEAT), P(FEAT, None), P(FEAT, None))
    return jax.shard_map(body, mesh=mesh, in_specs=in_specs, out_specs=out_specs, check_vma=False)
```

```python
import functools

import jax
import jax.numpy as jnp
from jax import lax
from jax.experimental import pallas as pl
from jax.experimental.pallas import tpu as pltpu
from jax.sharding import Mesh
from jax.sharding import PartitionSpec as P

BF = jnp.bfloat16
F32 = jnp.float32
NT = (((1,), (1,)), ((), ()))
TN = (((0,), (0,)), ((), ()))
ROWS = 64
GROUP = 4
FEAT = ("blk", "mem")
VMEM_LIMIT = 48 * 1024 * 1024


def call(kernel, out_shape, n_in, scratch=(), smem=(), late=(), flops=0, nbytes=0):
    spaces = {i: pltpu.SMEM for i in smem} | {i: pl.ANY for i in late}
    in_specs = [pl.BlockSpec(memory_space=spaces.get(i, pltpu.VMEM)) for i in range(n_in)]
    out_specs = jax.tree.map(lambda _: pl.BlockSpec(memory_space=pltpu.VMEM), out_shape)
    return pl.pallas_call(
        kernel,
        out_shape=out_shape,
        in_specs=in_specs,
        out_specs=out_specs,
        scratch_shapes=list(scratch),
        compiler_params=pltpu.CompilerParams(vmem_limit_bytes=VMEM_LIMIT),
        cost_estimate=pl.CostEstimate(flops=flops, bytes_accessed=nbytes, transcendentals=0),
    )


def pack_kernel(groups, tgt_rows, feats_ref, dst_ref, send_ref, masked):
    cols, edges = feats_ref.shape
    cap = send_ref.shape[2]
    dst = jnp.concatenate([dst_ref[i : i + 1, :] for i in range(dst_ref.shape[0])], axis=1)
    owner = dst // tgt_rows
    local = dst - owner * tgt_rows
    half = tgt_rows // 2
    code = jnp.where(local < half, local - half, local - (half - 1)).astype(F32)
    owner_hot = lax.broadcasted_iota(jnp.int32, (groups, edges), 0) == owner
    owner_hot = owner_hot.astype(F32)
    step = 256
    before = (
        lax.broadcasted_iota(jnp.int32, (step, step), 0)
        < lax.broadcasted_iota(jnp.int32, (step, step), 1)
    ).astype(BF)
    seen = jnp.zeros((groups, 1), F32)
    ranks = []
    for i in range(edges // step):
        part = owner_hot[:, i * step : (i + 1) * step]
        prior = jnp.dot(part.astype(BF), before, preferred_element_type=F32) + seen
        ranks.append(jnp.sum(prior * part, axis=0, keepdims=True))
        seen = seen + jnp.sum(part, axis=1, keepdims=True)
    rank = jnp.concatenate(ranks, axis=1).astype(jnp.int32)
    rank_hot = (lax.broadcasted_iota(jnp.int32, (cap, edges), 0) == rank).astype(F32).astype(BF)
    extra_row = lax.broadcasted_iota(jnp.int32, (ROWS - cols, edges), 0)
    extra = jnp.where(extra_row == 0, code, jnp.where(extra_row == 1, 1.0, 0.0)).astype(BF)
    hot = owner_hot.astype(BF)
    some = masked.shape[0] // ROWS
    for g in range(groups // some):
        for j in range(some):
            o = g * some + j
            live = hot[o : o + 1, :]
            masked[j * ROWS : j * ROWS + cols, :] = feats_ref[...] * live
            masked[j * ROWS + cols : (j + 1) * ROWS, :] = extra * live
        out = lax.dot_general(masked[...], rank_hot, NT, preferred_element_type=F32).astype(BF)
        for j in range(some):
            send_ref[g * some + j] = out[j * ROWS : (j + 1) * ROWS, :]


def far_place(block, column):
    return (block + column) % GROUP


def column_sets(weight, group):
    half = 64
    n = weight.shape[1] // half
    sets = []
    for h in range(group):
        at = [group * i + far_place(i, h) for i in range(n // group)]
        sets.append(jnp.concatenate([weight[:, b * half : (b + 1) * half] for b in at], axis=1))
    return sets


def first_pieces_kernel(
    block_ref, neigh_ref, own_ref, self_ref, cot_ref, late_ref, out_ref, cot_out_ref
):
    del late_ref
    rows = neigh_ref.shape[0]
    group, _, width = out_ref.shape
    both = zip(column_sets(neigh_ref[...], group), column_sets(own_ref[...], group))
    for h, (neigh, own) in enumerate(both):
        to = far_place(block_ref[0], h)
        out_ref[to, :rows, : width // 2] = neigh
        out_ref[to, :rows, width // 2 :] = own
        out_ref[to, rows:, :] = self_ref[...]
    cot_out_ref[...] = cot_ref[...]


def second_pieces_kernel(block_ref, neigh_ref, own_ref, late_ref, out_ref):
    del late_ref
    group, _, width = out_ref.shape
    both = zip(column_sets(neigh_ref[...], group), column_sets(own_ref[...], group))
    for h, (neigh, own) in enumerate(both):
        to = far_place(block_ref[0], h)
        out_ref[to, :, : width // 2] = neigh
        out_ref[to, :, width // 2 :] = own


def mean_kernel(cols, recv_ref, pieces_ref, late_ref, out_ref):
    del late_ref
    groups, rows, cap = recv_ref.shape
    targets = out_ref.shape[2]
    half = targets // 2
    vertex = lax.broadcasted_iota(jnp.int32, (targets, 1), 0)
    vertex = jnp.where(vertex < half, vertex - half, vertex - (half - 1)).astype(F32)
    acc = jnp.zeros((rows, targets), F32)
    some = 8
    for g in range(groups // some):
        part = jnp.concatenate([recv_ref[g * some + j] for j in range(some)], axis=1)
        code = part[cols : cols + 1, :].astype(F32)
        hot = (vertex == code).astype(F32).astype(BF)
        acc = acc + lax.dot_general(part, hot, NT, preferred_element_type=F32)
    degree = jnp.maximum(acc[cols + 1 : cols + 2, :], 1.0)
    mean = (acc[:cols, :] / degree).astype(BF)
    for j in range(out_ref.shape[0]):
        out_ref[j, :cols, :] = mean
        out_ref[j, cols:, :] = pieces_ref[j]


def first_kernel(got_ref, out_ref, weight, acts):
    group, rows, targets = got_ref.shape
    rows = rows // 3
    width = targets // 2
    for j in range(group):
        low, mid, high = 2 * rows * j, 2 * rows * j + rows, 2 * rows * (j + 1)
        acts[low:mid, :] = got_ref[j, :rows, :]
        weight[low:mid, :] = got_ref[j, rows : 2 * rows, :width]
        weight[mid:high, :] = got_ref[j, rows : 2 * rows, width:]
        acts[mid:high, :] = got_ref[j, 2 * rows :, :]
    total = lax.dot_general(weight[...], acts[...], TN, preferred_element_type=F32)
    cols = out_ref.shape[1]
    for z in range(out_ref.shape[0]):
        out_ref[z] = total[z * cols : (z + 1) * cols, :].astype(BF)


def hidden_kernel(parts_ref, bias_ref, pieces_ref, out_ref):
    cols = bias_ref.shape[0]
    total = parts_ref[0].astype(F32)
    for k in range(1, parts_ref.shape[0]):
        total = total + parts_ref[k].astype(F32)
    hidden = jnp.maximum(total + bias_ref[...], 0.0).astype(BF)
    for c in range(out_ref.shape[0]):
        out_ref[c, :cols, :] = hidden
        out_ref[c, cols:, :] = pieces_ref[c]


def grad_kernel(
    index_ref, got_ref, values_ref, live_ref, cot_ref, agg_ref, out_ref, left, source, acc
):
    group, cols, targets = got_ref.shape
    cols = cols // 2
    width = values_ref.shape[1]
    wide = group * cols
    for t in range(targets // width):
        for j in range(group):
            at = slice(j * cols, (j + 1) * cols)
            source[t, at, :] = got_ref[j, :cols, t * width : (t + 1) * width]
    acc[...] = jnp.zeros_like(acc)
    for k in range(values_ref.shape[0]):
        target = index_ref[k, 0]
        acc[target] += lax.dot_general(
            source[index_ref[k, 1]], values_ref[k], NT, preferred_element_type=F32
        )
    live = live_ref[...].astype(BF)
    for t in range(targets // width):
        at = slice(t * width, (t + 1) * width)
        tile = acc[t].astype(BF)
        agg_ref[:, at] = tile
        left[:wide, at] = tile * live[:, at]
        left[wide:, at] = source[t] * live[:, at]
    block = lax.dot_general(left[...], cot_ref[...], NT, preferred_element_type=F32)
    at = 0
    for w in range(2):
        for r in range(0, cols, 8):
            for c in range(0, cot_ref.shape[0], 128):
                rows_of = [
                    block[w * wide + j * cols + r : w * wide + j * cols + r + 8, c : c + 128]
                    for j in range(group)
                ]
                out_ref[at] = jnp.concatenate(rows_of, axis=0).astype(BF)
                at += 1


def second_kernel(block_ref, agg_ref, got_ref, out_ref, weight, acts):
    group, rows, targets = got_ref.shape
    rows = rows // 2
    width = targets // 2
    for j in range(group):
        low, mid, high = 2 * rows * j, 2 * rows * j + rows, 2 * rows * (j + 1)
        weight[low:mid, :] = got_ref[j, rows:, :width]
        acts[low:mid, :] = agg_ref[j * rows : (j + 1) * rows, :]
        weight[mid:high, :] = got_ref[j, rows:, width:]
        acts[mid:high, :] = got_ref[j, :rows, :]
    total = lax.dot_general(weight[...], acts[...], TN, preferred_element_type=F32)
    n, cols, _ = out_ref.shape
    for z in range(n):
        out_ref[jnp.bitwise_xor(block_ref[0], z)] = total[z * cols : (z + 1) * cols, :].astype(BF)


def copies_kernel(terms_ref, late1_ref, late2_ref, out_ref):
    del late1_ref, late2_ref
    total = terms_ref[0].astype(F32)
    for d in range(1, terms_ref.shape[0]):
        total = total + terms_ref[d].astype(F32)
    for d in range(out_ref.shape[0]):
        out_ref[d] = total


def place_kernel(block_ref, pieces_ref, neigh_ref, self_ref):
    half = 64
    starts = []
    for h in range(GROUP):
        starts.append(pl.multiple_of(far_place(block_ref[0], h) * 8, 8))
    at = 0
    for out_ref in (neigh_ref, self_ref):
        for r in range(0, out_ref.shape[0], 8):
            for c in range(2):
                parts = [pieces_ref[at, pl.ds(start, 8), :] for start in starts]
                for e in range(2):
                    block = 2 * c + e
                    for p in range(0, GROUP, 2):
                        pair = [
                            parts[(p + i - block) % GROUP][:, e * half : (e + 1) * half]
                            for i in range(2)
                        ]
                        to = (GROUP * block + p) * half
                        out_ref[r : r + 8, to : to + 2 * half] = jnp.concatenate(pair, axis=1)
                at += 1


def out_kernel(p0_ref, p1_ref, p2_ref, p3_ref, bias_ref, live_ref, out_ref):
    total = p0_ref[...].astype(F32) + p1_ref[...].astype(F32)
    total = total + (p2_ref[...].astype(F32) + p3_ref[...].astype(F32))
    out_ref[...] = ((total + bias_ref[...]) * live_ref[...]).astype(BF)


def body(
    edge_feats,
    edge_dst,
    self_feats,
    neigh_one,
    self_one,
    bias_one,
    tile_index,
    tile_values,
    seed_live,
    neigh_two,
    self_two,
    bias_two,
    cotangent,
):
    groups = lax.axis_size("dp")
    blocks = lax.axis_size("blk")
    edges, cols = edge_feats.shape
    targets = self_feats.shape[0]
    hid = bias_one.shape[0]
    full = neigh_one.shape[1]
    cap = 2 * edges // groups
    wide = full // GROUP
    far = [[GROUP * i + far_place(i, h) for i in range(blocks)] for h in range(GROUP)]
    block = lax.axis_index("blk").reshape(1)
    live = seed_live.reshape(1, targets).astype(F32)

    def swap(x, axis, among=None):
        return lax.all_to_all(
            x, axis, split_axis=0, concat_axis=0, tiled=True, axis_index_groups=among
        )

    def trade_far(x, k):
        pairs = [(group[i], group[i ^ k]) for group in far for i in range(blocks)]
        return lax.ppermute(x, FEAT, pairs)

    def shape(*dims, dtype=BF):
        return jax.ShapeDtypeStruct(dims, dtype)

    with jax.named_scope("edges"):
        send = call(
            functools.partial(pack_kernel, groups, targets),
            shape(groups, ROWS, cap),
            2,
            scratch=[pltpu.VMEM((8 * ROWS, edges), BF)],
            flops=2 * groups * ROWS * edges * cap,
            nbytes=8 << 20,
        )(edge_feats.T, edge_dst.reshape(-1, 128))
        recv = swap(send, "dp")
    with jax.named_scope("pieces"):
        pieces, cot = call(
            first_pieces_kernel,
            (shape(GROUP, 2 * cols, targets), shape(hid, targets)),
            6,
            smem=(0,),
            late=(5,),
            nbytes=2 << 20,
        )(block, neigh_one, self_one, self_feats.T, cotangent.T, send)
        cot = lax.all_gather(cot, FEAT, axis=0, tiled=True, axis_index_groups=far)
    with jax.named_scope("mean"):
        acts = call(
            functools.partial(mean_kernel, cols),
            shape(GROUP, 3 * cols, targets),
            3,
            late=(2,),
            flops=2 * groups * ROWS * cap * targets,
            nbytes=8 << 20,
        )(recv, pieces, cot)
        acts = swap(acts, "mem")
    with jax.named_scope("first"):
        first = call(
            first_kernel,
            shape(blocks, hid, targets),
            1,
            scratch=[pltpu.VMEM((8 * cols, wide), BF), pltpu.VMEM((8 * cols, targets), BF)],
            flops=2 * 8 * cols * wide * targets,
            nbytes=2 << 20,
        )(acts)
        parts = swap(first, FEAT, far)
    with jax.named_scope("pieces"):
        pieces = call(
            second_pieces_kernel,
            shape(GROUP, hid, targets),
            4,
            smem=(0,),
            late=(3,),
            nbytes=1 << 20,
        )(block, neigh_two, self_two, first)
    with jax.named_scope("hidden"):
        hidden = call(hidden_kernel, shape(GROUP, 2 * hid, targets), 3, nbytes=1 << 20)(
            parts, bias_one.reshape(hid, 1), pieces
        )
        hidden = swap(hidden, "mem")
    with jax.named_scope("grads"):
        agg, terms = call(
            grad_kernel,
            (shape(wide, targets), shape(groups, GROUP * 8, 128)),
            5,
            scratch=[
                pltpu.VMEM((2 * wide, targets), BF),
                pltpu.VMEM((targets // 128, wide, 128), BF),
                pltpu.VMEM((targets // 128, wide, 128), F32),
            ],
            smem=(0,),
            flops=2 * 2 * wide * targets * wide,
            nbytes=4 << 20,
        )(tile_index, hidden, tile_values, live, cot)
        terms = swap(terms.reshape(GROUP * groups, 8, 128), ("dp", "mem"))
    with jax.named_scope("second"):
        second = call(
            second_kernel,
            shape(blocks, hid, targets),
            3,
            scratch=[pltpu.VMEM((2 * wide, wide), BF), pltpu.VMEM((2 * wide, targets), BF)],
            smem=(0,),
            flops=2 * 2 * wide * wide * targets,
            nbytes=2 << 20,
        )(block, agg, hidden)
        sums = [second[0]] + [trade_far(second[k], k) for k in range(1, blocks)]
        second_out = call(out_kernel, shape(hid, targets), 6, nbytes=1 << 20)(
            *sums, bias_two.reshape(hid, 1), live
        ).T
    with jax.named_scope("place"):
        spread = call(
            copies_kernel,
            shape(groups, GROUP * 8, 128, dtype=F32),
            3,
            late=(1, 2),
            nbytes=1 << 20,
        )(terms.reshape(groups, GROUP * 8, 128), second, sums[3])
        spread = swap(spread, "dp")
        grad_neigh, grad_self = call(
            place_kernel,
            (shape(hid, full, dtype=F32), shape(hid, full, dtype=F32)),
            2,
            smem=(0,),
            nbytes=1 << 20,
        )(block, spread)
    return (second_out, grad_neigh, grad_self)


def solution(mesh):
    shards = mesh.devices.shape
    blocks = mesh.devices.reshape(shards[0], shards[1] // GROUP, GROUP)
    mesh = Mesh(blocks, ("dp",) + FEAT)
    in_specs = (
        P("dp", FEAT),
        P("dp"),
        P("dp", FEAT),
        P(FEAT, None),
        P(FEAT, None),
        P(FEAT),
        P("dp", None),
        P("dp", None, None),
        P("dp"),
        P(FEAT, None),
        P(FEAT, None),
        P(FEAT),
        P("dp", FEAT),
    )
    out_specs = (P("dp", FEAT), P(FEAT, None), P(FEAT, None))
    return jax.shard_map(body, mesh=mesh, in_specs=in_specs, out_specs=out_specs, check_vma=False)
```
